32 devices in a mesh: row: 4 (over z), col: 8 (over y, x, core).
Axes of the slice: x: 2, y: 2, z: 4, core: 2. Of those that a mesh axis runs over, the one named last changes fastest.
Arguments:
- activations: bfloat16 [256, 28672], P('row', 'col'), may hold values from -0.375 to 0.375
- cotangent: bfloat16 [256, 16384], P('col', 'row'), may hold values from -6 to 6
- down_weight: bfloat16 [28672, 16384], P('col', 'row'), may hold values from -0.046875 to 0.046875
- row_order: int32 [256], replicated, may hold values from 0 to 255, each once
Outputs:
- weight_grad: bfloat16 [28672, 16384], P('col', 'row')
- input_grad: bfloat16 [256, 28672], P('row', 'col')
The draws below stay inside these ranges and needn't reach their ends.
Inputs may be any that keep to these rules, and one draw needn't show every extreme that they name: `row_order`: each of the 256 rows is named exactly once.
All inputs are finite; a program needn't handle non-finite values.
Results may differ from the reference program's by a relative error of at most 0.001.
Values may be sent and summed in bfloat16 or wider, within the bound.
No kernel may reach another device: no remote copies, remote signals or barrier semaphores. Data moves between devices by JAX's collectives and lax.ppermute only.
A program may use at most 128 MiB of HBM per device.

```python
import jax
import jax.numpy as jnp

D = 16384
F = 28672
ROWS = 256


def with_spikes(result, stream_key, source, target, blocks, factor):
    def block_of(position):
        return (jnp.arange(result.shape[position]) // (result.shape[position] // blocks)).reshape((-1,) + (1,) * (result.ndim - 1 - position))

    first = jax.random.permutation(stream_key, blocks)[block_of(target)]
    far = (block_of(target) + blocks // 2) % blocks
    return jnp.where((block_of(source) == first) | (block_of(source) == far), factor * result, result)


def shard_levels(own_key, dims, pieces, least, top_value):
    def one(axis_at, blocks):
        heights = jax.random.uniform(jax.random.fold_in(jax.random.fold_in(own_key, 6), axis_at), (blocks,), jnp.float32, least / len(pieces), top_value / len(pieces))
        return jnp.repeat(jnp.exp(heights), dims[axis_at] // blocks).reshape((-1,) + (1,) * (len(dims) - axis_at - 1))

    gain = one(*pieces[0])
    for cut in pieces[1:]:
        gain = gain * one(*cut)
    return gain


def gaussian(rng, dims, deviation, most, pieces=(), dtype=jnp.bfloat16):
    drawn = jax.random.normal(rng, dims, jnp.float32) * deviation
    if len(pieces) > 0:
        drawn = shard_levels(rng, dims, pieces, -0.22, 0.18) * drawn
    return jnp.clip(drawn, min=-most, max=most).astype(dtype)


def gaussian_with(own_key, shape, spread, most, shards, heavy, kind=jnp.bfloat16):
    entries = spread * jax.random.normal(own_key, shape, jnp.float32)
    if shards:
        entries = entries * shard_levels(own_key, shape, shards, -0.22, 0.18)
    return jnp.clip(with_spikes(entries, jax.random.fold_in(own_key, 3), *heavy), -most, most).astype(kind)


def setup_inputs(seed: int = 0) -> dict:
    seeds = jax.random.split(jax.random.key(seed), 5)
    activations = gaussian(seeds[0], (ROWS, F), (1.0 / ROWS ** 0.5), 0.375, ((0, 4), (1, 8)))
    cotangent = gaussian_with(seeds[1], (ROWS, D), 1.0, 6.0, ((0, 8), (1, 4)), (1, 0, 8, 2.0))
    down_weight = gaussian(seeds[2], (F, D), D ** -0.5, 0.046875, ((0, 8), (1, 4)))
    row_order = jax.random.permutation(seeds[3], ROWS).astype(jnp.int32)
    return {"activations": activations, "cotangent": cotangent, "down_weight": down_weight, "row_order": row_order}


def reference(activations, cotangent, down_weight, row_order):
    aligned = jnp.take(cotangent, row_order.astype(jnp.int32), axis=0)
    weight_grad = jnp.dot(activations.T, aligned, preferred_element_type=jnp.float32).astype(jnp.bfloat16)
    input_grad = jnp.dot(aligned, down_weight.T, preferred_element_type=jnp.float32).astype(jnp.bfloat16)
    return weight_grad, input_grad
```

```python
import functools

import jax
import jax.numpy as jnp
from jax import lax
from jax.experimental import pallas as pl
from jax.experimental.pallas import tpu as pltpu
from jax.sharding import PartitionSpec as P

LANES = 128
STEPS_PER_OCTAVE = 128.0
TOP = 32766.0
LEAST = 2.0 ** -120
VMEM_LIMIT = 50 * 1024 * 1024


def tile_of(size, largest):
    tile = largest
    while size % tile:
        tile //= 2
    return tile


def dot(left, right, dims):
    return lax.dot_general(left, right, (dims, ((), ())), preferred_element_type=jnp.float32)


def encode(values):
    most = jnp.maximum(jnp.max(jnp.abs(values), axis=1, keepdims=True), LEAST)
    level = jnp.ceil(jnp.log2(most) * STEPS_PER_OCTAVE) + 1.0
    codes = jnp.round(values * jnp.exp2(level * (-1.0 / STEPS_PER_OCTAVE)) * TOP)
    return codes.astype(jnp.int32).astype(jnp.int16), level


def decode(codes, levels):
    scale = jnp.exp2(levels.astype(jnp.int32).astype(jnp.float32) * (1.0 / STEPS_PER_OCTAVE)) * (1.0 / TOP)
    return codes.astype(jnp.int32).astype(jnp.float32) * scale


def partial_kernel(n_pieces, n_groups, tile, *refs):
    pick_ref, weight_ref = refs[:2]
    pieces = refs[2:2 + n_pieces]
    aligned_ref, own_ref = refs[2 + n_pieces:4 + n_pieces]
    sent = refs[4 + n_pieces:3 + n_pieces + n_groups]
    levels_ref = refs[-1]
    step = pl.program_id(0)
    rows = own_ref.shape[0]
    width = sent[0].shape[1] - LANES
    depth = aligned_ref.shape[1]

    @pl.when(step == 0)
    def _():
        chunk = tile_of(depth, 512)
        for at in range(0, depth, chunk):
            cols = slice(at, at + chunk)
            gathered = jnp.concatenate([piece[:, cols] for piece in pieces], axis=0)
            aligned_ref[:, cols] = dot(pick_ref[...], gathered, ((1,), (0,))).astype(jnp.bfloat16)
        levels_ref[...] = jnp.zeros_like(levels_ref)

    sums = dot(aligned_ref[...], weight_ref[...], ((1,), (1,)))
    own_ref[...] = sums[:rows]
    codes, level = encode(sums[rows:])
    here = lax.broadcasted_iota(jnp.int32, levels_ref.shape, 1) == step
    levels_ref[...] = jnp.where(here, level, levels_ref[...])
    cols = pl.ds(pl.multiple_of(step * tile, tile), tile)
    for at, ref in enumerate(sent):
        ref[:, cols] = codes[at * rows:(at + 1) * rows]

    @pl.when(step == pl.num_programs(0) - 1)
    def _():
        for at, ref in enumerate(sent):
            ref[:, width:] = levels_ref[at * rows:(at + 1) * rows].astype(jnp.int32).astype(jnp.int16)


def partial_sums(pick, weight, pieces, n_groups):
    hidden, depth = weight.shape
    total = pick.shape[0]
    rows = total // n_groups
    tile = tile_of(hidden, 256)
    whole = lambda i: (0, 0)
    return pl.pallas_call(
        functools.partial(partial_kernel, len(pieces), n_groups, tile),
        grid=(hidden // tile,),
        in_specs=[
            pl.BlockSpec(pick.shape, whole),
            pl.BlockSpec((tile, depth), lambda i: (i, 0)),
        ] + [pl.BlockSpec(piece.shape, whole) for piece in pieces],
        out_specs=[
            pl.BlockSpec((total, depth), whole),
            pl.BlockSpec((rows, tile), lambda i: (0, i)),
        ] + [pl.BlockSpec((rows, hidden + LANES), whole)] * (n_groups - 1),
        out_shape=[
            jax.ShapeDtypeStruct((total, depth), jnp.bfloat16),
            jax.ShapeDtypeStruct((rows, hidden), jnp.float32),
        ] + [jax.ShapeDtypeStruct((rows, hidden + LANES), jnp.int16)] * (n_groups - 1),
        scratch_shapes=[pltpu.VMEM((total - rows, LANES), jnp.float32)],
        compiler_params=pltpu.CompilerParams(vmem_limit_bytes=VMEM_LIMIT),
        cost_estimate=pl.CostEstimate(
            flops=2 * total * hidden * depth, bytes_accessed=2 * hidden * depth + 6 * total * depth, transcendentals=0),
        name="partial_sums",
    )(pick, weight, *pieces)


def weight_kernel(n_groups, *refs):
    aligned_ref = refs[0]
    pieces = refs[1:1 + n_groups]
    out_ref = refs[-1]
    left = jnp.concatenate([piece[...] for piece in pieces], axis=0)
    depth = out_ref.shape[1]
    chunk = tile_of(depth, 1024)
    for at in range(0, depth, chunk):
        cols = slice(at, at + chunk)
        out_ref[:, cols] = dot(left, aligned_ref[:, cols], ((0,), (0,))).astype(jnp.bfloat16)


def weight_grads(aligned, pieces):
    total, depth = aligned.shape
    rows, hidden = pieces[0].shape
    tile = tile_of(hidden, 256)
    return pl.pallas_call(
        functools.partial(weight_kernel, len(pieces)),
        grid=(hidden // tile,),
        in_specs=[pl.BlockSpec((total, depth), lambda i: (0, 0))]
        + [pl.BlockSpec((rows, tile), lambda i: (0, i))] * len(pieces),
        out_specs=pl.BlockSpec((tile, depth), lambda i: (i, 0)),
        out_shape=jax.ShapeDtypeStruct((hidden, depth), jnp.bfloat16),
        compiler_params=pltpu.CompilerParams(vmem_limit_bytes=VMEM_LIMIT),
        cost_estimate=pl.CostEstimate(
            flops=2 * total * hidden * depth, bytes_accessed=2 * hidden * depth + 2 * total * (depth + hidden), transcendentals=0),
        name="weight_grads",
    )(aligned, *pieces)


def total_kernel(tile, own_ref, *refs):
    received, out_ref = refs[:-1], refs[-1]
    width = own_ref.shape[1]
    for at in range(width // tile):
        cols = slice(at * tile, (at + 1) * tile)
        total = own_ref[:, cols]
        for ref in received:
            total = total + decode(ref[:, cols], ref[:, width:][:, at:at + 1])
        out_ref[:, cols] = total.astype(jnp.bfloat16)


def totals(own, received):
    rows, hidden = own.shape
    return pl.pallas_call(
        functools.partial(total_kernel, tile_of(hidden, 256)),
        out_shape=jax.ShapeDtypeStruct((rows, hidden), jnp.bfloat16),
        compiler_params=pltpu.CompilerParams(vmem_limit_bytes=VMEM_LIMIT),
        cost_estimate=pl.CostEstimate(
            flops=rows * hidden * 8, bytes_accessed=rows * hidden * (6 + 2 * len(received)), transcendentals=0),
        name="totals",
    )(own, *received)


def gather_cotangent(cotangent, n_col):
    pieces, owners = [cotangent], [0]
    for flip in range(2, n_col, 2):
        pieces.append(lax.ppermute(cotangent, "col", [(i, i ^ flip) for i in range(n_col)]))
        owners.append(flip)
    swap = [(i, i ^ 1) for i in range(n_col)]
    pieces += [lax.ppermute(piece, "col", swap) for piece in pieces]
    owners += [flip ^ 1 for flip in owners]
    return pieces, owners


def gather_activations(activations, n_row):
    last = n_row - 1
    pieces = [activations]
    for o in range(1, n_row):
        pairs = [((i + o) % n_row, i) for i in range(n_row)]
        pairs = [pair for pair in pairs if abs(pair[0] - pair[1]) < max(last, 2)]
        pieces.append(lax.ppermute(activations, "row", pairs))
    if last >= 3:
        me = lax.axis_index("row")
        held = pieces[2] if n_row == 4 else jnp.where(me == 1, pieces[n_row - 2], pieces[2])
        far = lax.ppermute(held, "row", [(1, 0), (last - 1, last)])
        pieces[last] = jnp.where(me == 0, far, pieces[last])
        pieces[1] = jnp.where(me == last, far, pieces[1])
    return pieces


def body(n_row, n_col, activations, cotangent, down_weight, row_order):
    rows = activations.shape[0]
    shard = cotangent.shape[0]
    mine_row, mine_col = lax.axis_index("row"), lax.axis_index("col")

    cot_pieces, owners = gather_cotangent(cotangent, n_col)
    act_pieces = gather_activations(activations, n_row)

    order = row_order.reshape(n_row, rows)
    order = jnp.roll(order, -mine_row, axis=0).reshape(n_row * rows)
    owner = mine_col ^ jnp.asarray(owners, jnp.int32)
    named = (owner[:, None] * shard + jnp.arange(shard, dtype=jnp.int32)[None, :]).reshape(-1)
    pick = (order[:, None] == named[None, :]).astype(jnp.bfloat16)

    aligned, own, *sent = partial_sums(pick, down_weight, cot_pieces, n_row)
    received = [
        lax.ppermute(message, "row", [(i, (i + o) % n_row) for i in range(n_row)])
        for o, message in enumerate(sent, 1)
    ]
    weight_grad = weight_grads(aligned, act_pieces)
    input_grad = totals(own, received)
    return weight_grad, input_grad


def solution(mesh):
    in_specs = (P("row", "col"), P("col", "row"), P("col", "row"), P())
    out_specs = (P("col", "row"), P("row", "col"))
    fn = functools.partial(body, mesh.shape["row"], mesh.shape["col"])
    return jax.shard_map(fn, mesh=mesh, in_specs=in_specs, out_specs=out_specs, check_vma=False)
```

```python
import functools

import jax
import jax.numpy as jnp
from jax import lax
from jax.experimental import pallas as pl
from jax.experimental.pallas import tpu as pltpu
from jax.sharding import PartitionSpec as P

LANES = 128
STEPS_PER_OCTAVE = 128.0
TOP = 32766.0
LEAST = 2.0 ** -120
VMEM_LIMIT = 48 * 1024 * 1024
SUB = 256
LINE_GROUPS = ((0, 3, 1, 2), (1, 2, 0, 3), (2, 3, 1, 0), (3, 2, 0, 1))


def tile_of(size, largest):
    tile = largest
    while size % tile:
        tile //= 2
    return tile


def dot(left, right, dims):
    return lax.dot_general(left, right, (dims, ((), ())), preferred_element_type=jnp.float32)


def encode(values):
    most = jnp.maximum(jnp.max(jnp.abs(values), axis=1, keepdims=True), LEAST)
    level = jnp.ceil(jnp.log2(most) * STEPS_PER_OCTAVE) + 1.0
    codes = jnp.round(values * jnp.exp2(level * (-1.0 / STEPS_PER_OCTAVE)) * TOP)
    return codes.astype(jnp.int32).astype(jnp.int16), level


def decode(codes, levels):
    scale = jnp.exp2(levels.astype(jnp.int32).astype(jnp.float32) * (1.0 / STEPS_PER_OCTAVE)) * (1.0 / TOP)
    return codes.astype(jnp.int32).astype(jnp.float32) * scale


def to_levels(levels):
    return levels.astype(jnp.int32).astype(jnp.int16)


def params():
    return pltpu.CompilerParams(vmem_limit_bytes=VMEM_LIMIT)


def cost(flops, moved):
    return pl.CostEstimate(flops=flops, bytes_accessed=moved, transcendentals=0)


def align_rows(pick_ref, pieces, aligned_ref):
    depth = aligned_ref.shape[1]
    chunk = tile_of(depth, 512)
    for at in range(0, depth, chunk):
        cols = slice(at, at + chunk)
        gathered = jnp.concatenate([piece[:, cols] for piece in pieces], axis=0)
        aligned_ref[:, cols] = dot(pick_ref[...], gathered, ((1,), (0,))).astype(jnp.bfloat16)


def sums_kernel(n_pieces, n_groups, keeps, turned, tile, *refs):
    refs = list(refs)
    if n_pieces:
        pick_ref = refs.pop(0)
        pieces = [refs.pop(0) for _ in range(n_pieces)]
        weight_ref = refs.pop(0)
        aligned_ref = refs.pop(0)
    else:
        aligned_ref, weight_ref = refs.pop(0), refs.pop(0)
    kept = [refs.pop(0) for _ in keeps]
    sent = [refs.pop(0) for _ in range(n_groups - len(keeps))]
    sends = [at for at in range(n_groups) if at not in keeps]
    levels_ref = refs.pop(0)
    step = pl.program_id(0)
    rows = kept[0].shape[0]
    width = sent[0].shape[1] - LANES

    @pl.when(step == 0)
    def _():
        if n_pieces:
            align_rows(pick_ref, pieces, aligned_ref)
        if turned:
            refs[0][...] = aligned_ref[...].T
        levels_ref[...] = jnp.zeros_like(levels_ref)

    sub = tile_of(tile, SUB)
    spans = [slice(at, at + sub) for at in range(0, tile, sub)]
    if turned:
        products = dot(weight_ref[...], refs[0][...], ((1,), (0,)))
        sums = [products[span].T for span in spans]
    else:
        sums = [dot(aligned_ref[...], weight_ref[span], ((1,), (1,))) for span in spans]
    lane = lax.broadcasted_iota(jnp.int32, levels_ref.shape, 1)
    levels = levels_ref[...]
    for part, (span, values) in enumerate(zip(spans, sums)):
        for at, ref in zip(keeps, kept):
            ref[:, span] = values[at * rows:(at + 1) * rows]
        outgoing = jnp.concatenate([values[at * rows:(at + 1) * rows] for at in sends], axis=0)
        codes, level = encode(outgoing)
        levels = jnp.where(lane == step * len(spans) + part, level, levels)
        cols = pl.ds(pl.multiple_of(step * tile + span.start, sub), sub)
        for at, ref in enumerate(sent):
            ref[:, cols] = codes[at * rows:(at + 1) * rows]
    levels_ref[...] = levels

    @pl.when(step == pl.num_programs(0) - 1)
    def _():
        for at, ref in enumerate(sent):
            ref[:, width:] = to_levels(levels[at * rows:(at + 1) * rows])


def partial_sums(aligned, align, weight, tile, first, count, n_groups, keeps, turned, name):
    depth = weight.shape[1]
    width = count * tile
    whole = lambda i: (0, 0)
    operands = [align[0], *align[1]] if aligned is None else [aligned]
    total = operands[0].shape[0]
    rows = total // n_groups
    n_sent = n_groups - len(keeps)
    in_specs = [pl.BlockSpec(operand.shape, whole) for operand in operands]
    in_specs.append(pl.BlockSpec((tile, depth), lambda i: (i + first, 0)))
    out_specs = [pl.BlockSpec((rows, tile), lambda i: (0, i))] * len(keeps)
    out_specs += [pl.BlockSpec((rows, width + LANES), whole)] * n_sent
    out_shape = [jax.ShapeDtypeStruct((rows, width), jnp.float32)] * len(keeps)
    out_shape += [jax.ShapeDtypeStruct((rows, width + LANES), jnp.int16)] * n_sent
    if aligned is None:
        out_specs.insert(0, pl.BlockSpec((total, depth), whole))
        out_shape.insert(0, jax.ShapeDtypeStruct((total, depth), jnp.bfloat16))
    scratch = [pltpu.VMEM((n_sent * rows, LANES), jnp.float32)]
    if turned:
        scratch.append(pltpu.VMEM((depth, total), jnp.bfloat16))
    outs = pl.pallas_call(
        functools.partial(sums_kernel, 0 if aligned is not None else len(align[1]), n_groups, keeps, turned, tile),
        grid=(count,), in_specs=in_specs, out_specs=out_specs, out_shape=out_shape, scratch_shapes=scratch,
        compiler_params=params(), cost_estimate=cost(2 * total * width * depth, 2 * width * depth), name=name,
    )(*operands, weight)
    if aligned is None:
        aligned, *outs = outs
    return aligned, outs[:len(keeps)], outs[len(keeps):]


def weight_kernel(n_pieces, choose, me_ref, aligned_ref, *refs):
    out_ref = refs[-1]
    left = jnp.concatenate(choose(me_ref[0], [ref[...] for ref in refs[:n_pieces]]), axis=0)
    depth = out_ref.shape[1]
    chunk = tile_of(depth, 1024)
    for at in range(0, depth, chunk):
        cols = slice(at, at + chunk)
        out_ref[:, cols] = dot(left, aligned_ref[:, cols], ((0,), (0,))).astype(jnp.bfloat16)


def weight_grads(me, aligned, pieces, choose, later_than=()):
    total, depth = aligned.shape
    rows, hidden = pieces[0].shape
    tile = tile_of(hidden, 512)
    return pl.pallas_call(
        functools.partial(weight_kernel, len(pieces), choose),
        grid=(hidden // tile,),
        in_specs=[pl.BlockSpec(memory_space=pltpu.SMEM), pl.BlockSpec((total, depth), lambda i: (0, 0))]
        + [pl.BlockSpec((rows, tile), lambda i: (0, i))] * len(pieces)
        + [pl.BlockSpec(memory_space=pl.ANY)] * len(later_than),
        out_specs=pl.BlockSpec((tile, depth), lambda i: (i, 0)),
        out_shape=jax.ShapeDtypeStruct((hidden, depth), jnp.bfloat16),
        compiler_params=params(), cost_estimate=cost(2 * total * hidden * depth, 2 * hidden * depth), name="weight_grads",
    )(me, aligned, *pieces, *later_than)


def line_choose(me, pieces):
    own, left, right, two, far = pieces
    first = jnp.where(me == 0, far, jnp.where(me == 3, left, right))
    second = jnp.where(me == 0, right, jnp.where(me == 3, far, left))
    return [own, first, second, two]


def merge_kernel(me_ref, left_ref, right_ref, kept_ref, first_ref, second_ref, *refs):
    me = me_ref[0]
    two_ref, last_ref = refs[(len(refs) - 2) // 2:][:2]
    width = kept_ref.shape[1]
    last_ref[...] = jnp.where(me == 0, second_ref[...], first_ref[...])
    sub = tile_of(width, SUB)
    lane = lax.broadcasted_iota(jnp.int32, (kept_ref.shape[0], LANES), 1)
    levels = jnp.zeros(lane.shape, jnp.float32)
    inner = jnp.where((me == 1) | (me == 2), 1.0, 0.0)
    for at in range(width // sub):
        cols = slice(at * sub, (at + 1) * sub)
        codes = jnp.where(me == 1, left_ref[:, cols], right_ref[:, cols])
        level = jnp.where(me == 1, left_ref[:, width:], right_ref[:, width:])[:, at:at + 1]
        codes, level = encode(kept_ref[:, cols] + inner * decode(codes, level))
        two_ref[:, cols] = codes
        levels = jnp.where(lane == at, level, levels)
    two_ref[:, width:] = to_levels(levels)


def merged(me, left, right, kept, first, second, passed):
    vmem, anywhere = pl.BlockSpec(memory_space=pltpu.VMEM), pl.BlockSpec(memory_space=pl.ANY)
    like = jax.ShapeDtypeStruct(left.shape, left.dtype)
    onward, last, *passed = pl.pallas_call(
        merge_kernel,
        in_specs=[pl.BlockSpec(memory_space=pltpu.SMEM)] + [vmem] * 5 + [anywhere] * len(passed),
        out_specs=[vmem] * 2 + [anywhere] * len(passed),
        out_shape=[like, like] + [jax.ShapeDtypeStruct(array.shape, array.dtype) for array in passed],
        input_output_aliases={6 + at: 2 + at for at in range(len(passed))},
        compiler_params=params(), cost_estimate=cost(left.size * 20, left.size * 16), name="merged",
    )(me, left, right, kept, first, second, *passed)
    return onward, last, passed


def total_kernel(counts, choose, me_ref, *refs):
    refs = list(refs)
    out_ref = refs.pop()
    base = 0
    for count in counts:
        own_ref, received, refs = refs[0], refs[1:count], refs[count:]
        width = own_ref.shape[1]
        sub = tile_of(width, SUB)
        for at in range(width // sub):
            cols = slice(at * sub, (at + 1) * sub)
            total = own_ref[:, cols]
            codes = choose(me_ref[0], [ref[:, cols] for ref in received])
            levels = choose(me_ref[0], [ref[:, width:] for ref in received])
            for code, level in zip(codes, levels):
                total = total + decode(code, level[:, at:at + 1])
            out_ref[:, base + at * sub:base + (at + 1) * sub] = total.astype(jnp.bfloat16)
        base += width


def line_received(me, messages):
    left, right, two, last = messages
    return [jnp.where(me < 2, right, left), two, last]


def totals(me, parts, choose, later_than=()):
    rows = parts[0][0].shape[0]
    hidden = sum(part[0].shape[1] for part in parts)
    flat = [array for part in parts for array in part]
    return pl.pallas_call(
        functools.partial(total_kernel, [len(part) for part in parts], choose),
        in_specs=[pl.BlockSpec(memory_space=pltpu.SMEM)] + [pl.BlockSpec(memory_space=pltpu.VMEM)] * len(flat)
        + [pl.BlockSpec(memory_space=pl.ANY)] * len(later_than),
        out_shape=jax.ShapeDtypeStruct((rows, hidden), jnp.bfloat16),
        compiler_params=params(), cost_estimate=cost(rows * hidden * 40, rows * hidden * 14), name="totals",
    )(me, *flat, *later_than)


def send(value, axis, pairs):
    return lax.ppermute(value, axis, pairs)


def gather_cotangent(cotangent, n_col):
    pieces = [send(cotangent, "col", [(i, i ^ flip) for i in range(n_col)]) for flip in range(2, n_col, 2)]
    swap = [(i, i ^ 1) for i in range(n_col)]
    swapped = [send(piece, "col", swap) for piece in [cotangent] + pieces]
    flips = list(range(0, n_col, 2))
    return [cotangent] + pieces + swapped, flips + [flip ^ 1 for flip in flips]


def body(n_row, n_col, activations, cotangent, down_weight, row_order):
    rows, hidden = activations.shape
    shard = cotangent.shape[0]
    mine_row, mine_col = lax.axis_index("row"), lax.axis_index("col")
    me = mine_row.astype(jnp.int32).reshape(1)
    on_line = n_row == 4

    pieces, flips = gather_cotangent(cotangent, n_col)
    if on_line:
        groups = [sum(jnp.where(mine_row == row, LINE_GROUPS[row][at], 0) for row in range(n_row)) for at in range(n_row)]
        from_left = send(activations, "row", [(0, 1), (1, 2), (2, 3)])
        from_right = send(activations, "row", [(3, 2), (2, 1), (1, 0)])
    else:
        groups = [(mine_row + o) % n_row for o in range(n_row)]

    order = row_order.reshape(n_row, rows)
    order = jnp.concatenate([lax.dynamic_index_in_dim(order, group, 0, keepdims=False) for group in groups])
    owner = mine_col ^ jnp.asarray(flips, jnp.int32)
    named = (owner[:, None] * shard + jnp.arange(shard, dtype=jnp.int32)[None, :]).reshape(-1)
    pick = (order[:, None] == named[None, :]).astype(jnp.bfloat16)

    tile = tile_of(hidden, 512)
    tiles = hidden // tile
    cut = tiles // 2
    keeps = (0, 3) if on_line else (0,)

    if not on_line:
        aligned, kept, sent = partial_sums(None, (pick, pieces), down_weight, tile, 0, tiles, n_row, keeps, False, "partial_sums")
        shift = lambda o: [(i, (i + o) % n_row) for i in range(n_row)]
        received = [send(message, "row", shift(o)) for o, message in enumerate(sent, 1)]
        act_pieces = [activations] + [send(activations, "row", shift(n_row - o)) for o in range(1, n_row)]
        same = lambda _, values: values
        weight_grad = weight_grads(me, aligned, act_pieces, same)
        return weight_grad, totals(me, [kept + received], same)

    two_left = send(from_left, "row", [(1, 2), (2, 3)])
    two_right = send(from_right, "row", [(2, 1), (1, 0)])

    aligned, kept_a, sent_a = partial_sums(None, (pick, pieces), down_weight, tile, 0, cut, n_row, keeps, False, "sums_a")
    rights, lefts = [(0, 1), (1, 2), (2, 3)], [(3, 2), (2, 1), (1, 0)]
    got_a = [send(sent_a[0], "row", rights), send(sent_a[1], "row", lefts)]
    two = jnp.where(mine_row < 2, two_right, two_left)
    far = send(two, "row", [(2, 3), (1, 0)])

    _, kept_b, sent_b = partial_sums(aligned, None, down_weight, tile, cut, tiles - cut, n_row, keeps, True, "sums_b")
    def carry(onward, last):
        return [send(onward, "row", [(0, 2), (1, 3), (2, 0), (3, 1)]), send(last, "row", [(0, 1), (3, 2)])]

    onward_a, last_a, sent_b = merged(me, *got_a, kept_a[1], *sent_a, sent_b)
    got_b = [send(sent_b[0], "row", rights), send(sent_b[1], "row", lefts)]
    crossed_a = carry(onward_a, last_a)
    onward_b, last_b, _ = merged(me, *got_b, kept_b[1], *sent_b, [])
    crossed_b = carry(onward_b, last_b)
    parts = [[kept_a[0], *got_a, *crossed_a], [kept_b[0], *got_b, *crossed_b]]

    act_pieces = [activations, from_left, from_right, two, far]
    weight_grad = weight_grads(me, aligned, act_pieces, line_choose, [onward_b])
    return weight_grad, totals(me, parts, line_received, [weight_grad])


def solution(mesh):
    in_specs = (P("row", "col"), P("col", "row"), P("col", "row"), P())
    out_specs = (P("col", "row"), P("row", "col"))
    fn = functools.partial(body, mesh.shape["row"], mesh.shape["col"])
    return jax.shard_map(fn, mesh=mesh, in_specs=in_specs, out_specs=out_specs, check_vma=False)
```

```python
import functools

import jax
import jax.numpy as jnp
from jax import lax
from jax.experimental import pallas as pl
from jax.experimental.pallas import tpu as pltpu
from jax.sharding import PartitionSpec as P

LANES = 128
STEPS_PER_OCTAVE = 128.0
TOP = 32766.0
LEAST = 2.0 ** -120
VMEM_LIMIT = 48 * 1024 * 1024
SUB = 256


def tile_of(size, largest):
    tile = largest
    while size % tile:
        tile //= 2
    return tile


def dot(left, right, dims):
    return lax.dot_general(left, right, (dims, ((), ())), preferred_element_type=jnp.float32)


def encode(values):
    most = jnp.maximum(jnp.max(jnp.abs(values), axis=1, keepdims=True), LEAST)
    level = jnp.ceil(jnp.log2(most) * STEPS_PER_OCTAVE) + 1.0
    codes = jnp.round(values * jnp.exp2(level * (-1.0 / STEPS_PER_OCTAVE)) * TOP)
    return codes.astype(jnp.int32).astype(jnp.int16), level


def decode(codes, levels):
    scale = jnp.exp2(levels.astype(jnp.int32).astype(jnp.float32) * (1.0 / STEPS_PER_OCTAVE)) * (1.0 / TOP)
    return codes.astype(jnp.int32).astype(jnp.float32) * scale


def to_levels(levels):
    return levels.astype(jnp.int32).astype(jnp.int16)


def params():
    return pltpu.CompilerParams(vmem_limit_bytes=VMEM_LIMIT)


def cost(flops, moved):
    return pl.CostEstimate(flops=flops, bytes_accessed=moved, transcendentals=0)


def align_rows(pick_ref, pieces, aligned_ref):
    depth = aligned_ref.shape[1]
    chunk = tile_of(depth, 512)
    for at in range(0, depth, chunk):
        cols = slice(at, at + chunk)
        gathered = jnp.concatenate([piece[:, cols] for piece in pieces], axis=0)
        aligned_ref[:, cols] = dot(pick_ref[...], gathered, ((1,), (0,))).astype(jnp.bfloat16)


def sums_kernel(n_pieces, n_groups, n_blocks, tile, *refs):
    refs = list(refs)
    if n_pieces:
        pick_ref = refs.pop(0)
        pieces = [refs.pop(0) for _ in range(n_pieces)]
        blocks = [refs.pop(0) for _ in range(n_blocks)]
        aligned_ref = refs.pop(0)
    else:
        aligned_ref = refs.pop(0)
        blocks = [refs.pop(0) for _ in range(n_blocks)]
    own_ref, *sent, levels_ref = refs
    step = pl.program_id(0)
    rows = own_ref.shape[0]
    width = sent[0].shape[1] - LANES

    @pl.when(step == 0)
    def _():
        if n_pieces:
            align_rows(pick_ref, pieces, aligned_ref)
        levels_ref[...] = jnp.zeros_like(levels_ref)

    lane = lax.broadcasted_iota(jnp.int32, levels_ref.shape, 1)
    levels = levels_ref[...]
    for part, block in enumerate(blocks):
        values = dot(aligned_ref[...], block[...], ((1,), (1,)))
        own_ref[:, part * tile:(part + 1) * tile] = values[:rows]
        codes, level = encode(values[rows:])
        levels = jnp.where(lane == step * n_blocks + part, level, levels)
        cols = pl.ds(pl.multiple_of((step * n_blocks + part) * tile, tile), tile)
        for at, ref in enumerate(sent):
            ref[:, cols] = codes[at * rows:(at + 1) * rows]
    levels_ref[...] = levels

    @pl.when(step == pl.num_programs(0) - 1)
    def _():
        for at, ref in enumerate(sent):
            ref[:, width:] = to_levels(levels[at * rows:(at + 1) * rows])


def partial_sums(aligned, align, weight, tile, first, count, n_groups, name):
    depth = weight.shape[1]
    width = count * tile
    whole = lambda i: (0, 0)
    operands = [align[0], *align[1]] if aligned is None else [aligned]
    total = operands[0].shape[0]
    rows = total // n_groups
    n_sent = n_groups - 1
    n_blocks = 2 if count % 2 == 0 and first % 2 == 0 else 1
    block_at = lambda part: (lambda i: (i * n_blocks + first + part, 0))
    in_specs = [pl.BlockSpec(operand.shape, whole) for operand in operands]
    in_specs += [pl.BlockSpec((tile, depth), block_at(part)) for part in range(n_blocks)]
    out_specs = [pl.BlockSpec((rows, n_blocks * tile), lambda i: (0, i))]
    out_specs += [pl.BlockSpec((rows, width + LANES), whole)] * n_sent
    out_shape = [jax.ShapeDtypeStruct((rows, width), jnp.float32)]
    out_shape += [jax.ShapeDtypeStruct((rows, width + LANES), jnp.int16)] * n_sent
    if aligned is None:
        out_specs.insert(0, pl.BlockSpec((total, depth), whole))
        out_shape.insert(0, jax.ShapeDtypeStruct((total, depth), jnp.bfloat16))
    outs = pl.pallas_call(
        functools.partial(sums_kernel, 0 if aligned is not None else len(align[1]), n_groups, n_blocks, tile),
        grid=(count // n_blocks,), in_specs=in_specs, out_specs=out_specs, out_shape=out_shape,
        scratch_shapes=[pltpu.VMEM((n_sent * rows, LANES), jnp.float32)],
        compiler_params=params(), cost_estimate=cost(2 * total * width * depth, 2 * width * depth), name=name,
    )(*operands, *[weight] * n_blocks)
    if aligned is None:
        aligned, *outs = outs
    return aligned, outs[0], outs[1:]


def weight_kernel(aligned_ref, *refs):
    out_ref = refs[-1]
    left = jnp.concatenate([ref[...] for ref in refs[:-1]], axis=0)
    depth = out_ref.shape[1]
    chunk = tile_of(depth, 1024)
    for at in range(0, depth, chunk):
        cols = slice(at, at + chunk)
        out_ref[:, cols] = dot(left, aligned_ref[:, cols], ((0,), (0,))).astype(jnp.bfloat16)


def weight_grads(aligned, pieces):
    total, depth = aligned.shape
    rows, hidden = pieces[0].shape
    tile = tile_of(hidden, 512)
    return pl.pallas_call(
        weight_kernel,
        grid=(hidden // tile,),
        in_specs=[pl.BlockSpec((total, depth), lambda i: (0, 0))]
        + [pl.BlockSpec((rows, tile), lambda i: (0, i))] * len(pieces),
        out_specs=pl.BlockSpec((tile, depth), lambda i: (i, 0)),
        out_shape=jax.ShapeDtypeStruct((hidden, depth), jnp.bfloat16),
        compiler_params=params(), cost_estimate=cost(2 * total * hidden * depth, 2 * hidden * depth), name="weight_grads",
    )(aligned, *pieces)


def total_kernel(counts, *refs):
    refs = list(refs)
    out_ref = refs.pop()
    base = 0
    for count in counts:
        own_ref, received, refs = refs[0], refs[1:count], refs[count:]
        width = own_ref.shape[1]
        sub = tile_of(width, SUB)
        for at in range(width // sub):
            cols = slice(at * sub, (at + 1) * sub)
            total = own_ref[:, cols]
            for ref in received:
                total = total + decode(ref[:, cols], ref[:, width:][:, at:at + 1])
            out_ref[:, base + at * sub:base + (at + 1) * sub] = total.astype(jnp.bfloat16)
        base += width


def totals(parts, later_than):
    rows = parts[0][0].shape[0]
    hidden = sum(part[0].shape[1] for part in parts)
    flat = [array for part in parts for array in part]
    return pl.pallas_call(
        functools.partial(totals_with_order, len(later_than), [len(part) for part in parts]),
        in_specs=[pl.BlockSpec(memory_space=pltpu.VMEM)] * len(flat) + [pl.BlockSpec(memory_space=pl.ANY)] * len(later_than),
        out_shape=jax.ShapeDtypeStruct((rows, hidden), jnp.bfloat16),
        compiler_params=params(), cost_estimate=cost(rows * hidden * 40, rows * hidden * 14), name="totals",
    )(*flat, *later_than)


def totals_with_order(n_later, counts, *refs):
    total_kernel(counts, *refs[:len(refs) - 1 - n_later], refs[-1])


def send(value, axis, flip, size):
    return lax.ppermute(value, axis, [(i, i ^ flip) for i in range(size)])


def copy_kernel(value_ref, later_ref, out_ref):
    out_ref[...] = value_ref[...]


def copied(value, later_than):
    return pl.pallas_call(
        copy_kernel,
        in_specs=[pl.BlockSpec(memory_space=pltpu.VMEM), pl.BlockSpec(memory_space=pl.ANY)],
        out_shape=jax.ShapeDtypeStruct(value.shape, value.dtype),
        compiler_params=params(), cost_estimate=cost(value.size, value.size * 4), name="copied",
    )(value, later_than)


def same_kernel(*refs):
    pass


def handed_on(values, later_than):
    anywhere = pl.BlockSpec(memory_space=pl.ANY)
    return pl.pallas_call(
        same_kernel,
        in_specs=[anywhere] * (len(values) + len(later_than)), out_specs=[anywhere] * len(values),
        out_shape=[jax.ShapeDtypeStruct(value.shape, value.dtype) for value in values],
        input_output_aliases={at: at for at in range(len(values))},
        compiler_params=params(), cost_estimate=cost(0, 0), name="handed_on",
    )(*values, *later_than)


def gather_cotangent(cotangent, n_col):
    flips = list(range(0, n_col, 2))
    pieces = [send(cotangent, "col", flip, n_col) for flip in flips[1:]]
    pieces = [copied(cotangent, pieces[0])] + pieces
    pieces += [send(piece, "col", 1, n_col) for piece in pieces]
    return pieces, flips + [flip ^ 1 for flip in flips]


def body(n_row, n_col, activations, cotangent, down_weight, row_order):
    rows, hidden = activations.shape
    shard = cotangent.shape[0]
    mine_row, mine_col = lax.axis_index("row"), lax.axis_index("col")

    pieces, flips = gather_cotangent(cotangent, n_col)
    act_pieces = {o: send(activations, "row", o, n_row) for o in [*range(2, n_row, 2), 1]}
    act_pieces[0] = activations

    order = row_order.reshape(n_row, rows)
    order = jnp.concatenate([lax.dynamic_index_in_dim(order, mine_row ^ o, 0, keepdims=False) for o in range(n_row)])
    owner = mine_col ^ jnp.asarray(flips, jnp.int32)
    named = (owner[:, None] * shard + jnp.arange(shard, dtype=jnp.int32)[None, :]).reshape(-1)
    pick = (order[:, None] == named[None, :]).astype(jnp.bfloat16)

    tile = tile_of(hidden, 256)
    tiles = hidden // tile
    cut = tiles * 2 // 7
    aligned, own_a, sent_a = partial_sums(None, (pick, pieces), down_weight, tile, 0, cut, n_row, "sums_a")
    evens = range(2, n_row, 2)
    for o, piece in zip(evens, handed_on([act_pieces[o] for o in evens], [aligned])):
        act_pieces[o], act_pieces[o + 1] = piece, send(piece, "row", 1, n_row)
    got_a = [send(message, "row", o, n_row) for o, message in enumerate(sent_a, 1)]
    _, own_b, sent_b = partial_sums(aligned, None, down_weight, tile, cut, tiles - cut, n_row, "sums_b")
    sent_b = handed_on(sent_b, got_a)
    got_b = [send(message, "row", o, n_row) for o, message in enumerate(sent_b, 1)]
    weight_grad = weight_grads(aligned, [act_pieces[o] for o in range(n_row)])
    return weight_grad, totals([[own_a, *got_a], [own_b, *got_b]], [weight_grad])


def solution(mesh):
    in_specs = (P("row", "col"), P("col", "row"), P("col", "row"), P())
    out_specs = (P("col", "row"), P("row", "col"))
    fn = functools.partial(body, mesh.shape["row"], mesh.shape["col"])
    return jax.shard_map(fn, mesh=mesh, in_specs=in_specs, out_specs=out_specs, check_vma=False)
```

```python
import functools

import jax
import jax.numpy as jnp
from jax import lax
from jax.experimental import pallas as pl
from jax.experimental.pallas import tpu as pltpu
from jax.sharding import PartitionSpec as P

LANES = 128
STEPS_PER_OCTAVE = 128.0
TOP = 32766.0
LEAST = 2.0 ** -120
VMEM_LIMIT = 48 * 1024 * 1024
SUB = 256


def tile_of(size, largest):
    tile = largest
    while size % tile:
        tile //= 2
    return tile


def dot(left, right, dims):
    return lax.dot_general(left, right, (dims, ((), ())), preferred_element_type=jnp.float32)


def encode(values):
    most = jnp.maximum(jnp.max(jnp.abs(values), axis=1, keepdims=True), LEAST)
    level = jnp.ceil(jnp.log2(most) * STEPS_PER_OCTAVE) + 1.0
    codes = jnp.round(values * jnp.exp2(level * (-1.0 / STEPS_PER_OCTAVE)) * TOP)
    return codes.astype(jnp.int32).astype(jnp.int16), level


def decode(codes, levels):
    scale = jnp.exp2(levels.astype(jnp.int32).astype(jnp.float32) * (1.0 / STEPS_PER_OCTAVE)) * (1.0 / TOP)
    return codes.astype(jnp.int32).astype(jnp.float32) * scale


def to_levels(levels):
    return levels.astype(jnp.int32).astype(jnp.int16)


def params():
    return pltpu.CompilerParams(vmem_limit_bytes=VMEM_LIMIT)


def cost(flops, moved):
    return pl.CostEstimate(flops=flops, bytes_accessed=moved, transcendentals=0)


def align_rows(pick_ref, pieces, aligned_ref):
    depth = aligned_ref.shape[1]
    chunk = tile_of(depth, 512)
    for at in range(0, depth, chunk):
        cols = slice(at, at + chunk)
        gathered = jnp.concatenate([piece[:, cols] for piece in pieces], axis=0)
        aligned_ref[:, cols] = dot(pick_ref[...], gathered, ((1,), (0,))).astype(jnp.bfloat16)


def sums_kernel(n_pieces, n_blocks, n_later, tile, *refs):
    refs = list(refs)
    if n_pieces:
        pick_ref = refs.pop(0)
        pieces = [refs.pop(0) for _ in range(n_pieces)]
        blocks = [refs.pop(0) for _ in range(n_blocks)]
        del refs[:n_later]
        aligned_ref = refs.pop(0)
    else:
        aligned_ref = refs.pop(0)
        blocks = [refs.pop(0) for _ in range(n_blocks)]
        del refs[:n_later]
    kept_ref, sent_ref, levels_ref = refs
    step = pl.program_id(0)
    rows = kept_ref.shape[0]
    width = sent_ref.shape[1] - LANES

    @pl.when(step == 0)
    def _():
        if n_pieces:
            align_rows(pick_ref, pieces, aligned_ref)
        levels_ref[...] = jnp.zeros_like(levels_ref)

    lane = lax.broadcasted_iota(jnp.int32, levels_ref.shape, 1)
    levels = levels_ref[...]
    for part, block in enumerate(blocks):
        values = dot(aligned_ref[...], block[...], ((1,), (1,)))
        kept_ref[:, part * tile:(part + 1) * tile] = values[:rows]
        codes, level = encode(values[rows:])
        levels = jnp.where(lane == step * n_blocks + part, level, levels)
        cols = pl.ds(pl.multiple_of((step * n_blocks + part) * tile, tile), tile)
        sent_ref[:, cols] = codes
    levels_ref[...] = levels

    @pl.when(step == pl.num_programs(0) - 1)
    def _():
        sent_ref[:, width:] = to_levels(levels)


def partial_sums(aligned, align, weight, tile, first, count, later_than, name):
    depth = weight.shape[1]
    width = count * tile
    whole = lambda i: (0, 0)
    operands = [align[0], *align[1]] if aligned is None else [aligned]
    total = operands[0].shape[0]
    half = total // 2
    n_blocks = 2 if count % 2 == 0 and first % 2 == 0 else 1
    block_at = lambda part: (lambda i: (i * n_blocks + first + part, 0))
    in_specs = [pl.BlockSpec(operand.shape, whole) for operand in operands]
    in_specs += [pl.BlockSpec((tile, depth), block_at(part)) for part in range(n_blocks)]
    in_specs += [pl.BlockSpec(memory_space=pl.ANY)] * len(later_than)
    out_specs = [pl.BlockSpec((half, n_blocks * tile), lambda i: (0, i)), pl.BlockSpec((half, width + LANES), whole)]
    out_shape = [jax.ShapeDtypeStruct((half, width), jnp.float32), jax.ShapeDtypeStruct((half, width + LANES), jnp.int16)]
    if aligned is None:
        out_specs.insert(0, pl.BlockSpec((total, depth), whole))
        out_shape.insert(0, jax.ShapeDtypeStruct((total, depth), jnp.bfloat16))
    outs = pl.pallas_call(
        functools.partial(sums_kernel, 0 if aligned is not None else len(align[1]), n_blocks, len(later_than), tile),
        grid=(count // n_blocks,), in_specs=in_specs, out_specs=out_specs, out_shape=out_shape,
        scratch_shapes=[pltpu.VMEM((half, LANES), jnp.float32)],
        compiler_params=params(), cost_estimate=cost(2 * total * width * depth, 2 * width * depth), name=name,
    )(*operands, *[weight] * n_blocks, *later_than)
    return outs if aligned is None else (aligned, *outs)


def weight_kernel(n_pieces, n_later, aligned_ref, *refs):
    refs = list(refs)
    pieces = [refs.pop(0) for _ in range(n_pieces)]
    out_ref, left_ref = refs[n_later:]

    @pl.when(pl.program_id(0) == 0)
    def _():
        if n_pieces == 1:
            left_ref[...] = pieces[0][...]
        else:
            left_ref[...] = jnp.concatenate([piece[...] for piece in pieces], axis=0).T

    out_ref[...] = dot(left_ref[...], aligned_ref[...], ((1,), (0,))).astype(jnp.bfloat16)


def weight_grads(aligned, pieces, part, parts, filled, later_than):
    total, depth = aligned.shape
    hidden = pieces[0].size * len(pieces) // total
    tile = tile_of(depth // parts, 512)
    count = depth // parts // tile
    whole = lambda i: (0, 0)
    here = lambda i: (0, i + part * count)
    later = ([] if filled is None else [filled]) + list(later_than)
    return pl.pallas_call(
        functools.partial(weight_kernel, len(pieces), len(later)),
        grid=(count,),
        in_specs=[pl.BlockSpec((total, tile), here)] + [pl.BlockSpec(piece.shape, whole) for piece in pieces]
        + [pl.BlockSpec(memory_space=pl.ANY)] * len(later),
        out_specs=[pl.BlockSpec((hidden, tile), here), pl.BlockSpec((hidden, total), whole)],
        out_shape=[jax.ShapeDtypeStruct((hidden, depth), jnp.bfloat16), jax.ShapeDtypeStruct((hidden, total), jnp.bfloat16)],
        input_output_aliases={} if filled is None else {1 + len(pieces): 0},
        compiler_params=params(), cost_estimate=cost(2 * total * hidden * depth // parts, 2 * hidden * depth // parts),
        name="weight_grads",
    )(aligned, *pieces, *later)


def fold_kernel(kept_ref, got_ref, *refs):
    n_passed = (len(refs) - 2) // 2
    next_ref, sent_ref = refs[n_passed:n_passed + 2]
    width = kept_ref.shape[1]
    half = next_ref.shape[0]
    sub = tile_of(width, SUB)
    lane = lax.broadcasted_iota(jnp.int32, (half, LANES), 1)
    levels = jnp.zeros(lane.shape, jnp.float32)
    got_levels = got_ref[:, width:]
    for at in range(width // sub):
        cols = slice(at * sub, (at + 1) * sub)
        total = kept_ref[:, cols] + decode(got_ref[:, cols], got_levels[:, at:at + 1])
        next_ref[:, cols] = total[:half]
        codes, level = encode(total[half:])
        sent_ref[:, cols] = codes
        levels = jnp.where(lane == at, level, levels)
    sent_ref[:, width:] = to_levels(levels)


def fold(kept, got, passed):
    vmem, anywhere = pl.BlockSpec(memory_space=pltpu.VMEM), pl.BlockSpec(memory_space=pl.ANY)
    rows, width = kept.shape
    kept, sent, *passed = pl.pallas_call(
        fold_kernel,
        in_specs=[vmem] * 2 + [anywhere] * len(passed),
        out_specs=[vmem] * 2 + [anywhere] * len(passed),
        out_shape=[jax.ShapeDtypeStruct((rows // 2, width), kept.dtype), jax.ShapeDtypeStruct((rows // 2, got.shape[1]), got.dtype)]
        + [jax.ShapeDtypeStruct(array.shape, array.dtype) for array in passed],
        input_output_aliases={2 + at: 2 + at for at in range(len(passed))},
        compiler_params=params(), cost_estimate=cost(kept.size * 20, kept.size * 12), name="fold",
    )(kept, got, *passed)
    return kept, sent, passed


def total_kernel(n_parts, *refs):
    out_ref = refs[-1]
    base = 0
    for kept_ref, got_ref in zip(refs[:2 * n_parts:2], refs[1:2 * n_parts:2]):
        width = kept_ref.shape[1]
        sub = tile_of(width, SUB)
        got_levels = got_ref[:, width:]
        for at in range(width // sub):
            cols = slice(at * sub, (at + 1) * sub)
            total = kept_ref[:, cols] + decode(got_ref[:, cols], got_levels[:, at:at + 1])
            out_ref[:, base + at * sub:base + (at + 1) * sub] = total.astype(jnp.bfloat16)
        base += width


def totals(parts, later_than):
    rows = parts[0][0].shape[0]
    hidden = sum(part[0].shape[1] for part in parts)
    flat = [array for part in parts for array in part]
    return pl.pallas_call(
        functools.partial(total_kernel, len(parts)),
        in_specs=[pl.BlockSpec(memory_space=pltpu.VMEM)] * len(flat) + [pl.BlockSpec(memory_space=pl.ANY)] * len(later_than),
        out_shape=jax.ShapeDtypeStruct((rows, hidden), jnp.bfloat16),
        compiler_params=params(), cost_estimate=cost(rows * hidden * 20, rows * hidden * 8), name="totals",
    )(*flat, *later_than)


def send(value, axis, flip, size):
    return lax.ppermute(value, axis, [(i, i ^ flip) for i in range(size)])


def stack_kernel(n_values, *refs):
    out_ref = refs[-1]
    rows = refs[0].shape[0]
    for at, ref in enumerate(refs[:n_values]):
        out_ref[at * rows:(at + 1) * rows] = ref[...]


def stacked(values, later_than=()):
    rows, width = values[0].shape
    return pl.pallas_call(
        functools.partial(stack_kernel, len(values)),
        in_specs=[pl.BlockSpec(memory_space=pltpu.VMEM)] * len(values) + [pl.BlockSpec(memory_space=pl.ANY)] * len(later_than),
        out_shape=jax.ShapeDtypeStruct((len(values) * rows, width), values[0].dtype),
        compiler_params=params(), cost_estimate=cost(0, 4 * len(values) * rows * width), name="stacked",
    )(*values, *later_than)


def same_kernel(*refs):
    pass


def handed_on(values, later_than):
    anywhere = pl.BlockSpec(memory_space=pl.ANY)
    return pl.pallas_call(
        same_kernel,
        in_specs=[anywhere] * (len(values) + len(later_than)), out_specs=[anywhere] * len(values),
        out_shape=[jax.ShapeDtypeStruct(value.shape, value.dtype) for value in values],
        input_output_aliases={at: at for at in range(len(values))},
        compiler_params=params(), cost_estimate=cost(0, 0), name="handed_on",
    )(*values, *later_than)


def gather_cotangent(cotangent, n_col):
    flips = list(range(0, n_col, 2))
    pieces = [cotangent] + [send(cotangent, "col", flip, n_col) for flip in flips[1:]]
    stacks = [stacked(pieces[:2])]
    stacks.append(stacked(pieces[2:], stacks))
    stacks += [send(stack, "col", 1, n_col) for stack in stacks]
    return stacks, flips + [flip ^ 1 for flip in flips]


def halving_order(size):
    order = [0]
    while len(order) < size:
        order = [2 * o for o in order] + [2 * o + 1 for o in order]
    return order


def body(n_row, n_col, activations, cotangent, down_weight, row_order):
    rows, hidden = activations.shape
    shard = cotangent.shape[0]
    mine_row, mine_col = lax.axis_index("row"), lax.axis_index("col")
    offsets = halving_order(n_row)

    pieces, flips = gather_cotangent(cotangent, n_col)
    act_pieces = {o: send(activations, "row", o, n_row) for o in [1, *range(2, n_row, 2)]}
    act_pieces[0] = activations

    order = row_order.reshape(n_row, rows)
    order = jnp.concatenate([lax.dynamic_index_in_dim(order, mine_row ^ o, 0, keepdims=False) for o in offsets])
    owner = mine_col ^ jnp.asarray(flips, jnp.int32)
    named = (owner[:, None] * shard + jnp.arange(shard, dtype=jnp.int32)[None, :]).reshape(-1)
    pick = (order[:, None] == named[None, :]).astype(jnp.bfloat16)

    tile = tile_of(hidden, 256)
    tiles = hidden // tile
    cut = tiles * 3 // 7
    aligned, kept_a, sent_a = partial_sums(None, (pick, pieces), down_weight, tile, 0, cut, [act_pieces[1]], "sums_a")
    got_a = send(sent_a, "row", 1, n_row)
    evens = range(2, n_row, 2)
    for o, piece in zip(evens, handed_on([act_pieces[o] for o in evens], [aligned])):
        act_pieces[o], act_pieces[o + 1] = piece, send(piece, "row", 1, n_row)
    _, kept_b, sent_b = partial_sums(aligned, None, down_weight, tile, cut, tiles - cut, [], "sums_b")

    passed = [sent_b]
    step = 2
    while step < n_row:
        kept_a, sent_a, passed = fold(kept_a, got_a, passed)
        got_a = send(sent_a, "row", step, n_row)
        step *= 2
    got_b = send(passed[0], "row", 1, n_row)
    act_pieces = [act_pieces[o] for o in offsets]
    grad, turned = weight_grads(aligned, act_pieces, 0, 2, None, [sent_a])
    step = 2
    while step < n_row:
        kept_b, sent_b, _ = fold(kept_b, got_b, [])
        got_b = send(sent_b, "row", step, n_row)
        step *= 2
    weight_grad, _ = weight_grads(aligned, [turned], 1, 2, grad, [sent_b])
    return weight_grad, totals([[kept_a, got_a], [kept_b, got_b]], [weight_grad])


def solution(mesh):
    in_specs = (P("row", "col"), P("col", "row"), P("col", "row"), P())
    out_specs = (P("col", "row"), P("row", "col"))
    fn = functools.partial(body, mesh.shape["row"], mesh.shape["col"])
    return jax.shard_map(fn, mesh=mesh, in_specs=in_specs, out_specs=out_specs, check_vma=False)
```

```python
import functools

import jax
import jax.numpy as jnp
from jax import lax
from jax.experimental import pallas as pl
from jax.experimental.pallas import tpu as pltpu
from jax.sharding import PartitionSpec as P

LANES = 128
STEPS_PER_OCTAVE = 128.0
TOP = 32766.0
LEAST = 2.0 ** -120
VMEM_LIMIT = 48 * 1024 * 1024
SUMS_LIMIT = 24 * 1024 * 1024
SMALL_LIMIT = 8 * 1024 * 1024
WIDE_LIMIT = 40 * 1024 * 1024
SUB = 256


def tile_of(size, largest):
    tile = largest
    while size % tile:
        tile //= 2
    return tile


def dot(left, right, dims):
    return lax.dot_general(left, right, (dims, ((), ())), preferred_element_type=jnp.float32)


def encode(values):
    most = jnp.maximum(jnp.max(jnp.abs(values), axis=1, keepdims=True), LEAST)
    level = jnp.ceil(jnp.log2(most) * STEPS_PER_OCTAVE) + 1.0
    codes = jnp.round(values * jnp.exp2(level * (-1.0 / STEPS_PER_OCTAVE)) * TOP)
    return codes.astype(jnp.int32).astype(jnp.int16), level


def decode(codes, levels):
    scale = jnp.exp2(levels.astype(jnp.int32).astype(jnp.float32) * (1.0 / STEPS_PER_OCTAVE)) * (1.0 / TOP)
    return codes.astype(jnp.int32).astype(jnp.float32) * scale


def to_levels(levels):
    return levels.astype(jnp.int32).astype(jnp.int16)


def params(limit=VMEM_LIMIT):
    return pltpu.CompilerParams(vmem_limit_bytes=limit)


def cost(flops, moved):
    return pl.CostEstimate(flops=flops, bytes_accessed=moved, transcendentals=0)


def align_rows(pick_ref, pieces, aligned_ref):
    depth = aligned_ref.shape[1]
    chunk = tile_of(depth, 512)
    for at in range(0, depth, chunk):
        cols = slice(at, at + chunk)
        gathered = jnp.concatenate([piece[:, cols] for piece in pieces], axis=0)
        aligned_ref[:, cols] = dot(pick_ref[...], gathered, ((1,), (0,))).astype(jnp.bfloat16)


def sums_kernel(n_pieces, n_blocks, n_later, resident, tile, *refs):
    refs = list(refs)
    if n_pieces:
        pick_ref = refs.pop(0)
        pieces = [refs.pop(0) for _ in range(n_pieces)]
        blocks = [refs.pop(0) for _ in range(1 if resident else n_blocks)]
        del refs[:n_later]
        aligned_ref = refs.pop(0)
    else:
        aligned_ref = refs.pop(0)
        blocks = [refs.pop(0) for _ in range(1 if resident else n_blocks)]
        del refs[:n_later]
    kept_ref, sent_ref, levels_ref = refs
    step = pl.program_id(0)
    rows = kept_ref.shape[0]
    width = sent_ref.shape[1] - LANES

    @pl.when(step == 0)
    def _():
        if n_pieces:
            align_rows(pick_ref, pieces, aligned_ref)
        levels_ref[...] = jnp.zeros_like(levels_ref)

    lane = lax.broadcasted_iota(jnp.int32, levels_ref.shape, 1)
    levels = levels_ref[...]
    for part in range(n_blocks):
        if resident:
            block = blocks[0][pl.ds(pl.multiple_of((step * n_blocks + part) * tile, tile), tile)]
        else:
            block = blocks[part][...]
        values = dot(aligned_ref[...], block, ((1,), (1,)))
        kept_ref[:, part * tile:(part + 1) * tile] = values[:rows]
        codes, level = encode(values[rows:])
        levels = jnp.where(lane == step * n_blocks + part, level, levels)
        cols = pl.ds(pl.multiple_of((step * n_blocks + part) * tile, tile), tile)
        sent_ref[:, cols] = codes
    levels_ref[...] = levels

    @pl.when(step == pl.num_programs(0) - 1)
    def _():
        sent_ref[:, width:] = to_levels(levels)


def fetch_kernel(weight_ref, out_ref, arrived):
    count = arrived.shape[0]
    rows = out_ref.shape[0] // count
    parts = [pl.ds(at * rows, rows) for at in range(count)]
    copies = [pltpu.make_async_copy(weight_ref.at[part], out_ref.at[part], arrived.at[at]) for at, part in enumerate(parts)]
    for copy in copies:
        copy.start()
    for copy in copies:
        copy.wait()


def fetched(weight, tile, count):
    shape = (count * tile, weight.shape[1])
    return pl.pallas_call(
        fetch_kernel,
        in_specs=[pl.BlockSpec(memory_space=pl.ANY)],
        out_specs=pl.BlockSpec(memory_space=pltpu.VMEM),
        out_shape=jax.ShapeDtypeStruct(shape, weight.dtype),
        scratch_shapes=[pltpu.SemaphoreType.DMA((count,))],
        compiler_params=params(WIDE_LIMIT), cost_estimate=cost(0, 2 * shape[0] * shape[1]), name="fetched",
    )(weight)


def partial_sums(aligned, align, weight, resident, tile, first, count, later_than, name):
    depth = weight.shape[1]
    width = count * tile
    whole = lambda i: (0, 0)
    operands = [align[0], *align[1]] if aligned is None else [aligned]
    total = operands[0].shape[0]
    half = total // 2
    n_blocks = 2 if count % 2 == 0 and first % 2 == 0 else 1
    block_at = lambda part: (lambda i: (i * n_blocks + first + part, 0))
    in_specs = [pl.BlockSpec(operand.shape, whole) for operand in operands]
    if resident:
        in_specs.append(pl.BlockSpec(memory_space=pltpu.VMEM))
    else:
        in_specs += [pl.BlockSpec((tile, depth), block_at(part)) for part in range(n_blocks)]
    in_specs += [pl.BlockSpec(memory_space=pl.ANY)] * len(later_than)
    out_specs = [pl.BlockSpec((half, n_blocks * tile), lambda i: (0, i)), pl.BlockSpec((half, width + LANES), whole)]
    out_shape = [jax.ShapeDtypeStruct((half, width), jnp.float32), jax.ShapeDtypeStruct((half, width + LANES), jnp.int16)]
    if aligned is None:
        out_specs.insert(0, pl.BlockSpec((total, depth), whole))
        out_shape.insert(0, jax.ShapeDtypeStruct((total, depth), jnp.bfloat16))
    outs = pl.pallas_call(
        functools.partial(sums_kernel, 0 if aligned is not None else len(align[1]), n_blocks, len(later_than), resident, tile),
        grid=(count // n_blocks,), in_specs=in_specs, out_specs=out_specs, out_shape=out_shape,
        scratch_shapes=[pltpu.VMEM((half, LANES), jnp.float32)],
        compiler_params=params(SUMS_LIMIT if resident else WIDE_LIMIT), cost_estimate=cost(2 * total * width * depth, 2 * width * depth), name=name,
    )(*operands, *[weight] * (1 if resident else n_blocks), *later_than)
    return outs if aligned is None else (aligned, *outs)


def weight_kernel(n_pieces, aligned_ref, *refs):
    out_ref = refs[-1]
    left = jnp.concatenate([piece[...] for piece in refs[:n_pieces]], axis=0)
    depth = out_ref.shape[1]
    chunk = tile_of(depth, 1024)
    for at in range(0, depth, chunk):
        cols = slice(at, at + chunk)
        out_ref[:, cols] = dot(left, aligned_ref[:, cols], ((0,), (0,))).astype(jnp.bfloat16)


def weight_grads(aligned, pieces, tile, first, count, filled, later_than):
    total, depth = aligned.shape
    rows, hidden = pieces[0].shape
    later = ([] if filled is None else [filled]) + list(later_than)
    return pl.pallas_call(
        functools.partial(weight_kernel, len(pieces)),
        grid=(count,),
        in_specs=[pl.BlockSpec((total, depth), lambda i: (0, 0))]
        + [pl.BlockSpec((rows, tile), lambda i: (0, i + first))] * len(pieces)
        + [pl.BlockSpec(memory_space=pl.ANY)] * len(later),
        out_specs=pl.BlockSpec((tile, depth), lambda i: (i + first, 0)),
        out_shape=jax.ShapeDtypeStruct((hidden, depth), jnp.bfloat16),
        input_output_aliases={} if filled is None else {1 + len(pieces): 0},
        compiler_params=params(), cost_estimate=cost(2 * total * count * tile * depth, 2 * count * tile * depth),
        name="weight_grads",
    )(aligned, *pieces, *later)


def fold_kernel(kept_ref, got_ref, *refs):
    n_passed = (len(refs) - 2) // 2
    next_ref, sent_ref = refs[n_passed:n_passed + 2]
    width = kept_ref.shape[1]
    half = next_ref.shape[0]
    sub = tile_of(width, SUB)
    lane = lax.broadcasted_iota(jnp.int32, (half, LANES), 1)
    levels = jnp.zeros(lane.shape, jnp.float32)
    got_levels = got_ref[:, width:]
    for at in range(width // sub):
        cols = slice(at * sub, (at + 1) * sub)
        total = kept_ref[:, cols] + decode(got_ref[:, cols], got_levels[:, at:at + 1])
        next_ref[:, cols] = total[:half]
        codes, level = encode(total[half:])
        sent_ref[:, cols] = codes
        levels = jnp.where(lane == at, level, levels)
    sent_ref[:, width:] = to_levels(levels)


def fold(kept, got, passed):
    vmem, anywhere = pl.BlockSpec(memory_space=pltpu.VMEM), pl.BlockSpec(memory_space=pl.ANY)
    rows, width = kept.shape
    kept, sent, *passed = pl.pallas_call(
        fold_kernel,
        in_specs=[vmem] * 2 + [anywhere] * len(passed),
        out_specs=[vmem] * 2 + [anywhere] * len(passed),
        out_shape=[jax.ShapeDtypeStruct((rows // 2, width), kept.dtype), jax.ShapeDtypeStruct((rows // 2, got.shape[1]), got.dtype)]
        + [jax.ShapeDtypeStruct(array.shape, array.dtype) for array in passed],
        input_output_aliases={2 + at: 2 + at for at in range(len(passed))},
        compiler_params=params(), cost_estimate=cost(kept.size * 20, kept.size * 12), name="fold",
    )(kept, got, *passed)
    return kept, sent, passed


def total_kernel(n_parts, *refs):
    out_ref = refs[-1]
    base = 0
    for kept_ref, got_ref in zip(refs[:2 * n_parts:2], refs[1:2 * n_parts:2]):
        width = kept_ref.shape[1]
        sub = tile_of(width, SUB)
        got_levels = got_ref[:, width:]
        for at in range(width // sub):
            cols = slice(at * sub, (at + 1) * sub)
            total = kept_ref[:, cols] + decode(got_ref[:, cols], got_levels[:, at:at + 1])
            out_ref[:, base + at * sub:base + (at + 1) * sub] = total.astype(jnp.bfloat16)
        base += width


def totals(parts, later_than):
    rows = parts[0][0].shape[0]
    hidden = sum(part[0].shape[1] for part in parts)
    flat = [array for part in parts for array in part]
    return pl.pallas_call(
        functools.partial(total_kernel, len(parts)),
        in_specs=[pl.BlockSpec(memory_space=pltpu.VMEM)] * len(flat) + [pl.BlockSpec(memory_space=pl.ANY)] * len(later_than),
        out_shape=jax.ShapeDtypeStruct((rows, hidden), jnp.bfloat16),
        compiler_params=params(), cost_estimate=cost(rows * hidden * 20, rows * hidden * 8), name="totals",
    )(*flat, *later_than)


def send(value, axis, flip, size):
    return lax.ppermute(value, axis, [(i, i ^ flip) for i in range(size)])


def stack_kernel(n_values, *refs):
    out_ref = refs[-1]
    rows = refs[0].shape[0]
    for at, ref in enumerate(refs[:n_values]):
        out_ref[at * rows:(at + 1) * rows] = ref[...]


def stacked(values, later_than=()):
    rows, width = values[0].shape
    return pl.pallas_call(
        functools.partial(stack_kernel, len(values)),
        in_specs=[pl.BlockSpec(memory_space=pltpu.VMEM)] * len(values) + [pl.BlockSpec(memory_space=pl.ANY)] * len(later_than),
        out_shape=jax.ShapeDtypeStruct((len(values) * rows, width), values[0].dtype),
        compiler_params=params(SMALL_LIMIT), cost_estimate=cost(0, 4 * len(values) * rows * width), name="stacked",
    )(*values, *later_than)


def same_kernel(*refs):
    pass


def handed_on(values, later_than):
    anywhere = pl.BlockSpec(memory_space=pl.ANY)
    return pl.pallas_call(
        same_kernel,
        in_specs=[anywhere] * (len(values) + len(later_than)), out_specs=[anywhere] * len(values),
        out_shape=[jax.ShapeDtypeStruct(value.shape, value.dtype) for value in values],
        input_output_aliases={at: at for at in range(len(values))},
        compiler_params=params(SMALL_LIMIT), cost_estimate=cost(0, 0), name="handed_on",
    )(*values, *later_than)


def gather_cotangent(cotangent, n_col, later_than):
    flips = list(range(0, n_col, 2))
    pieces = [cotangent] + [send(cotangent, "col", flip, n_col) for flip in flips[1:]]
    stacks = [stacked(pieces[:2], later_than)]
    stacks.append(stacked(pieces[2:], stacks))
    stacks += [send(stack, "col", 1, n_col) for stack in stacks]
    return stacks, flips + [flip ^ 1 for flip in flips]


def halving_order(size):
    order = [0]
    while len(order) < size:
        order = [2 * o for o in order] + [2 * o + 1 for o in order]
    return order


def body(n_row, n_col, activations, cotangent, down_weight, row_order):
    rows, hidden = activations.shape
    shard = cotangent.shape[0]
    mine_row, mine_col = lax.axis_index("row"), lax.axis_index("col")
    offsets = halving_order(n_row)

    tile = tile_of(hidden, 256)
    tiles = hidden // tile
    cut = tiles * 3 // 7
    weight_a = fetched(down_weight, tile, cut)
    pieces, flips = gather_cotangent(cotangent, n_col, [weight_a])
    act_pieces = {o: send(activations, "row", o, n_row) for o in [1, *range(2, n_row, 2)]}
    act_pieces[0] = activations

    order = row_order.reshape(n_row, rows)
    order = jnp.concatenate([lax.dynamic_index_in_dim(order, mine_row ^ o, 0, keepdims=False) for o in offsets])
    owner = mine_col ^ jnp.asarray(flips, jnp.int32)
    named = (owner[:, None] * shard + jnp.arange(shard, dtype=jnp.int32)[None, :]).reshape(-1)
    pick = (order[:, None] == named[None, :]).astype(jnp.bfloat16)

    aligned, kept_a, sent_a = partial_sums(None, (pick, pieces), weight_a, True, tile, 0, cut, [], "sums_a")
    got_a = send(sent_a, "row", 1, n_row)
    evens = range(2, n_row, 2)
    for o, piece in zip(evens, handed_on([act_pieces[o] for o in evens], [aligned])):
        act_pieces[o], act_pieces[o + 1] = piece, send(piece, "row", 1, n_row)
    _, kept_b, sent_b = partial_sums(aligned, None, down_weight, False, tile, cut, tiles - cut, [act_pieces[1]], "sums_b")

    passed = [sent_b]
    step = 2
    while step < n_row:
        kept_a, sent_a, passed = fold(kept_a, got_a, passed)
        got_a = send(sent_a, "row", step, n_row)
        step *= 2
    got_b = send(passed[0], "row", 1, n_row)
    act_pieces = [act_pieces[o] for o in offsets]
    grad_tile = tile_of(hidden, 512)
    grad_tiles = hidden // grad_tile
    grad_cut = grad_tiles * 4 // 7
    grad = weight_grads(aligned, act_pieces, grad_tile, 0, grad_cut, None, [sent_a])
    step = 2
    while step < n_row:
        kept_b, sent_b, _ = fold(kept_b, got_b, [])
        got_b = send(sent_b, "row", step, n_row)
        step *= 2
    weight_grad = weight_grads(aligned, act_pieces, grad_tile, grad_cut, grad_tiles - grad_cut, grad, [sent_b])
    return weight_grad, totals([[kept_a, got_a], [kept_b, got_b]], [weight_grad])


def solution(mesh):
    in_specs = (P("row", "col"), P("col", "row"), P("col", "row"), P())
    out_specs = (P("col", "row"), P("row", "col"))
    fn = functools.partial(body, mesh.shape["row"], mesh.shape["col"])
    return jax.shard_map(fn, mesh=mesh, in_specs=in_specs, out_specs=out_specs, check_vma=False)
```

```python
import functools

import jax
import jax.numpy as jnp
from jax import lax
from jax.experimental import pallas as pl
from jax.experimental.pallas import tpu as pltpu
from jax.sharding import PartitionSpec as P

LANES = 128
STEPS_PER_OCTAVE = 128.0
TOP = 32766.0
LEAST = 2.0 ** -120
VMEM_LIMIT = 48 * 1024 * 1024
SUMS_LIMIT = 36 * 1024 * 1024
SLOTS = 4
SUB = 256


def tile_of(size, largest):
    tile = largest
    while size % tile:
        tile //= 2
    return tile


def dot(left, right, dims):
    return lax.dot_general(left, right, (dims, ((), ())), preferred_element_type=jnp.float32)


def encode(values):
    most = jnp.maximum(jnp.max(jnp.abs(values), axis=1, keepdims=True), LEAST)
    level = jnp.ceil(jnp.log2(most) * STEPS_PER_OCTAVE) + 1.0
    codes = jnp.round(values * jnp.exp2(level * (-1.0 / STEPS_PER_OCTAVE)) * TOP)
    return codes.astype(jnp.int32).astype(jnp.int16), level


def decode(codes, levels):
    scale = jnp.exp2(levels.astype(jnp.int32).astype(jnp.float32) * (1.0 / STEPS_PER_OCTAVE)) * (1.0 / TOP)
    return codes.astype(jnp.int32).astype(jnp.float32) * scale


def to_levels(levels):
    return levels.astype(jnp.int32).astype(jnp.int16)


def params(limit=VMEM_LIMIT):
    return pltpu.CompilerParams(vmem_limit_bytes=limit)


def cost(flops, moved):
    return pl.CostEstimate(flops=flops, bytes_accessed=moved, transcendentals=0)


def align_rows(pick_ref, pieces, aligned_ref):
    depth = aligned_ref.shape[1]
    chunk = tile_of(depth, 512)
    for at in range(0, depth, chunk):
        cols = slice(at, at + chunk)
        gathered = jnp.concatenate([piece[:, cols] for piece in pieces], axis=0)
        aligned_ref[:, cols] = dot(pick_ref[...], gathered, ((1,), (0,))).astype(jnp.bfloat16)


def sums_kernel(n_pieces, n_blocks, n_later, first, coded, kept_rows, sent_rows, tile, *refs):
    refs = list(refs)
    if n_pieces:
        pick_ref = refs.pop(0)
        pieces = [refs.pop(0) for _ in range(n_pieces)]
        weight_ref = refs.pop(0)
        del refs[:n_later]
        aligned_ref = refs.pop(0)
    else:
        aligned_ref = refs.pop(0)
        weight_ref = refs.pop(0)
        del refs[:n_later]
    kept = [refs.pop(0) for _ in kept_rows]
    sent = [refs.pop(0) for _ in sent_rows]
    levels_ref, held_ref, arrived = refs
    step = pl.program_id(0)
    width = sent[0].shape[1] - LANES

    def fetch(at):
        rows = pl.ds(pl.multiple_of((first + at) * tile, tile), tile)
        return pltpu.make_async_copy(weight_ref.at[rows], held_ref.at[at], arrived.at[at])

    @pl.when(step == 0)
    def _():
        for at in range(held_ref.shape[0]):
            fetch(at).start()
        if n_pieces:
            align_rows(pick_ref, pieces, aligned_ref)
        levels_ref[...] = jnp.zeros_like(levels_ref)

    lane = lax.broadcasted_iota(jnp.int32, levels_ref.shape, 1)
    levels = levels_ref[...]
    for part in range(n_blocks):
        at = step * n_blocks + part
        fetch(at).wait()
        values = dot(aligned_ref[...], held_ref[at], ((1,), (1,)))
        for ref, rows in zip(kept, kept_rows):
            ref[:, part * tile:(part + 1) * tile] = values[rows]
        codes, level = encode(values[coded:])
        levels = jnp.where(lane == at, level, levels)
        cols = pl.ds(pl.multiple_of(at * tile, tile), tile)
        for ref, rows in zip(sent, sent_rows):
            ref[:, cols] = codes[rows.start - coded:rows.stop - coded]
    levels_ref[...] = levels

    @pl.when(step == pl.num_programs(0) - 1)
    def _():
        for ref, rows in zip(sent, sent_rows):
            ref[:, width:] = to_levels(levels[rows.start - coded:rows.stop - coded])


def partial_sums(aligned, align, weight, tile, first, count, kept_rows, sent_rows, later_than, name):
    depth = weight.shape[1]
    width = count * tile
    whole = lambda i: (0, 0)
    operands = [align[0], *align[1]] if aligned is None else [aligned]
    total = operands[0].shape[0]
    coded = min(rows.start for rows in sent_rows)
    n_blocks = 2 if count % 2 == 0 else 1
    heights = lambda spans: [span.stop - span.start for span in spans]
    anywhere = pl.BlockSpec(memory_space=pl.ANY)
    in_specs = [pl.BlockSpec(operand.shape, whole) for operand in operands] + [anywhere] * (1 + len(later_than))
    out_specs = [pl.BlockSpec((height, n_blocks * tile), lambda i: (0, i)) for height in heights(kept_rows)]
    out_specs += [pl.BlockSpec((height, width + LANES), whole) for height in heights(sent_rows)]
    out_shape = [jax.ShapeDtypeStruct((height, width), jnp.float32) for height in heights(kept_rows)]
    out_shape += [jax.ShapeDtypeStruct((height, width + LANES), jnp.int16) for height in heights(sent_rows)]
    if aligned is None:
        out_specs.insert(0, pl.BlockSpec((total, depth), whole))
        out_shape.insert(0, jax.ShapeDtypeStruct((total, depth), jnp.bfloat16))
    outs = pl.pallas_call(
        functools.partial(
            sums_kernel, 0 if aligned is not None else len(align[1]), n_blocks, len(later_than), first, coded, kept_rows, sent_rows, tile),
        grid=(count // n_blocks,), in_specs=in_specs, out_specs=out_specs, out_shape=out_shape,
        scratch_shapes=[
            pltpu.VMEM((total - coded, LANES), jnp.float32),
            pltpu.VMEM((count, tile, depth), weight.dtype),
            pltpu.SemaphoreType.DMA((count,)),
        ],
        compiler_params=params(SUMS_LIMIT), cost_estimate=cost(2 * total * width * depth, 2 * width * depth), name=name,
    )(*operands, weight, *later_than)
    if aligned is None:
        aligned, *outs = outs
    return aligned, outs[:len(kept_rows)], outs[len(kept_rows):]


def weight_kernel(places, first, n_later, tile, aligned_ref, *refs):
    n_pieces = sum(len(place) for place in places)
    pieces = [ref[...] for ref in refs[:n_pieces]]
    out_ref, held_ref, left_sem = refs[n_pieces + n_later:]
    step = pl.program_id(0)
    last = pl.num_programs(0) - 1
    slots = held_ref.shape[0]

    def leave(at):
        rows = pl.ds(pl.multiple_of((first + at) * tile, tile), tile)
        slot = lax.rem(at, slots)
        return pltpu.make_async_copy(held_ref.at[slot], out_ref.at[rows], left_sem.at[slot])

    @pl.when(step >= slots)
    def _():
        leave(step - slots).wait()

    blocks = [functools.reduce(lambda x, y: x + y, [pieces[at] for at in place]) for place in places]
    left = jnp.concatenate(blocks, axis=0)
    depth = aligned_ref.shape[1]
    chunk = tile_of(depth, 1024)
    block = held_ref.at[lax.rem(step, slots)]
    for at in range(0, depth, chunk):
        cols = slice(at, at + chunk)
        block[:, cols] = dot(left, aligned_ref[:, cols], ((0,), (0,))).astype(jnp.bfloat16)
    leave(step).start()

    @pl.when(step == last)
    def _():
        for back in range(slots - 1, -1, -1):
            @pl.when(last >= back)
            def _():
                leave(last - back).wait()


def weight_grads(aligned, pieces, places, tile, first, count, filled, later_than):
    total, depth = aligned.shape
    rows, hidden = pieces[0].shape
    later = ([] if filled is None else [filled]) + list(later_than)
    return pl.pallas_call(
        functools.partial(weight_kernel, places, first, len(later), tile),
        grid=(count,),
        in_specs=[pl.BlockSpec((total, depth), lambda i: (0, 0))]
        + [pl.BlockSpec((rows, tile), lambda i: (0, i + first))] * len(pieces)
        + [pl.BlockSpec(memory_space=pl.ANY)] * len(later),
        out_specs=pl.BlockSpec(memory_space=pl.ANY),
        out_shape=jax.ShapeDtypeStruct((hidden, depth), jnp.bfloat16),
        scratch_shapes=[pltpu.VMEM((SLOTS, tile, depth), jnp.bfloat16), pltpu.SemaphoreType.DMA((SLOTS,))],
        input_output_aliases={} if filled is None else {1 + len(pieces): 0},
        compiler_params=params(), cost_estimate=cost(2 * total * count * tile * depth, 2 * count * tile * depth),
        name="weight_grads",
    )(aligned, *pieces, *later)


def fold_kernel(kept_ref, got_ref, *refs):
    n_passed = (len(refs) - 2) // 2
    next_ref, sent_ref = refs[n_passed:n_passed + 2]
    width = kept_ref.shape[1]
    half = next_ref.shape[0]
    sub = tile_of(width, SUB)
    lane = lax.broadcasted_iota(jnp.int32, (half, LANES), 1)
    levels = jnp.zeros(lane.shape, jnp.float32)
    got_levels = got_ref[:, width:]
    for at in range(width // sub):
        cols = slice(at * sub, (at + 1) * sub)
        total = kept_ref[:, cols] + decode(got_ref[:, cols], got_levels[:, at:at + 1])
        next_ref[:, cols] = total[:half]
        codes, level = encode(total[half:])
        sent_ref[:, cols] = codes
        levels = jnp.where(lane == at, level, levels)
    sent_ref[:, width:] = to_levels(levels)


def fold(kept, got, passed):
    vmem, anywhere = pl.BlockSpec(memory_space=pltpu.VMEM), pl.BlockSpec(memory_space=pl.ANY)
    rows, width = kept.shape
    kept, sent, *passed = pl.pallas_call(
        fold_kernel,
        in_specs=[vmem] * 2 + [anywhere] * len(passed),
        out_specs=[vmem] * 2 + [anywhere] * len(passed),
        out_shape=[jax.ShapeDtypeStruct((rows // 2, width), kept.dtype), jax.ShapeDtypeStruct((rows // 2, got.shape[1]), got.dtype)]
        + [jax.ShapeDtypeStruct(array.shape, array.dtype) for array in passed],
        input_output_aliases={2 + at: 2 + at for at in range(len(passed))},
        compiler_params=params(), cost_estimate=cost(kept.size * 20, kept.size * 12), name="fold",
    )(kept, got, *passed)
    return kept, sent, passed


def line_fold_kernel(kept_ref, got_ref, two_ref, three_ref):
    width = kept_ref.shape[1]
    rows = two_ref.shape[0]
    sub = tile_of(width, SUB)
    lane = lax.broadcasted_iota(jnp.int32, (2 * rows, LANES), 1)
    levels = jnp.zeros(lane.shape, jnp.float32)
    got_levels = got_ref[rows:, width:]
    for at in range(width // sub):
        cols = slice(at * sub, (at + 1) * sub)
        came = decode(got_ref[rows:, cols], got_levels[:, at:at + 1])
        came = jnp.concatenate([came[rows:], came[:rows]], axis=0)
        codes, level = encode(kept_ref[:, cols] + came)
        two_ref[:, cols] = codes[:rows]
        three_ref[:, cols] = codes[rows:]
        levels = jnp.where(lane == at, level, levels)
    two_ref[:, width:] = to_levels(levels[:rows])
    three_ref[:, width:] = to_levels(levels[rows:])


def line_fold(kept, got):
    rows = kept.shape[0] // 2
    like = jax.ShapeDtypeStruct((rows, got.shape[1]), got.dtype)
    return pl.pallas_call(
        line_fold_kernel, out_shape=[like, like], compiler_params=params(),
        cost_estimate=cost(kept.size * 20, kept.size * 12), name="line_fold",
    )(kept, got)


def total_kernel(counts, *refs):
    refs = list(refs)
    out_ref = refs.pop()
    base = 0
    for count in counts:
        kept_ref, got, refs = refs[0], refs[1:count], refs[count:]
        rows, width = kept_ref.shape
        sub = tile_of(width, SUB)
        for at in range(width // sub):
            cols = slice(at * sub, (at + 1) * sub)
            total = kept_ref[:, cols]
            for ref in got:
                total = total + decode(ref[:rows, cols], ref[:rows, width:][:, at:at + 1])
            out_ref[:, base + at * sub:base + (at + 1) * sub] = total.astype(jnp.bfloat16)
        base += width


def totals(parts, later_than):
    rows = parts[0][0].shape[0]
    hidden = sum(part[0].shape[1] for part in parts)
    flat = [array for part in parts for array in part]
    return pl.pallas_call(
        functools.partial(total_kernel, [len(part) for part in parts]),
        in_specs=[pl.BlockSpec(memory_space=pltpu.VMEM)] * len(flat) + [pl.BlockSpec(memory_space=pl.ANY)] * len(later_than),
        out_shape=jax.ShapeDtypeStruct((rows, hidden), jnp.bfloat16),
        compiler_params=params(), cost_estimate=cost(rows * hidden * 40, rows * hidden * 14), name="totals",
    )(*flat, *later_than)


def send(value, axis, flip, size):
    return lax.ppermute(value, axis, [(i, i ^ flip) for i in range(size)])


def stack_kernel(n_values, *refs):
    out_ref = refs[-1]
    rows = refs[0].shape[0]
    for at, ref in enumerate(refs[:n_values]):
        out_ref[at * rows:(at + 1) * rows] = ref[...]


def stacked(values, later_than=()):
    rows, width = values[0].shape
    return pl.pallas_call(
        functools.partial(stack_kernel, len(values)),
        in_specs=[pl.BlockSpec(memory_space=pltpu.VMEM)] * len(values) + [pl.BlockSpec(memory_space=pl.ANY)] * len(later_than),
        out_shape=jax.ShapeDtypeStruct((len(values) * rows, width), values[0].dtype),
        compiler_params=params(), cost_estimate=cost(0, 4 * len(values) * rows * width), name="stacked",
    )(*values, *later_than)


def same_kernel(*refs):
    pass


def handed_on(values, later_than):
    anywhere = pl.BlockSpec(memory_space=pl.ANY)
    return pl.pallas_call(
        same_kernel,
        in_specs=[anywhere] * (len(values) + len(later_than)), out_specs=[anywhere] * len(values),
        out_shape=[jax.ShapeDtypeStruct(value.shape, value.dtype) for value in values],
        input_output_aliases={at: at for at in range(len(values))},
        compiler_params=params(), cost_estimate=cost(0, 0), name="handed_on",
    )(*values, *later_than)


def gather_cotangent(cotangent, n_col):
    flips = list(range(0, n_col, 2))
    pieces = [cotangent] + [send(cotangent, "col", flip, n_col) for flip in flips[1:]]
    stacks = [stacked(pieces[:2])]
    stacks.append(stacked(pieces[2:], stacks))
    stacks += [send(stack, "col", 1, n_col) for stack in stacks]
    return stacks, flips + [flip ^ 1 for flip in flips]


def halving_order(size):
    order = [0]
    while len(order) < size:
        order = [2 * o for o in order] + [2 * o + 1 for o in order]
    return order


def part_slices(tiles, shares):
    ends = [tiles * sum(shares[:at]) // 7 for at in range(len(shares) + 1)]
    return [(first, last - first) for first, last in zip(ends, ends[1:])]


def halving_sums(align, weight, act_pieces, n_row, offsets, tile):
    total = align[0].shape[0]
    kept_rows, sent_rows = [slice(0, total // 2)], [slice(total // 2, total)]
    count = weight.shape[0] // tile
    aligned, [kept], [sent] = partial_sums(None, align, weight, tile, 0, count, kept_rows, sent_rows, [], "sums")
    got = send(sent, "row", 1, n_row)
    evens = range(2, n_row, 2)
    for o, piece in zip(evens, handed_on([act_pieces[o] for o in evens], [aligned])):
        act_pieces[o], act_pieces[o + 1] = piece, send(piece, "row", 1, n_row)
    step = 2
    while step < n_row:
        kept, sent, _ = fold(kept, got, [])
        got = send(sent, "row", step, n_row)
        step *= 2
    places = [[at] for at in range(n_row)]
    weight_grad = weight_grads(aligned, [act_pieces[o] for o in offsets], places, tile, 0, count, None, [sent])
    return weight_grad, totals([[kept, got]], [weight_grad])


def line_sums(align, weight, activations, act_pieces, tile):
    total = align[0].shape[0]
    rows = total // 4
    kept_rows = [slice(0, rows), slice(2 * rows, total)]
    sent_rows = [slice(rows, total), slice(rows, 2 * rows)]
    tiles = weight.shape[0] // tile
    first_part, second_part = part_slices(tiles, (3, 4))
    inwards, outwards, middle = [(0, 1), (3, 2)], [(1, 0), (2, 3)], [(1, 2), (2, 1)]

    def spread(sent):
        return lax.ppermute(sent[0], "row", inwards), lax.ppermute(sent[1], "row", outwards)

    def cross(kept, got):
        two, three = line_fold(kept, got)
        return two, lax.ppermute(three, "row", middle), lax.ppermute(two, "row", [(1, 3), (2, 0)])

    aligned, kept_a, sent_a = partial_sums(None, align, weight, tile, *first_part, kept_rows, sent_rows, [], "sums_a")
    got_a = spread(sent_a)
    act_pieces[2], activations = handed_on([act_pieces[2], stacked([activations], align[1][:1])], [aligned])
    across = lax.ppermute(act_pieces[2], "row", outwards)
    near = lax.ppermute(activations, "row", middle)
    _, kept_b, sent_b = partial_sums(aligned, None, weight, tile, *second_part, kept_rows, sent_rows, [act_pieces[1]], "sums_b")
    sent_b = handed_on(sent_b, [got_a[1]])
    got_b = spread(sent_b)
    two_a, *crossed_a = cross(kept_a[1], got_a[0])
    pieces = [activations, act_pieces[1], act_pieces[2], across, near]
    places = [[0], [1], [2], [3, 4]]
    (first_a, count_a), (first_b, count_b) = part_slices(tiles, (4, 3))
    grad = weight_grads(aligned, pieces, places, tile, first_a, count_a, None, [two_a])
    two_b, *crossed_b = cross(kept_b[1], got_b[0])
    weight_grad = weight_grads(aligned, pieces, places, tile, first_b, count_b, grad, [two_b])
    return weight_grad, totals([[kept_a[0], *got_a, *crossed_a], [kept_b[0], *got_b, *crossed_b]], [weight_grad])


def body(n_row, n_col, activations, cotangent, down_weight, row_order):
    rows, hidden = activations.shape
    shard = cotangent.shape[0]
    mine_row, mine_col = lax.axis_index("row"), lax.axis_index("col")
    offsets = list(range(4)) if n_row == 4 else halving_order(n_row)

    pieces, flips = gather_cotangent(cotangent, n_col)
    act_pieces = {o: send(activations, "row", o, n_row) for o in [1, *range(2, n_row, 2)]}
    act_pieces[0] = activations

    order = row_order.reshape(n_row, rows)
    order = jnp.concatenate([lax.dynamic_index_in_dim(order, mine_row ^ o, 0, keepdims=False) for o in offsets])
    owner = mine_col ^ jnp.asarray(flips, jnp.int32)
    named = (owner[:, None] * shard + jnp.arange(shard, dtype=jnp.int32)[None, :]).reshape(-1)
    pick = (order[:, None] == named[None, :]).astype(jnp.bfloat16)

    tile = tile_of(hidden, 256)
    if n_row == 4:
        return line_sums((pick, pieces), down_weight, activations, act_pieces, tile)
    return halving_sums((pick, pieces), down_weight, act_pieces, n_row, offsets, tile)


def solution(mesh):
    in_specs = (P("row", "col"), P("col", "row"), P("col", "row"), P())
    out_specs = (P("col", "row"), P("row", "col"))
    fn = functools.partial(body, mesh.shape["row"], mesh.shape["col"])
    return jax.shard_map(fn, mesh=mesh, in_specs=in_specs, out_specs=out_specs, check_vma=False)
```

```python
import functools

import jax
import jax.numpy as jnp
from jax import lax
from jax.experimental import pallas as pl
from jax.experimental.pallas import tpu as pltpu
from jax.sharding import PartitionSpec as P

LANES = 128
STEPS_PER_OCTAVE = 128.0
TOP = 32766.0
LEAST = 2.0 ** -120
VMEM_LIMIT = 48 * 1024 * 1024
FETCH_LIMIT = 32 * 1024 * 1024
SMALL_LIMIT = 8 * 1024 * 1024
SLOTS = 4
SUB = 256


def tile_of(size, largest):
    tile = largest
    while size % tile:
        tile //= 2
    return tile


def dot(left, right, dims):
    return lax.dot_general(left, right, (dims, ((), ())), preferred_element_type=jnp.float32)


def encode(values):
    most = jnp.maximum(jnp.max(jnp.abs(values), axis=1, keepdims=True), LEAST)
    level = jnp.ceil(jnp.log2(most) * STEPS_PER_OCTAVE) + 1.0
    codes = jnp.round(values * jnp.exp2(level * (-1.0 / STEPS_PER_OCTAVE)) * TOP)
    return codes.astype(jnp.int32).astype(jnp.int16), level


def decode(codes, levels):
    scale = jnp.exp2(levels.astype(jnp.int32).astype(jnp.float32) * (1.0 / STEPS_PER_OCTAVE)) * (1.0 / TOP)
    return codes.astype(jnp.int32).astype(jnp.float32) * scale


def to_levels(levels):
    return levels.astype(jnp.int32).astype(jnp.int16)


def params(limit=VMEM_LIMIT):
    return pltpu.CompilerParams(vmem_limit_bytes=limit)


def cost(flops, moved):
    return pl.CostEstimate(flops=flops, bytes_accessed=moved, transcendentals=0)


def align_rows(pick_ref, pieces, aligned_ref):
    depth = aligned_ref.shape[1]
    chunk = tile_of(depth, 512)
    for at in range(0, depth, chunk):
        cols = slice(at, at + chunk)
        gathered = jnp.concatenate([piece[:, cols] for piece in pieces], axis=0)
        aligned_ref[:, cols] = dot(pick_ref[...], gathered, ((1,), (0,))).astype(jnp.bfloat16)


def fetch_kernel(weight_ref, *refs):
    out_ref, arrived = refs[-2:]
    count = arrived.shape[0]
    rows = out_ref.shape[0] // count
    parts = [pl.ds(at * rows, rows) for at in range(count)]
    copies = [pltpu.make_async_copy(weight_ref.at[part], out_ref.at[part], arrived.at[at]) for at, part in enumerate(parts)]
    for copy in copies:
        copy.start()
    for copy in copies:
        copy.wait()


def fetched(weight, tile, count, later_than):
    shape = (count * tile, weight.shape[1])
    return pl.pallas_call(
        fetch_kernel,
        in_specs=[pl.BlockSpec(memory_space=pl.ANY)] * (1 + len(later_than)),
        out_specs=pl.BlockSpec(memory_space=pltpu.VMEM),
        out_shape=jax.ShapeDtypeStruct(shape, weight.dtype),
        scratch_shapes=[pltpu.SemaphoreType.DMA((count,))],
        compiler_params=params(FETCH_LIMIT), cost_estimate=cost(0, 2 * shape[0] * shape[1]), name="fetched",
    )(weight, *later_than)


def sums_kernel(n_pieces, n_blocks, n_later, resident, coded, kept_rows, sent_rows, tile, *refs):
    refs = list(refs)
    if n_pieces:
        pick_ref = refs.pop(0)
        pieces = [refs.pop(0) for _ in range(n_pieces)]
    else:
        aligned_ref = refs.pop(0)
    weights = [refs.pop(0) for _ in range(1 if resident else n_blocks)]
    del refs[:n_later]
    if n_pieces:
        aligned_ref = refs.pop(0)
    kept = [refs.pop(0) for _ in kept_rows]
    sent = [refs.pop(0) for _ in sent_rows]
    levels_ref, = refs
    step = pl.program_id(0)
    width = sent[0].shape[1] - LANES

    @pl.when(step == 0)
    def _():
        if n_pieces:
            align_rows(pick_ref, pieces, aligned_ref)
        levels_ref[...] = jnp.zeros_like(levels_ref)

    lane = lax.broadcasted_iota(jnp.int32, levels_ref.shape, 1)
    levels = levels_ref[...]
    for part in range(n_blocks):
        at = step * n_blocks + part
        cols = pl.ds(pl.multiple_of(at * tile, tile), tile)
        block = weights[0][cols] if resident else weights[part][...]
        values = dot(aligned_ref[...], block, ((1,), (1,)))
        for ref, rows in zip(kept, kept_rows):
            ref[:, part * tile:(part + 1) * tile] = values[rows]
        codes, level = encode(values[coded:])
        levels = jnp.where(lane == at, level, levels)
        for ref, rows in zip(sent, sent_rows):
            ref[:, cols] = codes[rows.start - coded:rows.stop - coded]
    levels_ref[...] = levels

    @pl.when(step == pl.num_programs(0) - 1)
    def _():
        for ref, rows in zip(sent, sent_rows):
            ref[:, width:] = to_levels(levels[rows.start - coded:rows.stop - coded])


def partial_sums(aligned, align, weight, resident, tile, first, count, kept_rows, sent_rows, later_than, name):
    depth = weight.shape[1]
    width = count * tile
    whole = lambda i: (0, 0)
    operands = [align[0], *align[1]] if aligned is None else [aligned]
    total = operands[0].shape[0]
    coded = min(rows.start for rows in sent_rows)
    n_blocks = 2 if count % 2 == 0 and first % 2 == 0 else 1
    block_at = lambda part: (lambda i: (i * n_blocks + first + part, 0))
    heights = lambda spans: [span.stop - span.start for span in spans]
    in_specs = [pl.BlockSpec(operand.shape, whole) for operand in operands]
    if resident:
        in_specs.append(pl.BlockSpec(memory_space=pltpu.VMEM))
    else:
        in_specs += [pl.BlockSpec((tile, depth), block_at(part)) for part in range(n_blocks)]
    in_specs += [pl.BlockSpec(memory_space=pl.ANY)] * len(later_than)
    out_specs = [pl.BlockSpec((height, n_blocks * tile), lambda i: (0, i)) for height in heights(kept_rows)]
    out_specs += [pl.BlockSpec((height, width + LANES), whole) for height in heights(sent_rows)]
    out_shape = [jax.ShapeDtypeStruct((height, width), jnp.float32) for height in heights(kept_rows)]
    out_shape += [jax.ShapeDtypeStruct((height, width + LANES), jnp.int16) for height in heights(sent_rows)]
    if aligned is None:
        out_specs.insert(0, pl.BlockSpec((total, depth), whole))
        out_shape.insert(0, jax.ShapeDtypeStruct((total, depth), jnp.bfloat16))
    outs = pl.pallas_call(
        functools.partial(
            sums_kernel, 0 if aligned is not None else len(align[1]), n_blocks, len(later_than), resident, coded, kept_rows, sent_rows, tile),
        grid=(count // n_blocks,), in_specs=in_specs, out_specs=out_specs, out_shape=out_shape,
        scratch_shapes=[pltpu.VMEM((total - coded, LANES), jnp.float32)],
        compiler_params=params(2 * SMALL_LIMIT if resident else VMEM_LIMIT),
        cost_estimate=cost(2 * total * width * depth, 2 * width * depth), name=name,
    )(*operands, *[weight] * (1 if resident else n_blocks), *later_than)
    if aligned is None:
        aligned, *outs = outs
    return aligned, outs[:len(kept_rows)], outs[len(kept_rows):]


def line_places(pieces):
    own, left, right, two, far = pieces
    even = lax.rem(lax.axis_index("row"), 2) == 0
    return [own, jnp.where(even, right, left), two, far + jnp.where(even, left, right)]


def weight_kernel(n_pieces, place, first, n_later, tile, aligned_ref, *refs):
    pieces = [ref[...] for ref in refs[:n_pieces]]
    out_ref, held_ref, left_sem = refs[n_pieces + n_later:]
    step = pl.program_id(0)
    last = pl.num_programs(0) - 1
    slots = held_ref.shape[0]

    def leave(at):
        rows = pl.ds(pl.multiple_of((first + at) * tile, tile), tile)
        slot = lax.rem(at, slots)
        return pltpu.make_async_copy(held_ref.at[slot], out_ref.at[rows], left_sem.at[slot])

    @pl.when(step >= slots)
    def _():
        leave(step - slots).wait()

    left = jnp.concatenate(place(pieces), axis=0)
    depth = aligned_ref.shape[1]
    chunk = tile_of(depth, 1024)
    block = held_ref.at[lax.rem(step, slots)]
    for at in range(0, depth, chunk):
        cols = slice(at, at + chunk)
        block[:, cols] = dot(left, aligned_ref[:, cols], ((0,), (0,))).astype(jnp.bfloat16)
    leave(step).start()

    @pl.when(step == last)
    def _():
        for back in range(slots - 1, -1, -1):
            @pl.when(last >= back)
            def _():
                leave(last - back).wait()


def weight_grads(aligned, pieces, place, tile, first, count, filled, later_than):
    total, depth = aligned.shape
    rows, hidden = pieces[0].shape
    later = ([] if filled is None else [filled]) + list(later_than)
    return pl.pallas_call(
        functools.partial(weight_kernel, len(pieces), place, first, len(later), tile),
        grid=(count,),
        in_specs=[pl.BlockSpec((total, depth), lambda i: (0, 0))]
        + [pl.BlockSpec((rows, tile), lambda i: (0, i + first))] * len(pieces)
        + [pl.BlockSpec(memory_space=pl.ANY)] * len(later),
        out_specs=pl.BlockSpec(memory_space=pl.ANY),
        out_shape=jax.ShapeDtypeStruct((hidden, depth), jnp.bfloat16),
        scratch_shapes=[pltpu.VMEM((SLOTS, tile, depth), jnp.bfloat16), pltpu.SemaphoreType.DMA((SLOTS,))],
        input_output_aliases={} if filled is None else {1 + len(pieces): 0},
        compiler_params=params(), cost_estimate=cost(2 * total * count * tile * depth, 2 * count * tile * depth),
        name="weight_grads",
    )(aligned, *pieces, *later)


def fold_kernel(kept_ref, got_ref, *refs):
    n_passed = (len(refs) - 2) // 2
    next_ref, sent_ref = refs[n_passed:n_passed + 2]
    width = kept_ref.shape[1]
    half = next_ref.shape[0]
    sub = tile_of(width, SUB)
    lane = lax.broadcasted_iota(jnp.int32, (half, LANES), 1)
    levels = jnp.zeros(lane.shape, jnp.float32)
    got_levels = got_ref[:, width:]
    for at in range(width // sub):
        cols = slice(at * sub, (at + 1) * sub)
        total = kept_ref[:, cols] + decode(got_ref[:, cols], got_levels[:, at:at + 1])
        next_ref[:, cols] = total[:half]
        codes, level = encode(total[half:])
        sent_ref[:, cols] = codes
        levels = jnp.where(lane == at, level, levels)
    sent_ref[:, width:] = to_levels(levels)


def fold(kept, got, passed):
    vmem, anywhere = pl.BlockSpec(memory_space=pltpu.VMEM), pl.BlockSpec(memory_space=pl.ANY)
    rows, width = kept.shape
    kept, sent, *passed = pl.pallas_call(
        fold_kernel,
        in_specs=[vmem] * 2 + [anywhere] * len(passed),
        out_specs=[vmem] * 2 + [anywhere] * len(passed),
        out_shape=[jax.ShapeDtypeStruct((rows // 2, width), kept.dtype), jax.ShapeDtypeStruct((rows // 2, got.shape[1]), got.dtype)]
        + [jax.ShapeDtypeStruct(array.shape, array.dtype) for array in passed],
        input_output_aliases={2 + at: 2 + at for at in range(len(passed))},
        compiler_params=params(), cost_estimate=cost(kept.size * 20, kept.size * 12), name="fold",
    )(kept, got, *passed)
    return kept, sent, passed


def line_fold_kernel(kept_ref, got_ref, two_ref, three_ref):
    width = kept_ref.shape[1]
    rows = two_ref.shape[0]
    sub = tile_of(width, SUB)
    lane = lax.broadcasted_iota(jnp.int32, (2 * rows, LANES), 1)
    levels = jnp.zeros(lane.shape, jnp.float32)
    got_levels = got_ref[rows:, width:]
    for at in range(width // sub):
        cols = slice(at * sub, (at + 1) * sub)
        came = decode(got_ref[rows:, cols], got_levels[:, at:at + 1])
        came = jnp.concatenate([came[rows:], came[:rows]], axis=0)
        codes, level = encode(kept_ref[:, cols] + came)
        two_ref[:, cols] = codes[:rows]
        three_ref[:, cols] = codes[rows:]
        levels = jnp.where(lane == at, level, levels)
    two_ref[:, width:] = to_levels(levels[:rows])
    three_ref[:, width:] = to_levels(levels[rows:])


def line_fold(kept, got):
    rows = kept.shape[0] // 2
    like = jax.ShapeDtypeStruct((rows, got.shape[1]), got.dtype)
    return pl.pallas_call(
        line_fold_kernel, out_shape=[like, like], compiler_params=params(),
        cost_estimate=cost(kept.size * 20, kept.size * 12), name="line_fold",
    )(kept, got)


def total_kernel(counts, *refs):
    refs = list(refs)
    out_ref = refs.pop()
    base = 0
    for count in counts:
        kept_ref, got, refs = refs[0], refs[1:count], refs[count:]
        rows, width = kept_ref.shape
        sub = tile_of(width, SUB)
        for at in range(width // sub):
            cols = slice(at * sub, (at + 1) * sub)
            total = kept_ref[:, cols]
            for ref in got:
                total = total + decode(ref[:rows, cols], ref[:rows, width:][:, at:at + 1])
            out_ref[:, base + at * sub:base + (at + 1) * sub] = total.astype(jnp.bfloat16)
        base += width


def totals(parts, later_than):
    rows = parts[0][0].shape[0]
    hidden = sum(part[0].shape[1] for part in parts)
    flat = [array for part in parts for array in part]
    return pl.pallas_call(
        functools.partial(total_kernel, [len(part) for part in parts]),
        in_specs=[pl.BlockSpec(memory_space=pltpu.VMEM)] * len(flat) + [pl.BlockSpec(memory_space=pl.ANY)] * len(later_than),
        out_shape=jax.ShapeDtypeStruct((rows, hidden), jnp.bfloat16),
        compiler_params=params(), cost_estimate=cost(rows * hidden * 40, rows * hidden * 14), name="totals",
    )(*flat, *later_than)


def send(value, axis, flip, size):
    return lax.ppermute(value, axis, [(i, i ^ flip) for i in range(size)])


def stack_kernel(n_values, *refs):
    out_ref = refs[-1]
    rows = refs[0].shape[0]
    for at, ref in enumerate(refs[:n_values]):
        out_ref[at * rows:(at + 1) * rows] = ref[...]


def stacked(values, later_than=()):
    rows, width = values[0].shape
    return pl.pallas_call(
        functools.partial(stack_kernel, len(values)),
        in_specs=[pl.BlockSpec(memory_space=pltpu.VMEM)] * len(values) + [pl.BlockSpec(memory_space=pl.ANY)] * len(later_than),
        out_shape=jax.ShapeDtypeStruct((len(values) * rows, width), values[0].dtype),
        compiler_params=params(SMALL_LIMIT), cost_estimate=cost(0, 4 * len(values) * rows * width), name="stacked",
    )(*values, *later_than)


def add_kernel(left_ref, right_ref, *refs):
    refs[-1][...] = left_ref[...] + right_ref[...]


def added(left, right, later_than):
    return pl.pallas_call(
        add_kernel,
        in_specs=[pl.BlockSpec(memory_space=pltpu.VMEM)] * 2 + [pl.BlockSpec(memory_space=pl.ANY)] * len(later_than),
        out_shape=jax.ShapeDtypeStruct(left.shape, left.dtype),
        compiler_params=params(SMALL_LIMIT), cost_estimate=cost(left.size, left.size * 6), name="added",
    )(left, right, *later_than)


def same_kernel(*refs):
    pass


def handed_on(values, later_than):
    anywhere = pl.BlockSpec(memory_space=pl.ANY)
    return pl.pallas_call(
        same_kernel,
        in_specs=[anywhere] * (len(values) + len(later_than)), out_specs=[anywhere] * len(values),
        out_shape=[jax.ShapeDtypeStruct(value.shape, value.dtype) for value in values],
        input_output_aliases={at: at for at in range(len(values))},
        compiler_params=params(SMALL_LIMIT), cost_estimate=cost(0, 0), name="handed_on",
    )(*values, *later_than)


def gather_cotangent(cotangent, n_col, before_first, before_second):
    pieces = [cotangent] + [send(cotangent, "col", flip, n_col) for flip in range(2, n_col, 2)]
    stacks = [stacked(pieces[:2], before_first)]
    stacks.append(stacked(pieces[2:], stacks + before_second))
    return stacks + [send(stack, "col", 1, n_col) for stack in stacks]


def halving_order(size):
    order = [0]
    while len(order) < size:
        order = [2 * o for o in order] + [2 * o + 1 for o in order]
    return order


def part_slices(tiles, shares):
    ends = [tiles * sum(shares[:at]) // 7 for at in range(len(shares) + 1)]
    return [(first, last - first) for first, last in zip(ends, ends[1:])]


def halving_sums(align, weight, act_pieces, n_row, offsets, tile):
    total = align[0].shape[0]
    kept_rows, sent_rows = [slice(0, total // 2)], [slice(total // 2, total)]
    count = weight.shape[0] // tile
    aligned, [kept], [sent] = partial_sums(None, align, weight, False, tile, 0, count, kept_rows, sent_rows, [], "sums")
    got = send(sent, "row", 1, n_row)
    evens = range(2, n_row, 2)
    for o, piece in zip(evens, handed_on([act_pieces[o] for o in evens], [aligned])):
        act_pieces[o], act_pieces[o + 1] = piece, send(piece, "row", 1, n_row)
    step = 2
    while step < n_row:
        kept, sent, _ = fold(kept, got, [])
        got = send(sent, "row", step, n_row)
        step *= 2
    weight_grad = weight_grads(aligned, [act_pieces[o] for o in offsets], lambda values: values, tile, 0, count, None, [sent])
    return weight_grad, totals([[kept, got]], [weight_grad])


def line_sums(align, weight, weight_a, act_pieces, tile):
    total = align[0].shape[0]
    rows = total // 4
    kept_rows = [slice(0, rows), slice(2 * rows, total)]
    sent_rows = [slice(rows, total), slice(rows, 2 * rows)]
    (first_a, count_a), (first_b, count_b) = part_slices(weight.shape[0] // tile, (4, 3))
    inwards, outwards, middle = [(0, 1), (3, 2)], [(1, 0), (2, 3)], [(1, 2), (2, 1)]

    def spread(sent):
        return lax.ppermute(sent[0], "row", inwards), lax.ppermute(sent[1], "row", outwards)

    def cross(kept, got):
        two, three = line_fold(kept, got)
        return two, lax.ppermute(three, "row", middle), lax.ppermute(two, "row", [(1, 3), (2, 0)])

    own, left, right = act_pieces
    two_left = lax.ppermute(left, "row", [(1, 2), (2, 3)])
    two_right = lax.ppermute(right, "row", [(2, 1), (1, 0)])
    aligned, kept_a, sent_a = partial_sums(None, align, weight_a, True, tile, first_a, count_a, kept_rows, sent_rows, [], "sums_a")
    got_a = spread(sent_a)
    _, kept_b, sent_b = partial_sums(
        aligned, None, weight, False, tile, first_b, count_b, kept_rows, sent_rows, [], "sums_b")
    two = added(two_left, two_right, kept_b[:1])
    far = lax.ppermute(two, "row", outwards)
    sent_b = handed_on(sent_b, [got_a[1]])
    got_b = spread(sent_b)
    two_a, *crossed_a = cross(kept_a[1], got_a[0])
    pieces = [own, left, right, two, far]
    grad = weight_grads(aligned, pieces, line_places, tile, first_a, count_a, None, [two_a])
    two_b, *crossed_b = cross(kept_b[1], got_b[0])
    weight_grad = weight_grads(aligned, pieces, line_places, tile, first_b, count_b, grad, [two_b])
    return weight_grad, totals([[kept_a[0], *got_a, *crossed_a], [kept_b[0], *got_b, *crossed_b]], [weight_grad])


def body(n_row, n_col, activations, cotangent, down_weight, row_order):
    rows, hidden = activations.shape
    shard = cotangent.shape[0]
    mine_row, mine_col = lax.axis_index("row"), lax.axis_index("col")
    offsets = list(range(4)) if n_row == 4 else halving_order(n_row)

    flips = list(range(0, n_col, 2))
    flips += [flip ^ 1 for flip in flips]
    order = row_order.reshape(n_row, rows)
    order = jnp.concatenate([lax.dynamic_index_in_dim(order, mine_row ^ o, 0, keepdims=False) for o in offsets])
    owner = mine_col ^ jnp.asarray(flips, jnp.int32)
    named = (owner[:, None] * shard + jnp.arange(shard, dtype=jnp.int32)[None, :]).reshape(-1)
    pick = (order[:, None] == named[None, :]).astype(jnp.bfloat16)

    tile = tile_of(hidden, 256)
    if n_row == 4:
        weight_a = fetched(down_weight, tile, part_slices(hidden // tile, (4, 3))[0][1], [pick])
        left = lax.ppermute(activations, "row", [(0, 1), (1, 2), (2, 3)])
        right = lax.ppermute(activations, "row", [(3, 2), (2, 1), (1, 0)])
        pieces = gather_cotangent(cotangent, n_col, [weight_a], [left, right])
        return line_sums((pick, pieces), down_weight, weight_a, [activations, left, right], tile)
    pieces = gather_cotangent(cotangent, n_col, [], [])
    act_pieces = {o: send(activations, "row", o, n_row) for o in [1, *range(2, n_row, 2)]}
    act_pieces[0] = activations
    return halving_sums((pick, pieces), down_weight, act_pieces, n_row, offsets, tile)


def solution(mesh):
    in_specs = (P("row", "col"), P("col", "row"), P("col", "row"), P())
    out_specs = (P("col", "row"), P("row", "col"))
    fn = functools.partial(body, mesh.shape["row"], mesh.shape["col"])
    return jax.shard_map(fn, mesh=mesh, in_specs=in_specs, out_specs=out_specs, check_vma=False)
```

```python
import functools

import jax
import jax.numpy as jnp
from jax import lax
from jax.experimental import pallas as pl
from jax.experimental.pallas import tpu as pltpu
from jax.sharding import PartitionSpec as P

LANES = 128
STEPS_PER_OCTAVE = 128.0
TOP = 32766.0
LEAST = 2.0 ** -120
VMEM_LIMIT = 48 * 1024 * 1024
SMALL_LIMIT = 8 * 1024 * 1024
SLOTS = 4
SHARES = (2, 3, 2)
SUB = 256


def tile_of(size, largest):
    tile = largest
    while size % tile:
        tile //= 2
    return tile


def dot(left, right, dims):
    return lax.dot_general(left, right, (dims, ((), ())), preferred_element_type=jnp.float32)


def encode(values):
    most = jnp.maximum(jnp.max(jnp.abs(values), axis=1, keepdims=True), LEAST)
    level = jnp.ceil(jnp.log2(most) * STEPS_PER_OCTAVE) + 1.0
    codes = jnp.round(values * jnp.exp2(level * (-1.0 / STEPS_PER_OCTAVE)) * TOP)
    return codes.astype(jnp.int32).astype(jnp.int16), level


def decode(codes, levels):
    scale = jnp.exp2(levels.astype(jnp.int32).astype(jnp.float32) * (1.0 / STEPS_PER_OCTAVE)) * (1.0 / TOP)
    return codes.astype(jnp.int32).astype(jnp.float32) * scale


def to_levels(levels):
    return levels.astype(jnp.int32).astype(jnp.int16)


def params(limit=VMEM_LIMIT):
    return pltpu.CompilerParams(vmem_limit_bytes=limit)


def cost(flops, moved):
    return pl.CostEstimate(flops=flops, bytes_accessed=moved, transcendentals=0)


def align_rows(pick_ref, pieces, aligned_ref):
    depth = aligned_ref.shape[1]
    chunk = tile_of(depth, 512)
    for at in range(0, depth, chunk):
        cols = slice(at, at + chunk)
        gathered = jnp.concatenate([piece[:, cols] for piece in pieces], axis=0)
        aligned_ref[:, cols] = dot(pick_ref[...], gathered, ((1,), (0,))).astype(jnp.bfloat16)


def sums_kernel(n_pieces, n_blocks, n_later, coded, kept_rows, sent_rows, tile, *refs):
    refs = list(refs)
    if n_pieces:
        pick_ref = refs.pop(0)
        pieces = [refs.pop(0) for _ in range(n_pieces)]
    else:
        aligned_ref = refs.pop(0)
    weights = [refs.pop(0) for _ in range(n_blocks)]
    del refs[:n_later]
    if n_pieces:
        aligned_ref = refs.pop(0)
    kept = [refs.pop(0) for _ in kept_rows]
    sent = [refs.pop(0) for _ in sent_rows]
    levels_ref, = refs
    step = pl.program_id(0)
    width = sent[0].shape[1] - LANES

    @pl.when(step == 0)
    def _():
        if n_pieces:
            align_rows(pick_ref, pieces, aligned_ref)
        levels_ref[...] = jnp.zeros_like(levels_ref)

    lane = lax.broadcasted_iota(jnp.int32, levels_ref.shape, 1)
    levels = levels_ref[...]
    for part in range(n_blocks):
        at = step * n_blocks + part
        cols = pl.ds(pl.multiple_of(at * tile, tile), tile)
        values = dot(aligned_ref[...], weights[part][...], ((1,), (1,)))
        for ref, rows in zip(kept, kept_rows):
            ref[:, part * tile:(part + 1) * tile] = values[rows]
        codes, level = encode(values[coded:])
        levels = jnp.where(lane == at, level, levels)
        for ref, rows in zip(sent, sent_rows):
            ref[:, cols] = codes[rows.start - coded:rows.stop - coded]
    levels_ref[...] = levels

    @pl.when(step == pl.num_programs(0) - 1)
    def _():
        for ref, rows in zip(sent, sent_rows):
            ref[:, width:] = to_levels(levels[rows.start - coded:rows.stop - coded])


def partial_sums(aligned, align, weight, tile, first, count, kept_rows, sent_rows, later_than, name):
    depth = weight.shape[1]
    width = count * tile
    whole = lambda i: (0, 0)
    operands = [align[0], *align[1]] if aligned is None else [aligned]
    total = operands[0].shape[0]
    coded = min(rows.start for rows in sent_rows)
    n_blocks = 2 if count % 2 == 0 and first % 2 == 0 else 1
    block_at = lambda part: (lambda i: (i * n_blocks + first + part, 0))
    heights = lambda spans: [span.stop - span.start for span in spans]
    in_specs = [pl.BlockSpec(operand.shape, whole) for operand in operands]
    in_specs += [pl.BlockSpec((tile, depth), block_at(part)) for part in range(n_blocks)]
    in_specs += [pl.BlockSpec(memory_space=pl.ANY)] * len(later_than)
    out_specs = [pl.BlockSpec((height, n_blocks * tile), lambda i: (0, i)) for height in heights(kept_rows)]
    out_specs += [pl.BlockSpec((height, width + LANES), whole) for height in heights(sent_rows)]
    out_shape = [jax.ShapeDtypeStruct((height, width), jnp.float32) for height in heights(kept_rows)]
    out_shape += [jax.ShapeDtypeStruct((height, width + LANES), jnp.int16) for height in heights(sent_rows)]
    if aligned is None:
        out_specs.insert(0, pl.BlockSpec((total, depth), whole))
        out_shape.insert(0, jax.ShapeDtypeStruct((total, depth), jnp.bfloat16))
    outs = pl.pallas_call(
        functools.partial(
            sums_kernel, 0 if aligned is not None else len(align[1]), n_blocks, len(later_than), coded, kept_rows, sent_rows, tile),
        grid=(count // n_blocks,), in_specs=in_specs, out_specs=out_specs, out_shape=out_shape,
        scratch_shapes=[pltpu.VMEM((total - coded, LANES), jnp.float32)],
        compiler_params=params(),
        cost_estimate=cost(2 * total * width * depth, 2 * width * depth), name=name,
    )(*operands, *[weight] * n_blocks, *later_than)
    if aligned is None:
        aligned, *outs = outs
    return aligned, outs[:len(kept_rows)], outs[len(kept_rows):]


def weight_kernel(n_pieces, first, n_later, tile, aligned_ref, *refs):
    pieces = [ref[...] for ref in refs[:n_pieces]]
    out_ref, held_ref, left_sem = refs[n_pieces + n_later:]
    step = pl.program_id(0)
    last = pl.num_programs(0) - 1
    slots = held_ref.shape[0]

    def leave(at):
        rows = pl.ds(pl.multiple_of((first + at) * tile, tile), tile)
        slot = lax.rem(at, slots)
        return pltpu.make_async_copy(held_ref.at[slot], out_ref.at[rows], left_sem.at[slot])

    @pl.when(step >= slots)
    def _():
        leave(step - slots).wait()

    left = jnp.concatenate(pieces, axis=0)
    depth = aligned_ref.shape[1]
    chunk = tile_of(depth, 1024)
    block = held_ref.at[lax.rem(step, slots)]
    for at in range(0, depth, chunk):
        cols = slice(at, at + chunk)
        block[:, cols] = dot(left, aligned_ref[:, cols], ((0,), (0,))).astype(jnp.bfloat16)
    leave(step).start()

    @pl.when(step == last)
    def _():
        for back in range(slots - 1, -1, -1):
            @pl.when(last >= back)
            def _():
                leave(last - back).wait()


def weight_grads(aligned, pieces, tile, first, count, filled, later_than):
    total, depth = aligned.shape
    rows, hidden = pieces[0].shape
    later = ([] if filled is None else [filled]) + list(later_than)
    return pl.pallas_call(
        functools.partial(weight_kernel, len(pieces), first, len(later), tile),
        grid=(count,),
        in_specs=[pl.BlockSpec((total, depth), lambda i: (0, 0))]
        + [pl.BlockSpec((rows, tile), lambda i: (0, i + first))] * len(pieces)
        + [pl.BlockSpec(memory_space=pl.ANY)] * len(later),
        out_specs=pl.BlockSpec(memory_space=pl.ANY),
        out_shape=jax.ShapeDtypeStruct((hidden, depth), jnp.bfloat16),
        scratch_shapes=[pltpu.VMEM((SLOTS, tile, depth), jnp.bfloat16), pltpu.SemaphoreType.DMA((SLOTS,))],
        input_output_aliases={} if filled is None else {1 + len(pieces): 0},
        compiler_params=params(), cost_estimate=cost(2 * total * count * tile * depth, 2 * count * tile * depth),
        name="weight_grads",
    )(aligned, *pieces, *later)


def fold_kernel(kept_ref, got_ref, *refs):
    n_passed = (len(refs) - 2) // 2
    next_ref, sent_ref = refs[n_passed:n_passed + 2]
    width = kept_ref.shape[1]
    half = next_ref.shape[0]
    sub = tile_of(width, SUB)
    lane = lax.broadcasted_iota(jnp.int32, (half, LANES), 1)
    levels = jnp.zeros(lane.shape, jnp.float32)
    got_levels = got_ref[:, width:]
    for at in range(width // sub):
        cols = slice(at * sub, (at + 1) * sub)
        total = kept_ref[:, cols] + decode(got_ref[:, cols], got_levels[:, at:at + 1])
        next_ref[:, cols] = total[:half]
        codes, level = encode(total[half:])
        sent_ref[:, cols] = codes
        levels = jnp.where(lane == at, level, levels)
    sent_ref[:, width:] = to_levels(levels)


def fold(kept, got, passed):
    vmem, anywhere = pl.BlockSpec(memory_space=pltpu.VMEM), pl.BlockSpec(memory_space=pl.ANY)
    rows, width = kept.shape
    kept, sent, *passed = pl.pallas_call(
        fold_kernel,
        in_specs=[vmem] * 2 + [anywhere] * len(passed),
        out_specs=[vmem] * 2 + [anywhere] * len(passed),
        out_shape=[jax.ShapeDtypeStruct((rows // 2, width), kept.dtype), jax.ShapeDtypeStruct((rows // 2, got.shape[1]), got.dtype)]
        + [jax.ShapeDtypeStruct(array.shape, array.dtype) for array in passed],
        input_output_aliases={2 + at: 2 + at for at in range(len(passed))},
        compiler_params=params(), cost_estimate=cost(kept.size * 20, kept.size * 12), name="fold",
    )(kept, got, *passed)
    return kept, sent, passed


def total_kernel(counts, *refs):
    refs = list(refs)
    out_ref = refs.pop()
    base = 0
    for count in counts:
        kept_ref, got, refs = refs[0], refs[1:count], refs[count:]
        rows, width = kept_ref.shape
        sub = tile_of(width, SUB)
        for at in range(width // sub):
            cols = slice(at * sub, (at + 1) * sub)
            total = kept_ref[:, cols]
            for ref in got:
                total = total + decode(ref[:rows, cols], ref[:rows, width:][:, at:at + 1])
            out_ref[:, base + at * sub:base + (at + 1) * sub] = total.astype(jnp.bfloat16)
        base += width


def totals(parts, later_than):
    rows = parts[0][0].shape[0]
    hidden = sum(part[0].shape[1] for part in parts)
    flat = [array for part in parts for array in part]
    return pl.pallas_call(
        functools.partial(total_kernel, [len(part) for part in parts]),
        in_specs=[pl.BlockSpec(memory_space=pltpu.VMEM)] * len(flat) + [pl.BlockSpec(memory_space=pl.ANY)] * len(later_than),
        out_shape=jax.ShapeDtypeStruct((rows, hidden), jnp.bfloat16),
        compiler_params=params(), cost_estimate=cost(rows * hidden * 40, rows * hidden * 14), name="totals",
    )(*flat, *later_than)


def send(value, axis, flip, size):
    return lax.ppermute(value, axis, [(i, i ^ flip) for i in range(size)])


def stack_kernel(n_values, *refs):
    out_ref = refs[-1]
    rows = refs[0].shape[0]
    for at, ref in enumerate(refs[:n_values]):
        out_ref[at * rows:(at + 1) * rows] = ref[...]


def stacked(values, later_than=()):
    rows, width = values[0].shape
    return pl.pallas_call(
        functools.partial(stack_kernel, len(values)),
        in_specs=[pl.BlockSpec(memory_space=pltpu.VMEM)] * len(values) + [pl.BlockSpec(memory_space=pl.ANY)] * len(later_than),
        out_shape=jax.ShapeDtypeStruct((len(values) * rows, width), values[0].dtype),
        compiler_params=params(SMALL_LIMIT), cost_estimate=cost(0, 4 * len(values) * rows * width), name="stacked",
    )(*values, *later_than)


def same_kernel(*refs):
    pass


def handed_on(values, later_than):
    anywhere = pl.BlockSpec(memory_space=pl.ANY)
    return pl.pallas_call(
        same_kernel,
        in_specs=[anywhere] * (len(values) + len(later_than)), out_specs=[anywhere] * len(values),
        out_shape=[jax.ShapeDtypeStruct(value.shape, value.dtype) for value in values],
        input_output_aliases={at: at for at in range(len(values))},
        compiler_params=params(SMALL_LIMIT), cost_estimate=cost(0, 0), name="handed_on",
    )(*values, *later_than)


def gather_cotangent(cotangent, n_col):
    pieces = [cotangent] + [send(cotangent, "col", flip, n_col) for flip in range(2, n_col, 2)]
    stacks = [stacked(pieces[:2])]
    stacks.append(stacked(pieces[2:], stacks))
    return stacks + [send(stack, "col", 1, n_col) for stack in stacks]


def halving_order(size):
    order = [0]
    while len(order) < size:
        order = [2 * o for o in order] + [2 * o + 1 for o in order]
    return order


def part_slices(tiles, shares):
    ends = [tiles * sum(shares[:at]) // 7 for at in range(len(shares) + 1)]
    return [(first, last - first) for first, last in zip(ends, ends[1:])]


def halved(kept, got, passed, n_row):
    step, sent = 2, None
    while step < n_row:
        kept, sent, passed = fold(kept, got, passed)
        got = send(sent, "row", step, n_row)
        step *= 2
    return [kept, got], [sent] if sent is not None else [], passed


def body(n_row, n_col, activations, cotangent, down_weight, row_order):
    rows, hidden = activations.shape
    shard = cotangent.shape[0]
    mine_row, mine_col = lax.axis_index("row"), lax.axis_index("col")
    offsets = halving_order(n_row)
    total = n_row * rows

    flips = list(range(0, n_col, 2))
    flips += [flip ^ 1 for flip in flips]
    order = row_order.reshape(n_row, rows)
    order = jnp.concatenate([lax.dynamic_index_in_dim(order, mine_row ^ o, 0, keepdims=False) for o in offsets])
    owner = mine_col ^ jnp.asarray(flips, jnp.int32)
    named = (owner[:, None] * shard + jnp.arange(shard, dtype=jnp.int32)[None, :]).reshape(-1)
    pick = (order[:, None] == named[None, :]).astype(jnp.bfloat16)

    tile = tile_of(hidden, 256)
    parts = part_slices(hidden // tile, SHARES)
    pieces = gather_cotangent(cotangent, n_col)
    act_pieces = {o: send(activations, "row", o, n_row) for o in [1, *range(2, n_row, 2)]}
    act_pieces[0] = activations

    kept_rows, sent_rows = [slice(0, total // 2)], [slice(total // 2, total)]
    aligned, [kept], [sent] = partial_sums(
        None, (pick, pieces), down_weight, tile, *parts[0], kept_rows, sent_rows, [], "sums_first")
    got = send(sent, "row", 1, n_row)
    evens = range(2, n_row, 2)
    for o, piece in zip(evens, handed_on([act_pieces[o] for o in evens], [aligned])):
        act_pieces[o], act_pieces[o + 1] = piece, send(piece, "row", 1, n_row)

    done, crossed = [], []
    for at, part in enumerate(parts[1:]):
        _, [next_kept], [sent] = partial_sums(
            aligned, None, down_weight, tile, *part, kept_rows, sent_rows, [act_pieces[1]] if at == 0 else [], "sums_next")
        ended, crossed, [sent] = halved(kept, got, [sent], n_row)
        done.append(ended)
        kept, got = next_kept, send(sent, "row", 1, n_row)

    grad_pieces = [act_pieces[o] for o in offsets]
    (first_a, count_a), (first_b, count_b) = part_slices(hidden // tile, (4, 3))
    grad = weight_grads(aligned, grad_pieces, tile, first_a, count_a, None, crossed)
    ended, crossed, _ = halved(kept, got, [], n_row)
    done.append(ended)
    weight_grad = weight_grads(aligned, grad_pieces, tile, first_b, count_b, grad, crossed)
    return weight_grad, totals(done, [weight_grad])


def solution(mesh):
    in_specs = (P("row", "col"), P("col", "row"), P("col", "row"), P())
    out_specs = (P("col", "row"), P("row", "col"))
    fn = functools.partial(body, mesh.shape["row"], mesh.shape["col"])
    return jax.shard_map(fn, mesh=mesh, in_specs=in_specs, out_specs=out_specs, check_vma=False)
```

```python
import functools

import jax
import jax.numpy as jnp
from jax import lax
from jax.experimental import pallas as pl
from jax.experimental.pallas import tpu as pltpu
from jax.sharding import PartitionSpec as P

LANES = 128
STEPS_PER_OCTAVE = 128.0
TOP = 32766.0
LEAST = 2.0 ** -120
VMEM_LIMIT = 48 * 1024 * 1024
SMALL_LIMIT = 8 * 1024 * 1024
SLOTS = 4
SHARES = (2, 3, 2)
GRAD_SHARES = (4, 3)
SUB = 512


def tile_of(size, largest):
    tile = largest
    while size % tile:
        tile //= 2
    return tile


def dot(left, right, dims):
    return lax.dot_general(left, right, (dims, ((), ())), preferred_element_type=jnp.float32)


def encode(values):
    most = jnp.maximum(jnp.max(jnp.abs(values), axis=1, keepdims=True), LEAST)
    level = jnp.ceil(jnp.log2(most) * STEPS_PER_OCTAVE) + 1.0
    codes = jnp.round(values * jnp.exp2(level * (-1.0 / STEPS_PER_OCTAVE)) * TOP)
    return codes.astype(jnp.int32).astype(jnp.int16), level


def decode(codes, levels):
    scale = jnp.exp2(levels.astype(jnp.int32).astype(jnp.float32) * (1.0 / STEPS_PER_OCTAVE)) * (1.0 / TOP)
    return codes.astype(jnp.int32).astype(jnp.float32) * scale


def to_levels(levels):
    return levels.astype(jnp.int32).astype(jnp.int16)


def params(limit=VMEM_LIMIT):
    return pltpu.CompilerParams(vmem_limit_bytes=limit)


def cost(flops, moved):
    return pl.CostEstimate(flops=flops, bytes_accessed=moved, transcendentals=0)


def align_rows(pick_ref, pieces, aligned_ref):
    depth = aligned_ref.shape[1]
    chunk = tile_of(depth, 512)
    for at in range(0, depth, chunk):
        cols = slice(at, at + chunk)
        gathered = jnp.concatenate([piece[:, cols] for piece in pieces], axis=0)
        aligned_ref[:, cols] = dot(pick_ref[...], gathered, ((1,), (0,))).astype(jnp.bfloat16)


def sums_kernel(n_pieces, n_blocks, n_later, coded, kept_rows, sent_rows, tile, *refs):
    refs = list(refs)
    if n_pieces:
        pick_ref = refs.pop(0)
        pieces = [refs.pop(0) for _ in range(n_pieces)]
    else:
        aligned_ref = refs.pop(0)
    weights = [refs.pop(0) for _ in range(n_blocks)]
    del refs[:n_later]
    if n_pieces:
        aligned_ref = refs.pop(0)
    kept = [refs.pop(0) for _ in kept_rows]
    sent = [refs.pop(0) for _ in sent_rows]
    levels_ref, = refs
    step = pl.program_id(0)
    width = sent[0].shape[1] - LANES

    @pl.when(step == 0)
    def _():
        if n_pieces:
            align_rows(pick_ref, pieces, aligned_ref)
        levels_ref[...] = jnp.zeros_like(levels_ref)

    lane = lax.broadcasted_iota(jnp.int32, levels_ref.shape, 1)
    levels = levels_ref[...]
    for part in range(n_blocks):
        at = step * n_blocks + part
        cols = pl.ds(pl.multiple_of(at * tile, tile), tile)
        values = dot(aligned_ref[...], weights[part][...], ((1,), (1,)))
        for ref, rows in zip(kept, kept_rows):
            ref[:, part * tile:(part + 1) * tile] = values[rows]
        codes, level = encode(values[coded:])
        levels = jnp.where(lane == at, level, levels)
        for ref, rows in zip(sent, sent_rows):
            ref[:, cols] = codes[rows.start - coded:rows.stop - coded]
    levels_ref[...] = levels

    @pl.when(step == pl.num_programs(0) - 1)
    def _():
        for ref, rows in zip(sent, sent_rows):
            ref[:, width:] = to_levels(levels[rows.start - coded:rows.stop - coded])


def partial_sums(aligned, align, weight, tile, first, count, kept_rows, sent_rows, later_than, name):
    depth = weight.shape[1]
    width = count * tile
    whole = lambda i: (0, 0)
    operands = [align[0], *align[1]] if aligned is None else [aligned]
    total = operands[0].shape[0]
    coded = min(rows.start for rows in sent_rows)
    n_blocks = 2 if count % 2 == 0 and first % 2 == 0 else 1
    block_at = lambda part: (lambda i: (i * n_blocks + first + part, 0))
    heights = lambda spans: [span.stop - span.start for span in spans]
    in_specs = [pl.BlockSpec(operand.shape, whole) for operand in operands]
    in_specs += [pl.BlockSpec((tile, depth), block_at(part)) for part in range(n_blocks)]
    in_specs += [pl.BlockSpec(memory_space=pl.ANY)] * len(later_than)
    out_specs = [pl.BlockSpec((height, n_blocks * tile), lambda i: (0, i)) for height in heights(kept_rows)]
    out_specs += [pl.BlockSpec((height, width + LANES), whole) for height in heights(sent_rows)]
    out_shape = [jax.ShapeDtypeStruct((height, width), jnp.float32) for height in heights(kept_rows)]
    out_shape += [jax.ShapeDtypeStruct((height, width + LANES), jnp.int16) for height in heights(sent_rows)]
    if aligned is None:
        out_specs.insert(0, pl.BlockSpec((total, depth), whole))
        out_shape.insert(0, jax.ShapeDtypeStruct((total, depth), jnp.bfloat16))
    outs = pl.pallas_call(
        functools.partial(
            sums_kernel, 0 if aligned is not None else len(align[1]), n_blocks, len(later_than), coded, kept_rows, sent_rows, tile),
        grid=(count // n_blocks,), in_specs=in_specs, out_specs=out_specs, out_shape=out_shape,
        scratch_shapes=[pltpu.VMEM((total - coded, LANES), jnp.float32)],
        compiler_params=params(),
        cost_estimate=cost(2 * total * width * depth, 2 * width * depth), name=name,
    )(*operands, *[weight] * n_blocks, *later_than)
    if aligned is None:
        aligned, *outs = outs
    return aligned, outs[:len(kept_rows)], outs[len(kept_rows):]


def weight_kernel(n_pieces, first, n_later, tile, aligned_ref, *refs):
    pieces = [ref[...] for ref in refs[:n_pieces]]
    out_ref, held_ref, left_sem = refs[n_pieces + n_later:]
    step = pl.program_id(0)
    last = pl.num_programs(0) - 1
    slots = held_ref.shape[0]

    def leave(at):
        rows = pl.ds(pl.multiple_of((first + at) * tile, tile), tile)
        slot = lax.rem(at, slots)
        return pltpu.make_async_copy(held_ref.at[slot], out_ref.at[rows], left_sem.at[slot])

    @pl.when(step >= slots)
    def _():
        leave(step - slots).wait()

    left = jnp.concatenate(pieces, axis=0)
    depth = aligned_ref.shape[1]
    chunk = tile_of(depth, 1024)
    block = held_ref.at[lax.rem(step, slots)]
    for at in range(0, depth, chunk):
        cols = slice(at, at + chunk)
        block[:, cols] = dot(left, aligned_ref[:, cols], ((0,), (0,))).astype(jnp.bfloat16)
    leave(step).start()

    @pl.when(step == last)
    def _():
        for back in range(slots - 1, -1, -1):
            @pl.when(last >= back)
            def _():
                leave(last - back).wait()


def weight_grads(aligned, pieces, tile, first, count, filled, later_than):
    total, depth = aligned.shape
    rows, hidden = pieces[0].shape
    later = ([] if filled is None else [filled]) + list(later_than)
    return pl.pallas_call(
        functools.partial(weight_kernel, len(pieces), first, len(later), tile),
        grid=(count,),
        in_specs=[pl.BlockSpec((total, depth), lambda i: (0, 0))]
        + [pl.BlockSpec((rows, tile), lambda i: (0, i + first))] * len(pieces)
        + [pl.BlockSpec(memory_space=pl.ANY)] * len(later),
        out_specs=pl.BlockSpec(memory_space=pl.ANY),
        out_shape=jax.ShapeDtypeStruct((hidden, depth), jnp.bfloat16),
        scratch_shapes=[pltpu.VMEM((SLOTS, tile, depth), jnp.bfloat16), pltpu.SemaphoreType.DMA((SLOTS,))],
        input_output_aliases={} if filled is None else {1 + len(pieces): 0},
        compiler_params=params(), cost_estimate=cost(2 * total * count * tile * depth, 2 * count * tile * depth),
        name="weight_grads",
    )(aligned, *pieces, *later)


def fold_kernel(n_others, kept_ref, got_ref, *refs):
    next_ref, sent_ref = refs[n_others:n_others + 2]
    width = kept_ref.shape[1]
    half = next_ref.shape[0]
    sub = tile_of(width, SUB)
    lane = lax.broadcasted_iota(jnp.int32, (half, LANES), 1)
    levels = jnp.zeros(lane.shape, jnp.float32)
    got_levels = got_ref[:, width:]
    for at in range(width // sub):
        cols = slice(at * sub, (at + 1) * sub)
        total = kept_ref[:, cols] + decode(got_ref[:, cols], got_levels[:, at:at + 1])
        next_ref[:, cols] = total[:half]
        codes, level = encode(total[half:])
        sent_ref[:, cols] = codes
        levels = jnp.where(lane == at, level, levels)
    sent_ref[:, width:] = to_levels(levels)


def fold(kept, got, passed, later_than):
    others = [*passed, *later_than]
    vmem, anywhere = pl.BlockSpec(memory_space=pltpu.VMEM), pl.BlockSpec(memory_space=pl.ANY)
    rows, width = kept.shape
    kept, sent, *passed = pl.pallas_call(
        functools.partial(fold_kernel, len(others)),
        in_specs=[vmem] * 2 + [anywhere] * len(others),
        out_specs=[vmem] * 2 + [anywhere] * len(passed),
        out_shape=[jax.ShapeDtypeStruct((rows // 2, width), kept.dtype), jax.ShapeDtypeStruct((rows // 2, got.shape[1]), got.dtype)]
        + [jax.ShapeDtypeStruct(array.shape, array.dtype) for array in passed],
        input_output_aliases={2 + at: 2 + at for at in range(len(passed))},
        compiler_params=params(), cost_estimate=cost(kept.size * 20, kept.size * 12), name="fold",
    )(kept, got, *others)
    return kept, sent, passed


def total_kernel(counts, *refs):
    refs = list(refs)
    out_ref = refs.pop()
    base = 0
    for count in counts:
        kept_ref, got, refs = refs[0], refs[1:count], refs[count:]
        rows, width = kept_ref.shape
        sub = tile_of(width, SUB)
        for at in range(width // sub):
            cols = slice(at * sub, (at + 1) * sub)
            total = kept_ref[:, cols]
            for ref in got:
                total = total + decode(ref[:rows, cols], ref[:rows, width:][:, at:at + 1])
            out_ref[:, base + at * sub:base + (at + 1) * sub] = total.astype(jnp.bfloat16)
        base += width


def totals(parts, later_than):
    rows = parts[0][0].shape[0]
    hidden = sum(part[0].shape[1] for part in parts)
    flat = [array for part in parts for array in part]
    return pl.pallas_call(
        functools.partial(total_kernel, [len(part) for part in parts]),
        in_specs=[pl.BlockSpec(memory_space=pltpu.VMEM)] * len(flat) + [pl.BlockSpec(memory_space=pl.ANY)] * len(later_than),
        out_shape=jax.ShapeDtypeStruct((rows, hidden), jnp.bfloat16),
        compiler_params=params(), cost_estimate=cost(rows * hidden * 40, rows * hidden * 14), name="totals",
    )(*flat, *later_than)


def send(value, axis, flip, size):
    return lax.ppermute(value, axis, [(i, i ^ flip) for i in range(size)])


def stack_kernel(n_values, *refs):
    out_ref = refs[-1]
    rows = refs[0].shape[0]
    for at, ref in enumerate(refs[:n_values]):
        out_ref[at * rows:(at + 1) * rows] = ref[...]


def stacked(values, later_than=()):
    rows, width = values[0].shape
    return pl.pallas_call(
        functools.partial(stack_kernel, len(values)),
        in_specs=[pl.BlockSpec(memory_space=pltpu.VMEM)] * len(values) + [pl.BlockSpec(memory_space=pl.ANY)] * len(later_than),
        out_shape=jax.ShapeDtypeStruct((len(values) * rows, width), values[0].dtype),
        compiler_params=params(SMALL_LIMIT), cost_estimate=cost(0, 4 * len(values) * rows * width), name="stacked",
    )(*values, *later_than)


def same_kernel(*refs):
    pass


def handed_on(values, later_than):
    anywhere = pl.BlockSpec(memory_space=pl.ANY)
    return pl.pallas_call(
        same_kernel,
        in_specs=[anywhere] * (len(values) + len(later_than)), out_specs=[anywhere] * len(values),
        out_shape=[jax.ShapeDtypeStruct(value.shape, value.dtype) for value in values],
        input_output_aliases={at: at for at in range(len(values))},
        compiler_params=params(SMALL_LIMIT), cost_estimate=cost(0, 0), name="handed_on",
    )(*values, *later_than)


def gather_cotangent(cotangent, n_col):
    pieces = [cotangent] + [send(cotangent, "col", flip, n_col) for flip in range(2, n_col, 2)]
    stacks = [stacked(pieces[:2])]
    stacks.append(stacked(pieces[2:], stacks))
    return stacks + [send(stack, "col", 1, n_col) for stack in stacks]


def halving_order(size):
    order = [0]
    while len(order) < size:
        order = [2 * o for o in order] + [2 * o + 1 for o in order]
    return order


def part_slices(tiles, shares):
    ends = [tiles * sum(shares[:at]) // 7 for at in range(len(shares) + 1)]
    return [(first, last - first) for first, last in zip(ends, ends[1:])]


def halved(kept, got, passed, later_than, n_row):
    step, sent = 2, None
    while step < n_row:
        kept, sent, passed = fold(kept, got, passed, later_than)
        got = send(sent, "row", step, n_row)
        step *= 2
    return [kept, got], [sent] if sent is not None else [], passed


def body(n_row, n_col, activations, cotangent, down_weight, row_order):
    rows, hidden = activations.shape
    shard = cotangent.shape[0]
    mine_row, mine_col = lax.axis_index("row"), lax.axis_index("col")
    offsets = halving_order(n_row)
    total = n_row * rows

    flips = list(range(0, n_col, 2))
    flips += [flip ^ 1 for flip in flips]
    order = row_order.reshape(n_row, rows)
    order = jnp.concatenate([lax.dynamic_index_in_dim(order, mine_row ^ o, 0, keepdims=False) for o in offsets])
    owner = mine_col ^ jnp.asarray(flips, jnp.int32)
    named = (owner[:, None] * shard + jnp.arange(shard, dtype=jnp.int32)[None, :]).reshape(-1)
    pick = (order[:, None] == named[None, :]).astype(jnp.bfloat16)

    tile = tile_of(hidden, SUB)
    parts = part_slices(hidden // tile, SHARES)
    pieces = gather_cotangent(cotangent, n_col)
    act_pieces = {o: send(activations, "row", o, n_row) for o in [1, *range(2, n_row, 2)]}
    act_pieces[0] = activations

    kept_rows, sent_rows = [slice(0, total // 2)], [slice(total // 2, total)]
    aligned, [kept], [sent] = partial_sums(
        None, (pick, pieces), down_weight, tile, *parts[0], kept_rows, sent_rows, [], "sums_first")
    got = send(sent, "row", 1, n_row)
    evens = range(2, n_row, 2)
    for o, piece in zip(evens, handed_on([act_pieces[o] for o in evens], [aligned])):
        act_pieces[o], act_pieces[o + 1] = piece, send(piece, "row", 1, n_row)

    grad_pieces = [act_pieces[o] for o in offsets]
    grad_tile = tile_of(hidden, 256)
    grad_parts = part_slices(hidden // grad_tile, GRAD_SHARES)
    done, crossed, grad = [], [], None
    for at, part in enumerate(parts[1:], 1):
        _, [next_kept], [sent] = partial_sums(
            aligned, None, down_weight, tile, *part, kept_rows, sent_rows, [act_pieces[1]] if at == 1 else [], "sums_next")
        earlier = [ended[1] for ended in done]
        if at == len(parts) - 1:
            grad = weight_grads(aligned, grad_pieces, grad_tile, *grad_parts[0], None, [sent, *crossed])
            earlier.append(grad)
        ended, crossed, [sent] = halved(kept, got, [sent], earlier, n_row)
        done.append(ended)
        kept, got = next_kept, send(sent, "row", 1, n_row)
    ended, crossed, _ = halved(kept, got, [], [], n_row)
    done.append(ended)
    weight_grad = weight_grads(aligned, grad_pieces, grad_tile, *grad_parts[1], grad, crossed)
    return weight_grad, totals(done, [weight_grad])


def solution(mesh):
    in_specs = (P("row", "col"), P("col", "row"), P("col", "row"), P())
    out_specs = (P("col", "row"), P("row", "col"))
    fn = functools.partial(body, mesh.shape["row"], mesh.shape["col"])
    return jax.shard_map(fn, mesh=mesh, in_specs=in_specs, out_specs=out_specs, check_vma=False)
```

```python
import functools

import jax
import jax.numpy as jnp
from jax import lax
from jax.experimental import pallas as pl
from jax.experimental.pallas import tpu as pltpu
from jax.sharding import PartitionSpec as P

LANES = 128
STEPS_PER_OCTAVE = 128.0
TOP = 32766.0
LEAST = 2.0 ** -120
VMEM_LIMIT = 48 * 1024 * 1024
SMALL_LIMIT = 8 * 1024 * 1024
SLOTS = 4
SHARES = (2, 4, 1)
GRAD_SHARES = (4, 3)
SUB = 256


def tile_of(size, largest):
    tile = largest
    while size % tile:
        tile //= 2
    return tile


def dot(left, right, dims):
    return lax.dot_general(left, right, (dims, ((), ())), preferred_element_type=jnp.float32)


def encode(values):
    most = jnp.maximum(jnp.max(jnp.abs(values), axis=1, keepdims=True), LEAST)
    level = jnp.ceil(jnp.log2(most) * STEPS_PER_OCTAVE) + 1.0
    codes = jnp.round(values * jnp.exp2(level * (-1.0 / STEPS_PER_OCTAVE)) * TOP)
    return codes.astype(jnp.int32).astype(jnp.int16), level


def decode(codes, levels):
    scale = jnp.exp2(levels.astype(jnp.int32).astype(jnp.float32) * (1.0 / STEPS_PER_OCTAVE)) * (1.0 / TOP)
    return codes.astype(jnp.int32).astype(jnp.float32) * scale


def to_levels(levels):
    return levels.astype(jnp.int32).astype(jnp.int16)


def params(limit=VMEM_LIMIT):
    return pltpu.CompilerParams(vmem_limit_bytes=limit)


def cost(flops, moved):
    return pl.CostEstimate(flops=flops, bytes_accessed=moved, transcendentals=0)


def align_rows(pick_ref, pieces, aligned_ref):
    depth = aligned_ref.shape[1]
    chunk = tile_of(depth, 512)
    for at in range(0, depth, chunk):
        cols = slice(at, at + chunk)
        gathered = jnp.concatenate([piece[:, cols] for piece in pieces], axis=0)
        aligned_ref[:, cols] = dot(pick_ref[...], gathered, ((1,), (0,))).astype(jnp.bfloat16)


def sums_kernel(n_pieces, n_blocks, n_later, coded, kept_rows, sent_rows, tile, *refs):
    refs = list(refs)
    if n_pieces:
        pick_ref = refs.pop(0)
        pieces = [refs.pop(0) for _ in range(n_pieces)]
    else:
        aligned_ref = refs.pop(0)
    weights = [refs.pop(0) for _ in range(n_blocks)]
    del refs[:n_later]
    if n_pieces:
        aligned_ref = refs.pop(0)
    kept = [refs.pop(0) for _ in kept_rows]
    sent = [refs.pop(0) for _ in sent_rows]
    levels_ref, = refs
    step = pl.program_id(0)
    width = sent[0].shape[1] - LANES

    @pl.when(step == 0)
    def _():
        if n_pieces:
            align_rows(pick_ref, pieces, aligned_ref)
        levels_ref[...] = jnp.zeros_like(levels_ref)

    lane = lax.broadcasted_iota(jnp.int32, levels_ref.shape, 1)
    levels = levels_ref[...]
    for part in range(n_blocks):
        at = step * n_blocks + part
        cols = pl.ds(pl.multiple_of(at * tile, tile), tile)
        values = dot(aligned_ref[...], weights[part][...], ((1,), (1,)))
        for ref, rows in zip(kept, kept_rows):
            ref[:, part * tile:(part + 1) * tile] = values[rows]
        codes, level = encode(values[coded:])
        levels = jnp.where(lane == at, level, levels)
        for ref, rows in zip(sent, sent_rows):
            ref[:, cols] = codes[rows.start - coded:rows.stop - coded]
    levels_ref[...] = levels

    @pl.when(step == pl.num_programs(0) - 1)
    def _():
        for ref, rows in zip(sent, sent_rows):
            ref[:, width:] = to_levels(levels[rows.start - coded:rows.stop - coded])


def partial_sums(aligned, align, weight, tile, first, count, kept_rows, sent_rows, later_than, name):
    depth = weight.shape[1]
    width = count * tile
    whole = lambda i: (0, 0)
    operands = [align[0], *align[1]] if aligned is None else [aligned]
    total = operands[0].shape[0]
    coded = min(rows.start for rows in sent_rows)
    n_blocks = 2 if count % 2 == 0 and first % 2 == 0 else 1
    block_at = lambda part: (lambda i: (i * n_blocks + first + part, 0))
    heights = lambda spans: [span.stop - span.start for span in spans]
    in_specs = [pl.BlockSpec(operand.shape, whole) for operand in operands]
    in_specs += [pl.BlockSpec((tile, depth), block_at(part)) for part in range(n_blocks)]
    in_specs += [pl.BlockSpec(memory_space=pl.ANY)] * len(later_than)
    out_specs = [pl.BlockSpec((height, n_blocks * tile), lambda i: (0, i)) for height in heights(kept_rows)]
    out_specs += [pl.BlockSpec((height, width + LANES), whole) for height in heights(sent_rows)]
    out_shape = [jax.ShapeDtypeStruct((height, width), jnp.float32) for height in heights(kept_rows)]
    out_shape += [jax.ShapeDtypeStruct((height, width + LANES), jnp.int16) for height in heights(sent_rows)]
    if aligned is None:
        out_specs.insert(0, pl.BlockSpec((total, depth), whole))
        out_shape.insert(0, jax.ShapeDtypeStruct((total, depth), jnp.bfloat16))
    outs = pl.pallas_call(
        functools.partial(
            sums_kernel, 0 if aligned is not None else len(align[1]), n_blocks, len(later_than), coded, kept_rows, sent_rows, tile),
        grid=(count // n_blocks,), in_specs=in_specs, out_specs=out_specs, out_shape=out_shape,
        scratch_shapes=[pltpu.VMEM((total - coded, LANES), jnp.float32)],
        compiler_params=params(),
        cost_estimate=cost(2 * total * width * depth, 2 * width * depth), name=name,
    )(*operands, *[weight] * n_blocks, *later_than)
    if aligned is None:
        aligned, *outs = outs
    return aligned, outs[:len(kept_rows)], outs[len(kept_rows):]


def weight_kernel(n_pieces, first, n_later, tile, aligned_ref, *refs):
    pieces = [ref[...] for ref in refs[:n_pieces]]
    out_ref, held_ref, left_sem = refs[n_pieces + n_later:]
    step = pl.program_id(0)
    last = pl.num_programs(0) - 1
    slots = held_ref.shape[0]

    def leave(at):
        rows = pl.ds(pl.multiple_of((first + at) * tile, tile), tile)
        slot = lax.rem(at, slots)
        return pltpu.make_async_copy(held_ref.at[slot], out_ref.at[rows], left_sem.at[slot])

    @pl.when(step >= slots)
    def _():
        leave(step - slots).wait()

    left = jnp.concatenate(pieces, axis=0)
    depth = aligned_ref.shape[1]
    chunk = tile_of(depth, 1024)
    block = held_ref.at[lax.rem(step, slots)]
    for at in range(0, depth, chunk):
        cols = slice(at, at + chunk)
        block[:, cols] = dot(left, aligned_ref[:, cols], ((0,), (0,))).astype(jnp.bfloat16)
    leave(step).start()

    @pl.when(step == last)
    def _():
        for back in range(slots - 1, -1, -1):
            @pl.when(last >= back)
            def _():
                leave(last - back).wait()


def weight_grads(aligned, pieces, tile, first, count, filled, later_than):
    total, depth = aligned.shape
    rows, hidden = pieces[0].shape
    later = ([] if filled is None else [filled]) + list(later_than)
    return pl.pallas_call(
        functools.partial(weight_kernel, len(pieces), first, len(later), tile),
        grid=(count,),
        in_specs=[pl.BlockSpec((total, depth), lambda i: (0, 0))]
        + [pl.BlockSpec((rows, tile), lambda i: (0, i + first))] * len(pieces)
        + [pl.BlockSpec(memory_space=pl.ANY)] * len(later),
        out_specs=pl.BlockSpec(memory_space=pl.ANY),
        out_shape=jax.ShapeDtypeStruct((hidden, depth), jnp.bfloat16),
        scratch_shapes=[pltpu.VMEM((SLOTS, tile, depth), jnp.bfloat16), pltpu.SemaphoreType.DMA((SLOTS,))],
        input_output_aliases={} if filled is None else {1 + len(pieces): 0},
        compiler_params=params(), cost_estimate=cost(2 * total * count * tile * depth, 2 * count * tile * depth),
        name="weight_grads",
    )(aligned, *pieces, *later)


def fold_kernel(n_others, kept_ref, got_ref, *refs):
    next_ref, sent_ref = refs[n_others:n_others + 2]
    width = kept_ref.shape[1]
    half = next_ref.shape[0]
    sub = tile_of(width, SUB)
    lane = lax.broadcasted_iota(jnp.int32, (half, LANES), 1)
    levels = jnp.zeros(lane.shape, jnp.float32)
    got_levels = got_ref[:, width:]
    for at in range(width // sub):
        cols = slice(at * sub, (at + 1) * sub)
        total = kept_ref[:, cols] + decode(got_ref[:, cols], got_levels[:, at:at + 1])
        next_ref[:, cols] = total[:half]
        codes, level = encode(total[half:])
        sent_ref[:, cols] = codes
        levels = jnp.where(lane == at, level, levels)
    sent_ref[:, width:] = to_levels(levels)


def fold(kept, got, passed, later_than):
    others = [*passed, *later_than]
    vmem, anywhere = pl.BlockSpec(memory_space=pltpu.VMEM), pl.BlockSpec(memory_space=pl.ANY)
    rows, width = kept.shape
    kept, sent, *passed = pl.pallas_call(
        functools.partial(fold_kernel, len(others)),
        in_specs=[vmem] * 2 + [anywhere] * len(others),
        out_specs=[vmem] * 2 + [anywhere] * len(passed),
        out_shape=[jax.ShapeDtypeStruct((rows // 2, width), kept.dtype), jax.ShapeDtypeStruct((rows // 2, got.shape[1]), got.dtype)]
        + [jax.ShapeDtypeStruct(array.shape, array.dtype) for array in passed],
        input_output_aliases={2 + at: 2 + at for at in range(len(passed))},
        compiler_params=params(), cost_estimate=cost(kept.size * 20, kept.size * 12), name="fold",
    )(kept, got, *others)
    return kept, sent, passed


def total_kernel(counts, *refs):
    refs = list(refs)
    out_ref = refs.pop()
    base = 0
    for count in counts:
        kept_ref, got, refs = refs[0], refs[1:count], refs[count:]
        rows, width = kept_ref.shape
        sub = tile_of(width, SUB)
        for at in range(width // sub):
            cols = slice(at * sub, (at + 1) * sub)
            total = kept_ref[:, cols]
            for ref in got:
                total = total + decode(ref[:rows, cols], ref[:rows, width:][:, at:at + 1])
            out_ref[:, base + at * sub:base + (at + 1) * sub] = total.astype(jnp.bfloat16)
        base += width


def totals(parts, later_than):
    rows = parts[0][0].shape[0]
    hidden = sum(part[0].shape[1] for part in parts)
    flat = [array for part in parts for array in part]
    return pl.pallas_call(
        functools.partial(total_kernel, [len(part) for part in parts]),
        in_specs=[pl.BlockSpec(memory_space=pltpu.VMEM)] * len(flat) + [pl.BlockSpec(memory_space=pl.ANY)] * len(later_than),
        out_shape=jax.ShapeDtypeStruct((rows, hidden), jnp.bfloat16),
        compiler_params=params(), cost_estimate=cost(rows * hidden * 40, rows * hidden * 14), name="totals",
    )(*flat, *later_than)


def send(value, axis, flip, size):
    return lax.ppermute(value, axis, [(i, i ^ flip) for i in range(size)])


def stack_kernel(n_values, *refs):
    out_ref = refs[-1]
    rows = refs[0].shape[0]
    for at, ref in enumerate(refs[:n_values]):
        out_ref[at * rows:(at + 1) * rows] = ref[...]


def stacked(values, later_than=()):
    rows, width = values[0].shape
    return pl.pallas_call(
        functools.partial(stack_kernel, len(values)),
        in_specs=[pl.BlockSpec(memory_space=pltpu.VMEM)] * len(values) + [pl.BlockSpec(memory_space=pl.ANY)] * len(later_than),
        out_shape=jax.ShapeDtypeStruct((len(values) * rows, width), values[0].dtype),
        compiler_params=params(SMALL_LIMIT), cost_estimate=cost(0, 4 * len(values) * rows * width), name="stacked",
    )(*values, *later_than)


def same_kernel(*refs):
    pass


def handed_on(values, later_than):
    anywhere = pl.BlockSpec(memory_space=pl.ANY)
    return pl.pallas_call(
        same_kernel,
        in_specs=[anywhere] * (len(values) + len(later_than)), out_specs=[anywhere] * len(values),
        out_shape=[jax.ShapeDtypeStruct(value.shape, value.dtype) for value in values],
        input_output_aliases={at: at for at in range(len(values))},
        compiler_params=params(SMALL_LIMIT), cost_estimate=cost(0, 0), name="handed_on",
    )(*values, *later_than)


def gather_cotangent(cotangent, n_col):
    pieces = [cotangent] + [send(cotangent, "col", flip, n_col) for flip in range(2, n_col, 2)]
    stacks = [stacked(pieces[:2])]
    stacks.append(stacked(pieces[2:], stacks))
    return stacks + [send(stack, "col", 1, n_col) for stack in stacks]


def halving_order(size):
    order = [0]
    while len(order) < size:
        order = [2 * o for o in order] + [2 * o + 1 for o in order]
    return order


def part_slices(tiles, shares):
    ends = [tiles * sum(shares[:at]) // 7 for at in range(len(shares) + 1)]
    return [(first, last - first) for first, last in zip(ends, ends[1:])]


def halved(kept, got, passed, later_than, n_row):
    step, sent = 2, None
    while step < n_row:
        kept, sent, passed = fold(kept, got, passed, later_than)
        got = send(sent, "row", step, n_row)
        step *= 2
    return [kept, got], [sent] if sent is not None else [], passed


def body(n_row, n_col, activations, cotangent, down_weight, row_order):
    rows, hidden = activations.shape
    shard = cotangent.shape[0]
    mine_row, mine_col = lax.axis_index("row"), lax.axis_index("col")
    offsets = halving_order(n_row)
    total = n_row * rows

    flips = list(range(0, n_col, 2))
    flips += [flip ^ 1 for flip in flips]
    order = row_order.reshape(n_row, rows)
    order = jnp.concatenate([lax.dynamic_index_in_dim(order, mine_row ^ o, 0, keepdims=False) for o in offsets])
    owner = mine_col ^ jnp.asarray(flips, jnp.int32)
    named = (owner[:, None] * shard + jnp.arange(shard, dtype=jnp.int32)[None, :]).reshape(-1)
    pick = (order[:, None] == named[None, :]).astype(jnp.bfloat16)

    tile = tile_of(hidden, SUB)
    parts = part_slices(hidden // tile, SHARES)
    pieces = gather_cotangent(cotangent, n_col)
    act_pieces = {o: send(activations, "row", o, n_row) for o in [1, *range(2, n_row, 2)]}
    act_pieces[0] = activations

    kept_rows, sent_rows = [slice(0, total // 2)], [slice(total // 2, total)]
    aligned, [kept], [sent] = partial_sums(
        None, (pick, pieces), down_weight, tile, *parts[0], kept_rows, sent_rows, [], "sums_first")
    got = send(sent, "row", 1, n_row)
    evens = range(2, n_row, 2)
    for o, piece in zip(evens, handed_on([act_pieces[o] for o in evens], [aligned])):
        act_pieces[o], act_pieces[o + 1] = piece, send(piece, "row", 1, n_row)

    grad_pieces = [act_pieces[o] for o in offsets]
    grad_tile = tile_of(hidden, 256)
    grad_parts = part_slices(hidden // grad_tile, GRAD_SHARES)
    done, crossed, grad = [], [], None
    for at, part in enumerate(parts[1:], 1):
        _, [next_kept], [sent] = partial_sums(
            aligned, None, down_weight, tile, *part, kept_rows, sent_rows, [act_pieces[1]] if at == 1 else [], "sums_next")
        earlier = [ended[1] for ended in done]
        if at == len(parts) - 1:
            grad = weight_grads(aligned, grad_pieces, grad_tile, *grad_parts[0], None, [sent, *crossed])
            earlier.append(grad)
        ended, crossed, [sent] = halved(kept, got, [sent], earlier, n_row)
        done.append(ended)
        kept, got = next_kept, send(sent, "row", 1, n_row)
    ended, crossed, _ = halved(kept, got, [], [], n_row)
    done.append(ended)
    weight_grad = weight_grads(aligned, grad_pieces, grad_tile, *grad_parts[1], grad, crossed)
    return weight_grad, totals(done, [weight_grad])


def solution(mesh):
    in_specs = (P("row", "col"), P("col", "row"), P("col", "row"), P())
    out_specs = (P("col", "row"), P("row", "col"))
    fn = functools.partial(body, mesh.shape["row"], mesh.shape["col"])
    return jax.shard_map(fn, mesh=mesh, in_specs=in_specs, out_specs=out_specs, check_vma=False)
```

```python
import functools

import jax
import jax.numpy as jnp
from jax import lax
from jax.experimental import pallas as pl
from jax.experimental.pallas import tpu as pltpu
from jax.sharding import PartitionSpec as P

LANES = 128
STEPS_PER_OCTAVE = 128.0
TOP = 32766.0
LEAST = 2.0 ** -120
VMEM_LIMIT = 48 * 1024 * 1024
SMALL_LIMIT = 8 * 1024 * 1024
SLOTS = 4
SHARES = (2, 3, 2)
SUB = 256


def tile_of(size, largest):
    tile = largest
    while size % tile:
        tile //= 2
    return tile


def dot(left, right, dims):
    return lax.dot_general(left, right, (dims, ((), ())), preferred_element_type=jnp.float32)


def encode(values):
    most = jnp.maximum(jnp.max(jnp.abs(values), axis=1, keepdims=True), LEAST)
    level = jnp.ceil(jnp.log2(most) * STEPS_PER_OCTAVE) + 1.0
    codes = jnp.round(values * jnp.exp2(level * (-1.0 / STEPS_PER_OCTAVE)) * TOP)
    return codes.astype(jnp.int32).astype(jnp.int16), level


def decode(codes, levels):
    scale = jnp.exp2(levels.astype(jnp.int32).astype(jnp.float32) * (1.0 / STEPS_PER_OCTAVE)) * (1.0 / TOP)
    return codes.astype(jnp.int32).astype(jnp.float32) * scale


def to_levels(levels):
    return levels.astype(jnp.int32).astype(jnp.int16)


def params(limit=VMEM_LIMIT):
    return pltpu.CompilerParams(vmem_limit_bytes=limit)


def cost(flops, moved):
    return pl.CostEstimate(flops=flops, bytes_accessed=moved, transcendentals=0)


def align_rows(pick_ref, pieces, aligned_ref):
    depth = aligned_ref.shape[1]
    chunk = tile_of(depth, 512)
    for at in range(0, depth, chunk):
        cols = slice(at, at + chunk)
        gathered = jnp.concatenate([piece[:, cols] for piece in pieces], axis=0)
        aligned_ref[:, cols] = dot(pick_ref[...], gathered, ((1,), (0,))).astype(jnp.bfloat16)


def sums_kernel(n_pieces, n_blocks, n_later, coded, kept_rows, sent_rows, tile, *refs):
    refs = list(refs)
    if n_pieces:
        pick_ref = refs.pop(0)
        pieces = [refs.pop(0) for _ in range(n_pieces)]
    else:
        aligned_ref = refs.pop(0)
    weights = [refs.pop(0) for _ in range(n_blocks)]
    del refs[:n_later]
    if n_pieces:
        aligned_ref = refs.pop(0)
    kept = [refs.pop(0) for _ in kept_rows]
    sent = [refs.pop(0) for _ in sent_rows]
    levels_ref, = refs
    step = pl.program_id(0)
    width = sent[0].shape[1] - LANES

    @pl.when(step == 0)
    def _():
        if n_pieces:
            align_rows(pick_ref, pieces, aligned_ref)
        levels_ref[...] = jnp.zeros_like(levels_ref)

    lane = lax.broadcasted_iota(jnp.int32, levels_ref.shape, 1)
    levels = levels_ref[...]
    for part in range(n_blocks):
        at = step * n_blocks + part
        cols = pl.ds(pl.multiple_of(at * tile, tile), tile)
        values = dot(aligned_ref[...], weights[part][...], ((1,), (1,)))
        for ref, rows in zip(kept, kept_rows):
            ref[:, part * tile:(part + 1) * tile] = values[rows]
        codes, level = encode(values[coded:])
        levels = jnp.where(lane == at, level, levels)
        for ref, rows in zip(sent, sent_rows):
            ref[:, cols] = codes[rows.start - coded:rows.stop - coded]
    levels_ref[...] = levels

    @pl.when(step == pl.num_programs(0) - 1)
    def _():
        for ref, rows in zip(sent, sent_rows):
            ref[:, width:] = to_levels(levels[rows.start - coded:rows.stop - coded])


def partial_sums(aligned, align, weight, tile, first, count, kept_rows, sent_rows, later_than, name):
    depth = weight.shape[1]
    width = count * tile
    whole = lambda i: (0, 0)
    operands = [align[0], *align[1]] if aligned is None else [aligned]
    total = operands[0].shape[0]
    coded = min(rows.start for rows in sent_rows)
    n_blocks = 2 if count % 2 == 0 and first % 2 == 0 else 1
    block_at = lambda part: (lambda i: (i * n_blocks + first + part, 0))
    heights = lambda spans: [span.stop - span.start for span in spans]
    in_specs = [pl.BlockSpec(operand.shape, whole) for operand in operands]
    in_specs += [pl.BlockSpec((tile, depth), block_at(part)) for part in range(n_blocks)]
    in_specs += [pl.BlockSpec(memory_space=pl.ANY)] * len(later_than)
    out_specs = [pl.BlockSpec((height, n_blocks * tile), lambda i: (0, i)) for height in heights(kept_rows)]
    out_specs += [pl.BlockSpec((height, width + LANES), whole) for height in heights(sent_rows)]
    out_shape = [jax.ShapeDtypeStruct((height, width), jnp.float32) for height in heights(kept_rows)]
    out_shape += [jax.ShapeDtypeStruct((height, width + LANES), jnp.int16) for height in heights(sent_rows)]
    if aligned is None:
        out_specs.insert(0, pl.BlockSpec((total, depth), whole))
        out_shape.insert(0, jax.ShapeDtypeStruct((total, depth), jnp.bfloat16))
    outs = pl.pallas_call(
        functools.partial(
            sums_kernel, 0 if aligned is not None else len(align[1]), n_blocks, len(later_than), coded, kept_rows, sent_rows, tile),
        grid=(count // n_blocks,), in_specs=in_specs, out_specs=out_specs, out_shape=out_shape,
        scratch_shapes=[pltpu.VMEM((total - coded, LANES), jnp.float32)],
        compiler_params=params(),
        cost_estimate=cost(2 * total * width * depth, 2 * width * depth), name=name,
    )(*operands, *[weight] * n_blocks, *later_than)
    if aligned is None:
        aligned, *outs = outs
    return aligned, outs[:len(kept_rows)], outs[len(kept_rows):]


def weight_kernel(n_pieces, first, n_later, tile, aligned_ref, *refs):
    pieces = [ref[...] for ref in refs[:n_pieces]]
    out_ref, held_ref, left_sem = refs[n_pieces + n_later:]
    step = pl.program_id(0)
    last = pl.num_programs(0) - 1
    slots = held_ref.shape[0]

    def leave(at):
        rows = pl.ds(pl.multiple_of((first + at) * tile, tile), tile)
        slot = lax.rem(at, slots)
        return pltpu.make_async_copy(held_ref.at[slot], out_ref.at[rows], left_sem.at[slot])

    @pl.when(step >= slots)
    def _():
        leave(step - slots).wait()

    left = jnp.concatenate(pieces, axis=0)
    depth = aligned_ref.shape[1]
    chunk = tile_of(depth, 1024)
    block = held_ref.at[lax.rem(step, slots)]
    for at in range(0, depth, chunk):
        cols = slice(at, at + chunk)
        block[:, cols] = dot(left, aligned_ref[:, cols], ((0,), (0,))).astype(jnp.bfloat16)
    leave(step).start()

    @pl.when(step == last)
    def _():
        for back in range(slots - 1, -1, -1):
            @pl.when(last >= back)
            def _():
                leave(last - back).wait()


def weight_grads(aligned, pieces, tile, first, count, filled, later_than):
    total, depth = aligned.shape
    rows, hidden = pieces[0].shape
    later = ([] if filled is None else [filled]) + list(later_than)
    return pl.pallas_call(
        functools.partial(weight_kernel, len(pieces), first, len(later), tile),
        grid=(count,),
        in_specs=[pl.BlockSpec((total, depth), lambda i: (0, 0))]
        + [pl.BlockSpec((rows, tile), lambda i: (0, i + first))] * len(pieces)
        + [pl.BlockSpec(memory_space=pl.ANY)] * len(later),
        out_specs=pl.BlockSpec(memory_space=pl.ANY),
        out_shape=jax.ShapeDtypeStruct((hidden, depth), jnp.bfloat16),
        scratch_shapes=[pltpu.VMEM((SLOTS, tile, depth), jnp.bfloat16), pltpu.SemaphoreType.DMA((SLOTS,))],
        input_output_aliases={} if filled is None else {1 + len(pieces): 0},
        compiler_params=params(), cost_estimate=cost(2 * total * count * tile * depth, 2 * count * tile * depth),
        name="weight_grads",
    )(aligned, *pieces, *later)


def fold_kernel(kept_ref, got_ref, *refs):
    n_passed = (len(refs) - 2) // 2
    next_ref, sent_ref = refs[n_passed:n_passed + 2]
    width = kept_ref.shape[1]
    half = next_ref.shape[0]
    sub = tile_of(width, SUB)
    lane = lax.broadcasted_iota(jnp.int32, (half, LANES), 1)
    levels = jnp.zeros(lane.shape, jnp.float32)
    got_levels = got_ref[:, width:]
    for at in range(width // sub):
        cols = slice(at * sub, (at + 1) * sub)
        total = kept_ref[:, cols] + decode(got_ref[:, cols], got_levels[:, at:at + 1])
        next_ref[:, cols] = total[:half]
        codes, level = encode(total[half:])
        sent_ref[:, cols] = codes
        levels = jnp.where(lane == at, level, levels)
    sent_ref[:, width:] = to_levels(levels)


def fold(kept, got, passed):
    vmem, anywhere = pl.BlockSpec(memory_space=pltpu.VMEM), pl.BlockSpec(memory_space=pl.ANY)
    rows, width = kept.shape
    kept, sent, *passed = pl.pallas_call(
        fold_kernel,
        in_specs=[vmem] * 2 + [anywhere] * len(passed),
        out_specs=[vmem] * 2 + [anywhere] * len(passed),
        out_shape=[jax.ShapeDtypeStruct((rows // 2, width), kept.dtype), jax.ShapeDtypeStruct((rows // 2, got.shape[1]), got.dtype)]
        + [jax.ShapeDtypeStruct(array.shape, array.dtype) for array in passed],
        input_output_aliases={2 + at: 2 + at for at in range(len(passed))},
        compiler_params=params(), cost_estimate=cost(kept.size * 20, kept.size * 12), name="fold",
    )(kept, got, *passed)
    return kept, sent, passed


def total_kernel(counts, *refs):
    refs = list(refs)
    out_ref = refs.pop()
    base = 0
    for count in counts:
        kept_ref, got, refs = refs[0], refs[1:count], refs[count:]
        rows, width = kept_ref.shape
        sub = tile_of(width, SUB)
        for at in range(width // sub):
            cols = slice(at * sub, (at + 1) * sub)
            total = kept_ref[:, cols]
            for ref in got:
                total = total + decode(ref[:rows, cols], ref[:rows, width:][:, at:at + 1])
            out_ref[:, base + at * sub:base + (at + 1) * sub] = total.astype(jnp.bfloat16)
        base += width


def totals(parts, later_than):
    rows = parts[0][0].shape[0]
    hidden = sum(part[0].shape[1] for part in parts)
    flat = [array for part in parts for array in part]
    return pl.pallas_call(
        functools.partial(total_kernel, [len(part) for part in parts]),
        in_specs=[pl.BlockSpec(memory_space=pltpu.VMEM)] * len(flat) + [pl.BlockSpec(memory_space=pl.ANY)] * len(later_than),
        out_shape=jax.ShapeDtypeStruct((rows, hidden), jnp.bfloat16),
        compiler_params=params(), cost_estimate=cost(rows * hidden * 40, rows * hidden * 14), name="totals",
    )(*flat, *later_than)


def send(value, axis, flip, size):
    return lax.ppermute(value, axis, [(i, i ^ flip) for i in range(size)])


def stack_kernel(n_values, *refs):
    out_ref = refs[-1]
    rows = refs[0].shape[0]
    for at, ref in enumerate(refs[:n_values]):
        out_ref[at * rows:(at + 1) * rows] = ref[...]


def stacked(values, later_than=()):
    rows, width = values[0].shape
    return pl.pallas_call(
        functools.partial(stack_kernel, len(values)),
        in_specs=[pl.BlockSpec(memory_space=pltpu.VMEM)] * len(values) + [pl.BlockSpec(memory_space=pl.ANY)] * len(later_than),
        out_shape=jax.ShapeDtypeStruct((len(values) * rows, width), values[0].dtype),
        compiler_params=params(SMALL_LIMIT), cost_estimate=cost(0, 4 * len(values) * rows * width), name="stacked",
    )(*values, *later_than)


def same_kernel(*refs):
    pass


def handed_on(values, later_than):
    anywhere = pl.BlockSpec(memory_space=pl.ANY)
    return pl.pallas_call(
        same_kernel,
        in_specs=[anywhere] * (len(values) + len(later_than)), out_specs=[anywhere] * len(values),
        out_shape=[jax.ShapeDtypeStruct(value.shape, value.dtype) for value in values],
        input_output_aliases={at: at for at in range(len(values))},
        compiler_params=params(SMALL_LIMIT), cost_estimate=cost(0, 0), name="handed_on",
    )(*values, *later_than)


def gather_cotangent(cotangent, n_col):
    pieces = [cotangent] + [send(cotangent, "col", flip, n_col) for flip in range(2, n_col, 2)]
    stacks = [stacked(pieces[:2])]
    stacks.append(stacked(pieces[2:], stacks))
    return stacks + [send(stack, "col", 1, n_col) for stack in stacks]


def halving_order(size):
    order = [0]
    while len(order) < size:
        order = [2 * o for o in order] + [2 * o + 1 for o in order]
    return order


def part_slices(tiles, shares):
    ends = [tiles * sum(shares[:at]) // 7 for at in range(len(shares) + 1)]
    return [(first, last - first) for first, last in zip(ends, ends[1:])]


def halved(kept, got, passed, n_row):
    step, sent = 2, None
    while step < n_row:
        kept, sent, passed = fold(kept, got, passed)
        got = send(sent, "row", step, n_row)
        step *= 2
    return [kept, got], [sent] if sent is not None else [], passed


def body(n_row, n_col, activations, cotangent, down_weight, row_order):
    rows, hidden = activations.shape
    shard = cotangent.shape[0]
    mine_row, mine_col = lax.axis_index("row"), lax.axis_index("col")
    offsets = halving_order(n_row)
    total = n_row * rows

    flips = list(range(0, n_col, 2))
    flips += [flip ^ 1 for flip in flips]
    order = row_order.reshape(n_row, rows)
    order = jnp.concatenate([lax.dynamic_index_in_dim(order, mine_row ^ o, 0, keepdims=False) for o in offsets])
    owner = mine_col ^ jnp.asarray(flips, jnp.int32)
    named = (owner[:, None] * shard + jnp.arange(shard, dtype=jnp.int32)[None, :]).reshape(-1)
    pick = (order[:, None] == named[None, :]).astype(jnp.bfloat16)

    tile = tile_of(hidden, 256)
    parts = part_slices(hidden // tile, SHARES)
    pieces = gather_cotangent(cotangent, n_col)
    act_pieces = {o: send(activations, "row", o, n_row) for o in [1, *range(2, n_row, 2)]}
    act_pieces[0] = activations

    kept_rows, sent_rows = [slice(0, total // 2)], [slice(total // 2, total)]
    aligned, [kept], [sent] = partial_sums(
        None, (pick, pieces), down_weight, tile, *parts[0], kept_rows, sent_rows, [], "sums_first")
    got = send(sent, "row", 1, n_row)
    done, crossed = [], []
    for at, part in enumerate(parts[1:]):
        _, [next_kept], [sent] = partial_sums(
            aligned, None, down_weight, tile, *part, kept_rows, sent_rows, [act_pieces[1]] if at == 0 else [], "sums_next")
        ended, crossed, [sent] = halved(kept, got, [sent], n_row)
        if at == 0:
            evens = range(2, n_row, 2)
            for o, piece in zip(evens, handed_on([act_pieces[o] for o in evens], crossed)):
                act_pieces[o], act_pieces[o + 1] = piece, send(piece, "row", 1, n_row)
        done.append(ended)
        kept, got = next_kept, send(sent, "row", 1, n_row)

    grad_pieces = [act_pieces[o] for o in offsets]
    (first_a, count_a), (first_b, count_b) = part_slices(hidden // tile, (4, 3))
    grad = weight_grads(aligned, grad_pieces, tile, first_a, count_a, None, crossed)
    ended, crossed, _ = halved(kept, got, [], n_row)
    done.append(ended)
    weight_grad = weight_grads(aligned, grad_pieces, tile, first_b, count_b, grad, crossed)
    return weight_grad, totals(done, [weight_grad])


def solution(mesh):
    in_specs = (P("row", "col"), P("col", "row"), P("col", "row"), P())
    out_specs = (P("col", "row"), P("row", "col"))
    fn = functools.partial(body, mesh.shape["row"], mesh.shape["col"])
    return jax.shard_map(fn, mesh=mesh, in_specs=in_specs, out_specs=out_specs, check_vma=False)
```

```python
import functools

import jax
import jax.numpy as jnp
from jax import lax
from jax.experimental import pallas as pl
from jax.experimental.pallas import tpu as pltpu
from jax.sharding import PartitionSpec as P

LANES = 128
STEPS_PER_OCTAVE = 128.0
TOP = 32766.0
LEAST = 2.0 ** -120
VMEM_LIMIT = 48 * 1024 * 1024
SMALL_LIMIT = 8 * 1024 * 1024
SLOTS = 4
SHARES = (2, 2, 3)
SUB = 256


def tile_of(size, largest):
    tile = largest
    while size % tile:
        tile //= 2
    return tile


def dot(left, right, dims):
    return lax.dot_general(left, right, (dims, ((), ())), preferred_element_type=jnp.float32)


def encode(values):
    most = jnp.maximum(jnp.max(jnp.abs(values), axis=1, keepdims=True), LEAST)
    level = jnp.ceil(jnp.log2(most) * STEPS_PER_OCTAVE) + 1.0
    codes = jnp.round(values * jnp.exp2(level * (-1.0 / STEPS_PER_OCTAVE)) * TOP)
    return codes.astype(jnp.int32).astype(jnp.int16), level


def decode(codes, levels):
    scale = jnp.exp2(levels.astype(jnp.int32).astype(jnp.float32) * (1.0 / STEPS_PER_OCTAVE)) * (1.0 / TOP)
    return codes.astype(jnp.int32).astype(jnp.float32) * scale


def to_levels(levels):
    return levels.astype(jnp.int32).astype(jnp.int16)


def params(limit=VMEM_LIMIT):
    return pltpu.CompilerParams(vmem_limit_bytes=limit)


def cost(flops, moved):
    return pl.CostEstimate(flops=flops, bytes_accessed=moved, transcendentals=0)


def align_rows(pick_ref, pieces, aligned_ref):
    depth = aligned_ref.shape[1]
    chunk = tile_of(depth, 512)
    for at in range(0, depth, chunk):
        cols = slice(at, at + chunk)
        gathered = jnp.concatenate([piece[:, cols] for piece in pieces], axis=0)
        aligned_ref[:, cols] = dot(pick_ref[...], gathered, ((1,), (0,))).astype(jnp.bfloat16)


def sums_kernel(n_pieces, n_blocks, n_later, coded, kept_rows, sent_rows, tile, *refs):
    refs = list(refs)
    if n_pieces:
        pick_ref = refs.pop(0)
        pieces = [refs.pop(0) for _ in range(n_pieces)]
    else:
        aligned_ref = refs.pop(0)
    weights = [refs.pop(0) for _ in range(n_blocks)]
    del refs[:n_later]
    if n_pieces:
        aligned_ref = refs.pop(0)
    kept = [refs.pop(0) for _ in kept_rows]
    sent = [refs.pop(0) for _ in sent_rows]
    levels_ref, = refs
    step = pl.program_id(0)
    width = sent[0].shape[1] - LANES

    @pl.when(step == 0)
    def _():
        if n_pieces:
            align_rows(pick_ref, pieces, aligned_ref)
        levels_ref[...] = jnp.zeros_like(levels_ref)

    lane = lax.broadcasted_iota(jnp.int32, levels_ref.shape, 1)
    levels = levels_ref[...]
    for part in range(n_blocks):
        at = step * n_blocks + part
        cols = pl.ds(pl.multiple_of(at * tile, tile), tile)
        values = dot(aligned_ref[...], weights[part][...], ((1,), (1,)))
        for ref, rows in zip(kept, kept_rows):
            ref[:, part * tile:(part + 1) * tile] = values[rows]
        codes, level = encode(values[coded:])
        levels = jnp.where(lane == at, level, levels)
        for ref, rows in zip(sent, sent_rows):
            ref[:, cols] = codes[rows.start - coded:rows.stop - coded]
    levels_ref[...] = levels

    @pl.when(step == pl.num_programs(0) - 1)
    def _():
        for ref, rows in zip(sent, sent_rows):
            ref[:, width:] = to_levels(levels[rows.start - coded:rows.stop - coded])


def partial_sums(aligned, align, weight, tile, first, count, kept_rows, sent_rows, later_than, name):
    depth = weight.shape[1]
    width = count * tile
    whole = lambda i: (0, 0)
    operands = [align[0], *align[1]] if aligned is None else [aligned]
    total = operands[0].shape[0]
    coded = min(rows.start for rows in sent_rows)
    n_blocks = 2 if count % 2 == 0 and first % 2 == 0 else 1
    block_at = lambda part: (lambda i: (i * n_blocks + first + part, 0))
    heights = lambda spans: [span.stop - span.start for span in spans]
    in_specs = [pl.BlockSpec(operand.shape, whole) for operand in operands]
    in_specs += [pl.BlockSpec((tile, depth), block_at(part)) for part in range(n_blocks)]
    in_specs += [pl.BlockSpec(memory_space=pl.ANY)] * len(later_than)
    out_specs = [pl.BlockSpec((height, n_blocks * tile), lambda i: (0, i)) for height in heights(kept_rows)]
    out_specs += [pl.BlockSpec((height, width + LANES), whole) for height in heights(sent_rows)]
    out_shape = [jax.ShapeDtypeStruct((height, width), jnp.float32) for height in heights(kept_rows)]
    out_shape += [jax.ShapeDtypeStruct((height, width + LANES), jnp.int16) for height in heights(sent_rows)]
    if aligned is None:
        out_specs.insert(0, pl.BlockSpec((total, depth), whole))
        out_shape.insert(0, jax.ShapeDtypeStruct((total, depth), jnp.bfloat16))
    outs = pl.pallas_call(
        functools.partial(
            sums_kernel, 0 if aligned is not None else len(align[1]), n_blocks, len(later_than), coded, kept_rows, sent_rows, tile),
        grid=(count // n_blocks,), in_specs=in_specs, out_specs=out_specs, out_shape=out_shape,
        scratch_shapes=[pltpu.VMEM((total - coded, LANES), jnp.float32)],
        compiler_params=params(),
        cost_estimate=cost(2 * total * width * depth, 2 * width * depth), name=name,
    )(*operands, *[weight] * n_blocks, *later_than)
    if aligned is None:
        aligned, *outs = outs
    return aligned, outs[:len(kept_rows)], outs[len(kept_rows):]


def weight_kernel(n_pieces, first, n_later, tile, aligned_ref, *refs):
    pieces = [ref[...] for ref in refs[:n_pieces]]
    out_ref, held_ref, left_sem = refs[n_pieces + n_later:]
    step = pl.program_id(0)
    last = pl.num_programs(0) - 1
    slots = held_ref.shape[0]

    def leave(at):
        rows = pl.ds(pl.multiple_of((first + at) * tile, tile), tile)
        slot = lax.rem(at, slots)
        return pltpu.make_async_copy(held_ref.at[slot], out_ref.at[rows], left_sem.at[slot])

    @pl.when(step >= slots)
    def _():
        leave(step - slots).wait()

    left = jnp.concatenate(pieces, axis=0)
    depth = aligned_ref.shape[1]
    chunk = tile_of(depth, 1024)
    block = held_ref.at[lax.rem(step, slots)]
    for at in range(0, depth, chunk):
        cols = slice(at, at + chunk)
        block[:, cols] = dot(left, aligned_ref[:, cols], ((0,), (0,))).astype(jnp.bfloat16)
    leave(step).start()

    @pl.when(step == last)
    def _():
        for back in range(slots - 1, -1, -1):
            @pl.when(last >= back)
            def _():
                leave(last - back).wait()


def weight_grads(aligned, pieces, tile, first, count, filled, later_than):
    total, depth = aligned.shape
    rows, hidden = pieces[0].shape
    later = ([] if filled is None else [filled]) + list(later_than)
    return pl.pallas_call(
        functools.partial(weight_kernel, len(pieces), first, len(later), tile),
        grid=(count,),
        in_specs=[pl.BlockSpec((total, depth), lambda i: (0, 0))]
        + [pl.BlockSpec((rows, tile), lambda i: (0, i + first))] * len(pieces)
        + [pl.BlockSpec(memory_space=pl.ANY)] * len(later),
        out_specs=pl.BlockSpec(memory_space=pl.ANY),
        out_shape=jax.ShapeDtypeStruct((hidden, depth), jnp.bfloat16),
        scratch_shapes=[pltpu.VMEM((SLOTS, tile, depth), jnp.bfloat16), pltpu.SemaphoreType.DMA((SLOTS,))],
        input_output_aliases={} if filled is None else {1 + len(pieces): 0},
        compiler_params=params(), cost_estimate=cost(2 * total * count * tile * depth, 2 * count * tile * depth),
        name="weight_grads",
    )(aligned, *pieces, *later)


def fold_kernel(n_others, kept_ref, got_ref, *refs):
    next_ref, sent_ref = refs[n_others:n_others + 2]
    width = kept_ref.shape[1]
    half = next_ref.shape[0]
    sub = tile_of(width, SUB)
    lane = lax.broadcasted_iota(jnp.int32, (half, LANES), 1)
    levels = jnp.zeros(lane.shape, jnp.float32)
    got_levels = got_ref[:, width:]
    for at in range(width // sub):
        cols = slice(at * sub, (at + 1) * sub)
        total = kept_ref[:, cols] + decode(got_ref[:, cols], got_levels[:, at:at + 1])
        next_ref[:, cols] = total[:half]
        codes, level = encode(total[half:])
        sent_ref[:, cols] = codes
        levels = jnp.where(lane == at, level, levels)
    sent_ref[:, width:] = to_levels(levels)


def fold(kept, got, passed, later_than):
    others = [*passed, *later_than]
    vmem, anywhere = pl.BlockSpec(memory_space=pltpu.VMEM), pl.BlockSpec(memory_space=pl.ANY)
    rows, width = kept.shape
    kept, sent, *passed = pl.pallas_call(
        functools.partial(fold_kernel, len(others)),
        in_specs=[vmem] * 2 + [anywhere] * len(others),
        out_specs=[vmem] * 2 + [anywhere] * len(passed),
        out_shape=[jax.ShapeDtypeStruct((rows // 2, width), kept.dtype), jax.ShapeDtypeStruct((rows // 2, got.shape[1]), got.dtype)]
        + [jax.ShapeDtypeStruct(array.shape, array.dtype) for array in passed],
        input_output_aliases={2 + at: 2 + at for at in range(len(passed))},
        compiler_params=params(), cost_estimate=cost(kept.size * 20, kept.size * 12), name="fold",
    )(kept, got, *others)
    return kept, sent, passed


def total_kernel(counts, *refs):
    refs = list(refs)
    out_ref = refs.pop()
    base = 0
    for count in counts:
        kept_ref, got, refs = refs[0], refs[1:count], refs[count:]
        rows, width = kept_ref.shape
        sub = tile_of(width, SUB)
        for at in range(width // sub):
            cols = slice(at * sub, (at + 1) * sub)
            total = kept_ref[:, cols]
            for ref in got:
                total = total + decode(ref[:rows, cols], ref[:rows, width:][:, at:at + 1])
            out_ref[:, base + at * sub:base + (at + 1) * sub] = total.astype(jnp.bfloat16)
        base += width


def totals(parts, later_than):
    rows = parts[0][0].shape[0]
    hidden = sum(part[0].shape[1] for part in parts)
    flat = [array for part in parts for array in part]
    return pl.pallas_call(
        functools.partial(total_kernel, [len(part) for part in parts]),
        in_specs=[pl.BlockSpec(memory_space=pltpu.VMEM)] * len(flat) + [pl.BlockSpec(memory_space=pl.ANY)] * len(later_than),
        out_shape=jax.ShapeDtypeStruct((rows, hidden), jnp.bfloat16),
        compiler_params=params(), cost_estimate=cost(rows * hidden * 40, rows * hidden * 14), name="totals",
    )(*flat, *later_than)


def send(value, axis, flip, size):
    return lax.ppermute(value, axis, [(i, i ^ flip) for i in range(size)])


def stack_kernel(n_values, *refs):
    out_ref = refs[-1]
    rows = refs[0].shape[0]
    for at, ref in enumerate(refs[:n_values]):
        out_ref[at * rows:(at + 1) * rows] = ref[...]


def stacked(values, later_than=()):
    rows, width = values[0].shape
    return pl.pallas_call(
        functools.partial(stack_kernel, len(values)),
        in_specs=[pl.BlockSpec(memory_space=pltpu.VMEM)] * len(values) + [pl.BlockSpec(memory_space=pl.ANY)] * len(later_than),
        out_shape=jax.ShapeDtypeStruct((len(values) * rows, width), values[0].dtype),
        compiler_params=params(SMALL_LIMIT), cost_estimate=cost(0, 4 * len(values) * rows * width), name="stacked",
    )(*values, *later_than)


def same_kernel(*refs):
    pass


def handed_on(values, later_than):
    anywhere = pl.BlockSpec(memory_space=pl.ANY)
    return pl.pallas_call(
        same_kernel,
        in_specs=[anywhere] * (len(values) + len(later_than)), out_specs=[anywhere] * len(values),
        out_shape=[jax.ShapeDtypeStruct(value.shape, value.dtype) for value in values],
        input_output_aliases={at: at for at in range(len(values))},
        compiler_params=params(SMALL_LIMIT), cost_estimate=cost(0, 0), name="handed_on",
    )(*values, *later_than)


def gather_cotangent(cotangent, n_col):
    pieces = [cotangent] + [send(cotangent, "col", flip, n_col) for flip in range(2, n_col, 2)]
    stacks = [stacked(pieces[:2])]
    stacks.append(stacked(pieces[2:], stacks))
    return stacks + [send(stack, "col", 1, n_col) for stack in stacks]


def halving_order(size):
    order = [0]
    while len(order) < size:
        order = [2 * o for o in order] + [2 * o + 1 for o in order]
    return order


def part_slices(tiles, shares):
    ends = [tiles * sum(shares[:at]) // 7 for at in range(len(shares) + 1)]
    return [(first, last - first) for first, last in zip(ends, ends[1:])]


def halved(kept, got, passed, later_than, n_row):
    step = 2
    while step < n_row:
        kept, sent, passed = fold(kept, got, passed, later_than)
        got = send(sent, "row", step, n_row)
        step *= 2
    return [kept, got], [sent], passed


def body(n_row, n_col, activations, cotangent, down_weight, row_order):
    rows, hidden = activations.shape
    shard = cotangent.shape[0]
    mine_row, mine_col = lax.axis_index("row"), lax.axis_index("col")
    offsets = halving_order(n_row)
    total = n_row * rows

    flips = list(range(0, n_col, 2))
    flips += [flip ^ 1 for flip in flips]
    order = row_order.reshape(n_row, rows)
    order = jnp.concatenate([lax.dynamic_index_in_dim(order, mine_row ^ o, 0, keepdims=False) for o in offsets])
    owner = mine_col ^ jnp.asarray(flips, jnp.int32)
    named = (owner[:, None] * shard + jnp.arange(shard, dtype=jnp.int32)[None, :]).reshape(-1)
    pick = (order[:, None] == named[None, :]).astype(jnp.bfloat16)

    tile = tile_of(hidden, 256)
    parts = part_slices(hidden // tile, SHARES)
    pieces = gather_cotangent(cotangent, n_col)
    act_pieces = {o: send(activations, "row", o, n_row) for o in [1, *range(2, n_row, 2)]}
    act_pieces[0] = activations

    kept_rows, sent_rows = [slice(0, total // 2)], [slice(total // 2, total)]
    aligned, [kept], [sent] = partial_sums(
        None, (pick, pieces), down_weight, tile, *parts[0], kept_rows, sent_rows, [], "sums_first")
    got = send(sent, "row", 1, n_row)
    evens = range(2, n_row, 2)
    for o, piece in zip(evens, handed_on([act_pieces[o] for o in evens], [aligned])):
        act_pieces[o], act_pieces[o + 1] = piece, send(piece, "row", 1, n_row)

    _, [kept_b], [sent_b] = partial_sums(
        aligned, None, down_weight, tile, *parts[1], kept_rows, sent_rows, [act_pieces[1]], "sums_second")
    done_a, crossed, [sent_b] = halved(kept, got, [sent_b], [], n_row)
    got_b = send(sent_b, "row", 1, n_row)

    spans = [slice(at * rows, (at + 1) * rows) for at in range(n_row)]
    _, [kept_c], sent_c = partial_sums(
        aligned, None, down_weight, tile, *parts[2], spans[:1], spans[1:], crossed, "sums_last")
    done_c = [kept_c] + [send(message, "row", o, n_row) for message, o in zip(sent_c, offsets[1:])]

    grad_pieces = [act_pieces[o] for o in offsets]
    grad_tile = tile_of(hidden, 256)
    (first_a, count_a), (first_b, count_b) = part_slices(hidden // grad_tile, (3, 4))
    grad = weight_grads(aligned, grad_pieces, grad_tile, first_a, count_a, None, sent_c[:1])
    done_b, crossed_b, _ = halved(kept_b, got_b, [], [grad], n_row)
    weight_grad = weight_grads(aligned, grad_pieces, grad_tile, first_b, count_b, grad, crossed_b)
    return weight_grad, totals([done_a, done_b, done_c], [weight_grad])


def solution(mesh):
    in_specs = (P("row", "col"), P("col", "row"), P("col", "row"), P())
    out_specs = (P("col", "row"), P("row", "col"))
    fn = functools.partial(body, mesh.shape["row"], mesh.shape["col"])
    return jax.shard_map(fn, mesh=mesh, in_specs=in_specs, out_specs=out_specs, check_vma=False)
```

```python
import functools

import jax
import jax.numpy as jnp
from jax import lax
from jax.experimental import pallas as pl
from jax.experimental.pallas import tpu as pltpu
from jax.sharding import PartitionSpec as P

LANES = 128
STEPS_PER_OCTAVE = 128.0
TOP = 32766.0
LEAST = 2.0 ** -120
VMEM_LIMIT = 48 * 1024 * 1024
SMALL_LIMIT = 8 * 1024 * 1024
SLOTS = 4
SHARES = (2, 3, 2)
SUB = 256


def tile_of(size, largest):
    tile = largest
    while size % tile:
        tile //= 2
    return tile


def dot(left, right, dims):
    return lax.dot_general(left, right, (dims, ((), ())), preferred_element_type=jnp.float32)


def encode(values):
    most = jnp.maximum(jnp.max(jnp.abs(values), axis=1, keepdims=True), LEAST)
    level = jnp.ceil(jnp.log2(most) * STEPS_PER_OCTAVE) + 1.0
    codes = jnp.round(values * jnp.exp2(level * (-1.0 / STEPS_PER_OCTAVE)) * TOP)
    return codes.astype(jnp.int32).astype(jnp.int16), level


def decode(codes, levels):
    scale = jnp.exp2(levels.astype(jnp.int32).astype(jnp.float32) * (1.0 / STEPS_PER_OCTAVE)) * (1.0 / TOP)
    return codes.astype(jnp.int32).astype(jnp.float32) * scale


def to_levels(levels):
    return levels.astype(jnp.int32).astype(jnp.int16)


def params(limit=VMEM_LIMIT):
    return pltpu.CompilerParams(vmem_limit_bytes=limit)


def cost(flops, moved):
    return pl.CostEstimate(flops=flops, bytes_accessed=moved, transcendentals=0)


def align_rows(pick_ref, pieces, aligned_ref):
    depth = aligned_ref.shape[1]
    chunk = tile_of(depth, 512)
    for at in range(0, depth, chunk):
        cols = slice(at, at + chunk)
        gathered = jnp.concatenate([piece[:, cols] for piece in pieces], axis=0)
        aligned_ref[:, cols] = dot(pick_ref[...], gathered, ((1,), (0,))).astype(jnp.bfloat16)


def sums_kernel(n_pieces, n_blocks, n_later, coded, kept_rows, sent_rows, tile, *refs):
    refs = list(refs)
    if n_pieces:
        pick_ref = refs.pop(0)
        pieces = [refs.pop(0) for _ in range(n_pieces)]
    else:
        aligned_ref = refs.pop(0)
    weights = [refs.pop(0) for _ in range(n_blocks)]
    del refs[:n_later]
    if n_pieces:
        aligned_ref = refs.pop(0)
    kept = [refs.pop(0) for _ in kept_rows]
    sent = [refs.pop(0) for _ in sent_rows]
    levels_ref, = refs
    step = pl.program_id(0)
    width = sent[0].shape[1] - LANES

    @pl.when(step == 0)
    def _():
        if n_pieces:
            align_rows(pick_ref, pieces, aligned_ref)
        levels_ref[...] = jnp.zeros_like(levels_ref)

    lane = lax.broadcasted_iota(jnp.int32, levels_ref.shape, 1)
    levels = levels_ref[...]
    for part in range(n_blocks):
        at = step * n_blocks + part
        cols = pl.ds(pl.multiple_of(at * tile, tile), tile)
        values = dot(aligned_ref[...], weights[part][...], ((1,), (1,)))
        for ref, rows in zip(kept, kept_rows):
            ref[:, part * tile:(part + 1) * tile] = values[rows]
        codes, level = encode(values[coded:])
        levels = jnp.where(lane == at, level, levels)
        for ref, rows in zip(sent, sent_rows):
            ref[:, cols] = codes[rows.start - coded:rows.stop - coded]
    levels_ref[...] = levels

    @pl.when(step == pl.num_programs(0) - 1)
    def _():
        for ref, rows in zip(sent, sent_rows):
            ref[:, width:] = to_levels(levels[rows.start - coded:rows.stop - coded])


def partial_sums(aligned, align, weight, tile, first, count, kept_rows, sent_rows, later_than, name):
    depth = weight.shape[1]
    width = count * tile
    whole = lambda i: (0, 0)
    operands = [align[0], *align[1]] if aligned is None else [aligned]
    total = operands[0].shape[0]
    coded = min(rows.start for rows in sent_rows)
    n_blocks = 2 if count % 2 == 0 and first % 2 == 0 else 1
    block_at = lambda part: (lambda i: (i * n_blocks + first + part, 0))
    heights = lambda spans: [span.stop - span.start for span in spans]
    in_specs = [pl.BlockSpec(operand.shape, whole) for operand in operands]
    in_specs += [pl.BlockSpec((tile, depth), block_at(part)) for part in range(n_blocks)]
    in_specs += [pl.BlockSpec(memory_space=pl.ANY)] * len(later_than)
    out_specs = [pl.BlockSpec((height, n_blocks * tile), lambda i: (0, i)) for height in heights(kept_rows)]
    out_specs += [pl.BlockSpec((height, width + LANES), whole) for height in heights(sent_rows)]
    out_shape = [jax.ShapeDtypeStruct((height, width), jnp.float32) for height in heights(kept_rows)]
    out_shape += [jax.ShapeDtypeStruct((height, width + LANES), jnp.int16) for height in heights(sent_rows)]
    if aligned is None:
        out_specs.insert(0, pl.BlockSpec((total, depth), whole))
        out_shape.insert(0, jax.ShapeDtypeStruct((total, depth), jnp.bfloat16))
    outs = pl.pallas_call(
        functools.partial(
            sums_kernel, 0 if aligned is not None else len(align[1]), n_blocks, len(later_than), coded, kept_rows, sent_rows, tile),
        grid=(count // n_blocks,), in_specs=in_specs, out_specs=out_specs, out_shape=out_shape,
        scratch_shapes=[pltpu.VMEM((total - coded, LANES), jnp.float32)],
        compiler_params=params(),
        cost_estimate=cost(2 * total * width * depth, 2 * width * depth), name=name,
    )(*operands, *[weight] * n_blocks, *later_than)
    if aligned is None:
        aligned, *outs = outs
    return aligned, outs[:len(kept_rows)], outs[len(kept_rows):]


def weight_kernel(n_pieces, first, n_later, tile, aligned_ref, *refs):
    pieces = [ref[...] for ref in refs[:n_pieces]]
    out_ref, held_ref, left_sem = refs[n_pieces + n_later:]
    step = pl.program_id(0)
    last = pl.num_programs(0) - 1
    slots = held_ref.shape[0]

    def leave(at):
        rows = pl.ds(pl.multiple_of((first + at) * tile, tile), tile)
        slot = lax.rem(at, slots)
        return pltpu.make_async_copy(held_ref.at[slot], out_ref.at[rows], left_sem.at[slot])

    @pl.when(step >= slots)
    def _():
        leave(step - slots).wait()

    left = jnp.concatenate(pieces, axis=0)
    depth = aligned_ref.shape[1]
    chunk = tile_of(depth, 1024)
    block = held_ref.at[lax.rem(step, slots)]
    for at in range(0, depth, chunk):
        cols = slice(at, at + chunk)
        block[:, cols] = dot(left, aligned_ref[:, cols], ((0,), (0,))).astype(jnp.bfloat16)
    leave(step).start()

    @pl.when(step == last)
    def _():
        for back in range(slots - 1, -1, -1):
            @pl.when(last >= back)
            def _():
                leave(last - back).wait()


def weight_grads(aligned, pieces, tile, first, count, filled, later_than):
    total, depth = aligned.shape
    rows, hidden = pieces[0].shape
    later = ([] if filled is None else [filled]) + list(later_than)
    return pl.pallas_call(
        functools.partial(weight_kernel, len(pieces), first, len(later), tile),
        grid=(count,),
        in_specs=[pl.BlockSpec((total, depth), lambda i: (0, 0))]
        + [pl.BlockSpec((rows, tile), lambda i: (0, i + first))] * len(pieces)
        + [pl.BlockSpec(memory_space=pl.ANY)] * len(later),
        out_specs=pl.BlockSpec(memory_space=pl.ANY),
        out_shape=jax.ShapeDtypeStruct((hidden, depth), jnp.bfloat16),
        scratch_shapes=[pltpu.VMEM((SLOTS, tile, depth), jnp.bfloat16), pltpu.SemaphoreType.DMA((SLOTS,))],
        input_output_aliases={} if filled is None else {1 + len(pieces): 0},
        compiler_params=params(), cost_estimate=cost(2 * total * count * tile * depth, 2 * count * tile * depth),
        name="weight_grads",
    )(aligned, *pieces, *later)


def fold_kernel(n_others, kept_ref, got_ref, *refs):
    next_ref, sent_ref = refs[n_others:n_others + 2]
    width = kept_ref.shape[1]
    half = next_ref.shape[0]
    sub = tile_of(width, SUB)
    lane = lax.broadcasted_iota(jnp.int32, (half, LANES), 1)
    levels = jnp.zeros(lane.shape, jnp.float32)
    got_levels = got_ref[:, width:]
    for at in range(width // sub):
        cols = slice(at * sub, (at + 1) * sub)
        total = kept_ref[:, cols] + decode(got_ref[:, cols], got_levels[:, at:at + 1])
        next_ref[:, cols] = total[:half]
        codes, level = encode(total[half:])
        sent_ref[:, cols] = codes
        levels = jnp.where(lane == at, level, levels)
    sent_ref[:, width:] = to_levels(levels)


def fold(kept, got, passed, later_than):
    others = [*passed, *later_than]
    vmem, anywhere = pl.BlockSpec(memory_space=pltpu.VMEM), pl.BlockSpec(memory_space=pl.ANY)
    rows, width = kept.shape
    kept, sent, *passed = pl.pallas_call(
        functools.partial(fold_kernel, len(others)),
        in_specs=[vmem] * 2 + [anywhere] * len(others),
        out_specs=[vmem] * 2 + [anywhere] * len(passed),
        out_shape=[jax.ShapeDtypeStruct((rows // 2, width), kept.dtype), jax.ShapeDtypeStruct((rows // 2, got.shape[1]), got.dtype)]
        + [jax.ShapeDtypeStruct(array.shape, array.dtype) for array in passed],
        input_output_aliases={2 + at: 2 + at for at in range(len(passed))},
        compiler_params=params(), cost_estimate=cost(kept.size * 20, kept.size * 12), name="fold",
    )(kept, got, *others)
    return kept, sent, passed


def total_kernel(counts, *refs):
    refs = list(refs)
    out_ref = refs.pop()
    base = 0
    for count in counts:
        kept_ref, got, refs = refs[0], refs[1:count], refs[count:]
        rows, width = kept_ref.shape
        sub = tile_of(width, SUB)
        for at in range(width // sub):
            cols = slice(at * sub, (at + 1) * sub)
            total = kept_ref[:, cols]
            for ref in got:
                total = total + decode(ref[:rows, cols], ref[:rows, width:][:, at:at + 1])
            out_ref[:, base + at * sub:base + (at + 1) * sub] = total.astype(jnp.bfloat16)
        base += width


def totals(parts, later_than):
    rows = parts[0][0].shape[0]
    hidden = sum(part[0].shape[1] for part in parts)
    flat = [array for part in parts for array in part]
    return pl.pallas_call(
        functools.partial(total_kernel, [len(part) for part in parts]),
        in_specs=[pl.BlockSpec(memory_space=pltpu.VMEM)] * len(flat) + [pl.BlockSpec(memory_space=pl.ANY)] * len(later_than),
        out_shape=jax.ShapeDtypeStruct((rows, hidden), jnp.bfloat16),
        compiler_params=params(), cost_estimate=cost(rows * hidden * 40, rows * hidden * 14), name="totals",
    )(*flat, *later_than)


def send(value, axis, flip, size):
    return lax.ppermute(value, axis, [(i, i ^ flip) for i in range(size)])


def stack_kernel(n_values, *refs):
    out_ref = refs[-1]
    rows = refs[0].shape[0]
    for at, ref in enumerate(refs[:n_values]):
        out_ref[at * rows:(at + 1) * rows] = ref[...]


def stacked(values, later_than=()):
    rows, width = values[0].shape
    return pl.pallas_call(
        functools.partial(stack_kernel, len(values)),
        in_specs=[pl.BlockSpec(memory_space=pltpu.VMEM)] * len(values) + [pl.BlockSpec(memory_space=pl.ANY)] * len(later_than),
        out_shape=jax.ShapeDtypeStruct((len(values) * rows, width), values[0].dtype),
        compiler_params=params(SMALL_LIMIT), cost_estimate=cost(0, 4 * len(values) * rows * width), name="stacked",
    )(*values, *later_than)


def same_kernel(*refs):
    pass


def handed_on(values, later_than):
    anywhere = pl.BlockSpec(memory_space=pl.ANY)
    return pl.pallas_call(
        same_kernel,
        in_specs=[anywhere] * (len(values) + len(later_than)), out_specs=[anywhere] * len(values),
        out_shape=[jax.ShapeDtypeStruct(value.shape, value.dtype) for value in values],
        input_output_aliases={at: at for at in range(len(values))},
        compiler_params=params(SMALL_LIMIT), cost_estimate=cost(0, 0), name="handed_on",
    )(*values, *later_than)


def chip_order(n_col):
    return [2, *range(n_col - 2, 2, -2)]


def gather_cotangent(cotangent, n_col):
    pieces = [cotangent] + [send(cotangent, "col", flip, n_col) for flip in chip_order(n_col)]
    stacks = [stacked(pieces[:2])]
    stacks.append(stacked(pieces[2:], stacks))
    return stacks + [send(stack, "col", 1, n_col) for stack in stacks]


def halving_order(size):
    order = [0]
    while len(order) < size:
        order = [2 * o for o in order] + [2 * o + 1 for o in order]
    return order


def part_slices(tiles, shares):
    ends = [tiles * sum(shares[:at]) // 7 for at in range(len(shares) + 1)]
    return [(first, last - first) for first, last in zip(ends, ends[1:])]


def halved(kept, got, passed, later_than, n_row):
    step = 2
    while step < n_row:
        kept, sent, passed = fold(kept, got, passed, later_than)
        got = send(sent, "row", step, n_row)
        step *= 2
    return [kept, got], [sent], passed


def body(n_row, n_col, activations, cotangent, down_weight, row_order):
    rows, hidden = activations.shape
    shard = cotangent.shape[0]
    mine_row, mine_col = lax.axis_index("row"), lax.axis_index("col")
    offsets = halving_order(n_row)
    total = n_row * rows

    flips = [0, *chip_order(n_col)]
    flips += [flip ^ 1 for flip in flips]
    order = row_order.reshape(n_row, rows)
    order = jnp.concatenate([lax.dynamic_index_in_dim(order, mine_row ^ o, 0, keepdims=False) for o in offsets])
    owner = mine_col ^ jnp.asarray(flips, jnp.int32)
    named = (owner[:, None] * shard + jnp.arange(shard, dtype=jnp.int32)[None, :]).reshape(-1)
    pick = (order[:, None] == named[None, :]).astype(jnp.bfloat16)

    tile = tile_of(hidden, 256)
    parts = part_slices(hidden // tile, SHARES)
    pieces = gather_cotangent(cotangent, n_col)
    act_pieces = {o: send(activations, "row", o, n_row) for o in [1, *range(2, n_row, 2)]}
    act_pieces[0] = activations

    kept_rows, sent_rows = [slice(0, total // 2)], [slice(total // 2, total)]
    aligned, [kept], [sent] = partial_sums(
        None, (pick, pieces), down_weight, tile, *parts[0], kept_rows, sent_rows, [], "sums_first")
    got = send(sent, "row", 1, n_row)
    evens = range(2, n_row, 2)
    for o, piece in zip(evens, handed_on([act_pieces[o] for o in evens], [aligned])):
        act_pieces[o], act_pieces[o + 1] = piece, send(piece, "row", 1, n_row)

    _, [kept_b], [sent_b] = partial_sums(
        aligned, None, down_weight, tile, *parts[1], kept_rows, sent_rows, [act_pieces[1]], "sums_second")
    done_a, crossed, [sent_b] = halved(kept, got, [sent_b], [], n_row)
    got_b = send(sent_b, "row", 1, n_row)

    spans = [slice(at * rows, (at + 1) * rows) for at in range(n_row)]
    _, [kept_c], sent_c = partial_sums(
        aligned, None, down_weight, tile, *parts[2], spans[:1], spans[1:], crossed, "sums_last")
    done_c = [kept_c] + [send(message, "row", o, n_row) for message, o in zip(sent_c, offsets[1:])]

    grad_pieces = [act_pieces[o] for o in offsets]
    grad_tile = tile_of(hidden, 256)
    (first_a, count_a), (first_b, count_b) = part_slices(hidden // grad_tile, (3, 4))
    grad = weight_grads(aligned, grad_pieces, grad_tile, first_a, count_a, None, sent_c[:1])
    done_b, crossed_b, _ = halved(kept_b, got_b, [], [grad], n_row)
    weight_grad = weight_grads(aligned, grad_pieces, grad_tile, first_b, count_b, grad, crossed_b)
    return weight_grad, totals([done_a, done_b, done_c], [weight_grad])


def solution(mesh):
    in_specs = (P("row", "col"), P("col", "row"), P("col", "row"), P())
    out_specs = (P("col", "row"), P("row", "col"))
    fn = functools.partial(body, mesh.shape["row"], mesh.shape["col"])
    return jax.shard_map(fn, mesh=mesh, in_specs=in_specs, out_specs=out_specs, check_vma=False)
```

```python
import functools

import jax
import jax.numpy as jnp
from jax import lax
from jax.experimental import pallas as pl
from jax.experimental.pallas import tpu as pltpu
from jax.sharding import PartitionSpec as P

LANES = 128
STEPS_PER_OCTAVE = 128.0
TOP = 32766.0
LEAST = 2.0 ** -120
VMEM_LIMIT = 48 * 1024 * 1024
SMALL_LIMIT = 8 * 1024 * 1024
SLOTS = 4
SHARES = (3, 2, 2)
SUB = 256


def tile_of(size, largest):
    tile = largest
    while size % tile:
        tile //= 2
    return tile


def dot(left, right, dims):
    return lax.dot_general(left, right, (dims, ((), ())), preferred_element_type=jnp.float32)


def encode(values):
    most = jnp.maximum(jnp.max(jnp.abs(values), axis=1, keepdims=True), LEAST)
    level = jnp.ceil(jnp.log2(most) * STEPS_PER_OCTAVE) + 1.0
    codes = jnp.round(values * jnp.exp2(level * (-1.0 / STEPS_PER_OCTAVE)) * TOP)
    return codes.astype(jnp.int32).astype(jnp.int16), level


def decode(codes, levels):
    scale = jnp.exp2(levels.astype(jnp.int32).astype(jnp.float32) * (1.0 / STEPS_PER_OCTAVE)) * (1.0 / TOP)
    return codes.astype(jnp.int32).astype(jnp.float32) * scale


def to_levels(levels):
    return levels.astype(jnp.int32).astype(jnp.int16)


def params(limit=VMEM_LIMIT):
    return pltpu.CompilerParams(vmem_limit_bytes=limit)


def cost(flops, moved):
    return pl.CostEstimate(flops=flops, bytes_accessed=moved, transcendentals=0)


def align_rows(pick_ref, pieces, aligned_ref):
    depth = aligned_ref.shape[1]
    chunk = tile_of(depth, 512)
    for at in range(0, depth, chunk):
        cols = slice(at, at + chunk)
        gathered = jnp.concatenate([piece[:, cols] for piece in pieces], axis=0)
        aligned_ref[:, cols] = dot(pick_ref[...], gathered, ((1,), (0,))).astype(jnp.bfloat16)


def sums_kernel(n_pieces, n_blocks, n_later, coded, kept_rows, sent_rows, tile, *refs):
    refs = list(refs)
    if n_pieces:
        pick_ref = refs.pop(0)
        pieces = [refs.pop(0) for _ in range(n_pieces)]
    else:
        aligned_ref = refs.pop(0)
    weights = [refs.pop(0) for _ in range(n_blocks)]
    del refs[:n_later]
    if n_pieces:
        aligned_ref = refs.pop(0)
    kept = [refs.pop(0) for _ in kept_rows]
    sent = [refs.pop(0) for _ in sent_rows]
    levels_ref, = refs
    step = pl.program_id(0)
    width = sent[0].shape[1] - LANES

    @pl.when(step == 0)
    def _():
        if n_pieces:
            align_rows(pick_ref, pieces, aligned_ref)
        levels_ref[...] = jnp.zeros_like(levels_ref)

    lane = lax.broadcasted_iota(jnp.int32, levels_ref.shape, 1)
    levels = levels_ref[...]
    for part in range(n_blocks):
        at = step * n_blocks + part
        cols = pl.ds(pl.multiple_of(at * tile, tile), tile)
        values = dot(aligned_ref[...], weights[part][...], ((1,), (1,)))
        for ref, rows in zip(kept, kept_rows):
            ref[:, part * tile:(part + 1) * tile] = values[rows]
        codes, level = encode(values[coded:])
        levels = jnp.where(lane == at, level, levels)
        for ref, rows in zip(sent, sent_rows):
            ref[:, cols] = codes[rows.start - coded:rows.stop - coded]
    levels_ref[...] = levels

    @pl.when(step == pl.num_programs(0) - 1)
    def _():
        for ref, rows in zip(sent, sent_rows):
            ref[:, width:] = to_levels(levels[rows.start - coded:rows.stop - coded])


def partial_sums(aligned, align, weight, tile, first, count, kept_rows, sent_rows, later_than, name):
    depth = weight.shape[1]
    width = count * tile
    whole = lambda i: (0, 0)
    operands = [align[0], *align[1]] if aligned is None else [aligned]
    total = operands[0].shape[0]
    coded = min(rows.start for rows in sent_rows)
    n_blocks = 2 if count % 2 == 0 and first % 2 == 0 else 1
    block_at = lambda part: (lambda i: (i * n_blocks + first + part, 0))
    heights = lambda spans: [span.stop - span.start for span in spans]
    in_specs = [pl.BlockSpec(operand.shape, whole) for operand in operands]
    in_specs += [pl.BlockSpec((tile, depth), block_at(part)) for part in range(n_blocks)]
    in_specs += [pl.BlockSpec(memory_space=pl.ANY)] * len(later_than)
    out_specs = [pl.BlockSpec((height, n_blocks * tile), lambda i: (0, i)) for height in heights(kept_rows)]
    out_specs += [pl.BlockSpec((height, width + LANES), whole) for height in heights(sent_rows)]
    out_shape = [jax.ShapeDtypeStruct((height, width), jnp.float32) for height in heights(kept_rows)]
    out_shape += [jax.ShapeDtypeStruct((height, width + LANES), jnp.int16) for height in heights(sent_rows)]
    if aligned is None:
        out_specs.insert(0, pl.BlockSpec((total, depth), whole))
        out_shape.insert(0, jax.ShapeDtypeStruct((total, depth), jnp.bfloat16))
    outs = pl.pallas_call(
        functools.partial(
            sums_kernel, 0 if aligned is not None else len(align[1]), n_blocks, len(later_than), coded, kept_rows, sent_rows, tile),
        grid=(count // n_blocks,), in_specs=in_specs, out_specs=out_specs, out_shape=out_shape,
        scratch_shapes=[pltpu.VMEM((total - coded, LANES), jnp.float32)],
        compiler_params=params(),
        cost_estimate=cost(2 * total * width * depth, 2 * width * depth), name=name,
    )(*operands, *[weight] * n_blocks, *later_than)
    if aligned is None:
        aligned, *outs = outs
    return aligned, outs[:len(kept_rows)], outs[len(kept_rows):]


def weight_kernel(n_pieces, first, n_later, tile, aligned_ref, *refs):
    pieces = [ref[...] for ref in refs[:n_pieces]]
    out_ref, held_ref, left_sem = refs[n_pieces + n_later:]
    step = pl.program_id(0)
    last = pl.num_programs(0) - 1
    slots = held_ref.shape[0]

    def leave(at):
        rows = pl.ds(pl.multiple_of((first + at) * tile, tile), tile)
        slot = lax.rem(at, slots)
        return pltpu.make_async_copy(held_ref.at[slot], out_ref.at[rows], left_sem.at[slot])

    @pl.when(step >= slots)
    def _():
        leave(step - slots).wait()

    left = jnp.concatenate(pieces, axis=0)
    depth = aligned_ref.shape[1]
    chunk = tile_of(depth, 1024)
    block = held_ref.at[lax.rem(step, slots)]
    for at in range(0, depth, chunk):
        cols = slice(at, at + chunk)
        block[:, cols] = dot(left, aligned_ref[:, cols], ((0,), (0,))).astype(jnp.bfloat16)
    leave(step).start()

    @pl.when(step == last)
    def _():
        for back in range(slots - 1, -1, -1):
            @pl.when(last >= back)
            def _():
                leave(last - back).wait()


def weight_grads(aligned, pieces, tile, first, count, filled, later_than):
    total, depth = aligned.shape
    rows, hidden = pieces[0].shape
    later = ([] if filled is None else [filled]) + list(later_than)
    return pl.pallas_call(
        functools.partial(weight_kernel, len(pieces), first, len(later), tile),
        grid=(count,),
        in_specs=[pl.BlockSpec((total, depth), lambda i: (0, 0))]
        + [pl.BlockSpec((rows, tile), lambda i: (0, i + first))] * len(pieces)
        + [pl.BlockSpec(memory_space=pl.ANY)] * len(later),
        out_specs=pl.BlockSpec(memory_space=pl.ANY),
        out_shape=jax.ShapeDtypeStruct((hidden, depth), jnp.bfloat16),
        scratch_shapes=[pltpu.VMEM((SLOTS, tile, depth), jnp.bfloat16), pltpu.SemaphoreType.DMA((SLOTS,))],
        input_output_aliases={} if filled is None else {1 + len(pieces): 0},
        compiler_params=params(), cost_estimate=cost(2 * total * count * tile * depth, 2 * count * tile * depth),
        name="weight_grads",
    )(aligned, *pieces, *later)


def fold_kernel(n_others, kept_ref, got_ref, *refs):
    next_ref, sent_ref = refs[n_others:n_others + 2]
    width = kept_ref.shape[1]
    half = next_ref.shape[0]
    sub = tile_of(width, SUB)
    lane = lax.broadcasted_iota(jnp.int32, (half, LANES), 1)
    levels = jnp.zeros(lane.shape, jnp.float32)
    got_levels = got_ref[:, width:]
    for at in range(width // sub):
        cols = slice(at * sub, (at + 1) * sub)
        total = kept_ref[:, cols] + decode(got_ref[:, cols], got_levels[:, at:at + 1])
        next_ref[:, cols] = total[:half]
        codes, level = encode(total[half:])
        sent_ref[:, cols] = codes
        levels = jnp.where(lane == at, level, levels)
    sent_ref[:, width:] = to_levels(levels)


def fold(kept, got, passed, later_than):
    others = [*passed, *later_than]
    vmem, anywhere = pl.BlockSpec(memory_space=pltpu.VMEM), pl.BlockSpec(memory_space=pl.ANY)
    rows, width = kept.shape
    kept, sent, *passed = pl.pallas_call(
        functools.partial(fold_kernel, len(others)),
        in_specs=[vmem] * 2 + [anywhere] * len(others),
        out_specs=[vmem] * 2 + [anywhere] * len(passed),
        out_shape=[jax.ShapeDtypeStruct((rows // 2, width), kept.dtype), jax.ShapeDtypeStruct((rows // 2, got.shape[1]), got.dtype)]
        + [jax.ShapeDtypeStruct(array.shape, array.dtype) for array in passed],
        input_output_aliases={2 + at: 2 + at for at in range(len(passed))},
        compiler_params=params(), cost_estimate=cost(kept.size * 20, kept.size * 12), name="fold",
    )(kept, got, *others)
    return kept, sent, passed


def total_kernel(counts, *refs):
    refs = list(refs)
    out_ref = refs.pop()
    base = 0
    for count in counts:
        kept_ref, got, refs = refs[0], refs[1:count], refs[count:]
        rows, width = kept_ref.shape
        sub = tile_of(width, SUB)
        for at in range(width // sub):
            cols = slice(at * sub, (at + 1) * sub)
            total = kept_ref[:, cols]
            for ref in got:
                total = total + decode(ref[:rows, cols], ref[:rows, width:][:, at:at + 1])
            out_ref[:, base + at * sub:base + (at + 1) * sub] = total.astype(jnp.bfloat16)
        base += width


def totals(parts, later_than):
    rows = parts[0][0].shape[0]
    hidden = sum(part[0].shape[1] for part in parts)
    flat = [array for part in parts for array in part]
    return pl.pallas_call(
        functools.partial(total_kernel, [len(part) for part in parts]),
        in_specs=[pl.BlockSpec(memory_space=pltpu.VMEM)] * len(flat) + [pl.BlockSpec(memory_space=pl.ANY)] * len(later_than),
        out_shape=jax.ShapeDtypeStruct((rows, hidden), jnp.bfloat16),
        compiler_params=params(), cost_estimate=cost(rows * hidden * 40, rows * hidden * 14), name="totals",
    )(*flat, *later_than)


def send(value, axis, flip, size):
    return lax.ppermute(value, axis, [(i, i ^ flip) for i in range(size)])


def stack_kernel(n_values, *refs):
    out_ref = refs[-1]
    rows = refs[0].shape[0]
    for at, ref in enumerate(refs[:n_values]):
        out_ref[at * rows:(at + 1) * rows] = ref[...]


def stacked(values, later_than=()):
    rows, width = values[0].shape
    return pl.pallas_call(
        functools.partial(stack_kernel, len(values)),
        in_specs=[pl.BlockSpec(memory_space=pltpu.VMEM)] * len(values) + [pl.BlockSpec(memory_space=pl.ANY)] * len(later_than),
        out_shape=jax.ShapeDtypeStruct((len(values) * rows, width), values[0].dtype),
        compiler_params=params(SMALL_LIMIT), cost_estimate=cost(0, 4 * len(values) * rows * width), name="stacked",
    )(*values, *later_than)


def same_kernel(*refs):
    pass


def handed_on(values, later_than):
    anywhere = pl.BlockSpec(memory_space=pl.ANY)
    return pl.pallas_call(
        same_kernel,
        in_specs=[anywhere] * (len(values) + len(later_than)), out_specs=[anywhere] * len(values),
        out_shape=[jax.ShapeDtypeStruct(value.shape, value.dtype) for value in values],
        input_output_aliases={at: at for at in range(len(values))},
        compiler_params=params(SMALL_LIMIT), cost_estimate=cost(0, 0), name="handed_on",
    )(*values, *later_than)


def chip_order(n_col):
    return [2, *range(n_col - 2, 2, -2)]


def gather_cotangent(cotangent, n_col):
    pieces = [cotangent] + [send(cotangent, "col", flip, n_col) for flip in chip_order(n_col)]
    stacks = [stacked(pieces[:2])]
    stacks.append(stacked(pieces[2:], stacks))
    return stacks + [send(stack, "col", 1, n_col) for stack in stacks]


def halving_order(size):
    order = [0]
    while len(order) < size:
        order = [2 * o for o in order] + [2 * o + 1 for o in order]
    return order


def part_slices(tiles, shares):
    ends = [tiles * sum(shares[:at]) // 7 for at in range(len(shares) + 1)]
    return [(first, last - first) for first, last in zip(ends, ends[1:])]


def halved(kept, got, passed, later_than, n_row):
    step = 2
    while step < n_row:
        kept, sent, passed = fold(kept, got, passed, later_than)
        got = send(sent, "row", step, n_row)
        step *= 2
    return [kept, got], [sent], passed


def body(n_row, n_col, activations, cotangent, down_weight, row_order):
    rows, hidden = activations.shape
    shard = cotangent.shape[0]
    mine_row, mine_col = lax.axis_index("row"), lax.axis_index("col")
    offsets = halving_order(n_row)
    total = n_row * rows

    flips = [0, *chip_order(n_col)]
    flips += [flip ^ 1 for flip in flips]
    order = row_order.reshape(n_row, rows)
    order = jnp.concatenate([lax.dynamic_index_in_dim(order, mine_row ^ o, 0, keepdims=False) for o in offsets])
    owner = mine_col ^ jnp.asarray(flips, jnp.int32)
    named = (owner[:, None] * shard + jnp.arange(shard, dtype=jnp.int32)[None, :]).reshape(-1)
    pick = (order[:, None] == named[None, :]).astype(jnp.bfloat16)

    tile = tile_of(hidden, 256)
    parts = part_slices(hidden // tile, SHARES)
    pieces = gather_cotangent(cotangent, n_col)
    act_pieces = {o: send(activations, "row", o, n_row) for o in [1, *range(2, n_row, 2)]}
    act_pieces[0] = activations

    kept_rows, sent_rows = [slice(0, total // 2)], [slice(total // 2, total)]
    aligned, [kept], [sent] = partial_sums(
        None, (pick, pieces), down_weight, tile, *parts[0], kept_rows, sent_rows, [], "sums_first")
    got = send(sent, "row", 1, n_row)
    evens = range(2, n_row, 2)
    for o, piece in zip(evens, handed_on([act_pieces[o] for o in evens], [aligned])):
        act_pieces[o], act_pieces[o + 1] = piece, send(piece, "row", 1, n_row)

    _, [kept_b], [sent_b] = partial_sums(
        aligned, None, down_weight, tile, *parts[1], kept_rows, sent_rows, [act_pieces[1]], "sums_second")
    done_a, crossed, [sent_b] = halved(kept, got, [sent_b], [], n_row)
    got_b = send(sent_b, "row", 1, n_row)

    spans = [slice(at * rows, (at + 1) * rows) for at in range(n_row)]
    _, [kept_c], sent_c = partial_sums(
        aligned, None, down_weight, tile, *parts[2], spans[:1], spans[1:], crossed, "sums_last")
    done_c = [kept_c] + [send(message, "row", o, n_row) for message, o in zip(sent_c, offsets[1:])]

    grad_pieces = [act_pieces[o] for o in offsets]
    grad_tile = tile_of(hidden, 256)
    (first_a, count_a), (first_b, count_b) = part_slices(hidden // grad_tile, (3, 4))
    grad = weight_grads(aligned, grad_pieces, grad_tile, first_a, count_a, None, sent_c[:1])
    done_b, crossed_b, _ = halved(kept_b, got_b, [], [grad], n_row)
    weight_grad = weight_grads(aligned, grad_pieces, grad_tile, first_b, count_b, grad, crossed_b)
    return weight_grad, totals([done_a, done_b, done_c], [weight_grad])


def solution(mesh):
    in_specs = (P("row", "col"), P("col", "row"), P("col", "row"), P())
    out_specs = (P("col", "row"), P("row", "col"))
    fn = functools.partial(body, mesh.shape["row"], mesh.shape["col"])
    return jax.shard_map(fn, mesh=mesh, in_specs=in_specs, out_specs=out_specs, check_vma=False)
```

```python
import functools

import jax
import jax.numpy as jnp
from jax import lax
from jax.experimental import pallas as pl
from jax.experimental.pallas import tpu as pltpu
from jax.sharding import PartitionSpec as P

LANES = 128
LEVEL_ROWS = 16
STEPS_PER_OCTAVE = 128.0
TOP = 32766.0
LEAST = 2.0 ** -120
VMEM_LIMIT = 48 * 1024 * 1024
SMALL_LIMIT = 8 * 1024 * 1024
SLOTS = 4
SHARES = (2, 3, 2)
SUB = 256


def tile_of(size, largest):
    tile = largest
    while size % tile:
        tile //= 2
    return tile


def dot(left, right, dims):
    return lax.dot_general(left, right, (dims, ((), ())), preferred_element_type=jnp.float32)


def encode(values):
    most = jnp.maximum(jnp.max(jnp.abs(values), axis=1, keepdims=True), LEAST)
    level = jnp.ceil(jnp.log2(most) * STEPS_PER_OCTAVE) + 1.0
    codes = jnp.round(values * jnp.exp2(level * (-1.0 / STEPS_PER_OCTAVE)) * TOP)
    return codes.astype(jnp.int32).astype(jnp.int16), level


def decode(codes, levels):
    return codes.astype(jnp.int32).astype(jnp.float32) * (jnp.exp2(levels * (1.0 / STEPS_PER_OCTAVE)) * (1.0 / TOP))


def message_shape(rows, width):
    return (width // LANES * rows + pl.cdiv(rows, LANES) * LEVEL_ROWS, LANES)


def turned_levels(levels):
    blocks = []
    for at in range(0, levels.shape[0], LANES):
        block = levels[at:at + LANES]
        if block.shape[0] < LANES:
            block = jnp.concatenate([block, jnp.zeros((LANES - block.shape[0], LANES), jnp.float32)], axis=0)
        blocks.append(block.T[:LEVEL_ROWS])
    return jnp.concatenate(blocks, axis=0).astype(jnp.int32).astype(jnp.int16)


def levels_of(message_ref, rows, width):
    turned = message_ref[width // LANES * rows:].astype(jnp.int32).astype(jnp.float32)
    blocks = []
    for at in range(0, turned.shape[0], LEVEL_ROWS):
        block = turned[at:at + LEVEL_ROWS]
        blocks.append(jnp.concatenate([block, jnp.zeros((LANES - LEVEL_ROWS, LANES), jnp.float32)], axis=0).T)
    return jnp.concatenate(blocks, axis=0)[:rows]


def codes_of(message_ref, rows, first, count):
    return jnp.concatenate([message_ref[at * rows:(at + 1) * rows] for at in range(first, first + count)], axis=1)


def params(limit=VMEM_LIMIT):
    return pltpu.CompilerParams(vmem_limit_bytes=limit)


def cost(flops, moved):
    return pl.CostEstimate(flops=flops, bytes_accessed=moved, transcendentals=0)


def align_rows(pick_ref, pieces, aligned_ref):
    depth = aligned_ref.shape[1]
    chunk = tile_of(depth, 512)
    for at in range(0, depth, chunk):
        cols = slice(at, at + chunk)
        gathered = jnp.concatenate([piece[:, cols] for piece in pieces], axis=0)
        aligned_ref[:, cols] = dot(pick_ref[...], gathered, ((1,), (0,))).astype(jnp.bfloat16)


def sums_kernel(n_pieces, n_blocks, n_later, coded, kept_rows, sent_rows, tile, *refs):
    refs = list(refs)
    if n_pieces:
        pick_ref = refs.pop(0)
        pieces = [refs.pop(0) for _ in range(n_pieces)]
    else:
        aligned_ref = refs.pop(0)
    weights = [refs.pop(0) for _ in range(n_blocks)]
    del refs[:n_later]
    if n_pieces:
        aligned_ref = refs.pop(0)
    kept = [refs.pop(0) for _ in kept_rows]
    sent = [refs.pop(0) for _ in sent_rows]
    levels_ref, = refs
    step = pl.program_id(0)
    per_tile = tile // LANES

    @pl.when(step == 0)
    def _():
        if n_pieces:
            align_rows(pick_ref, pieces, aligned_ref)
        levels_ref[...] = jnp.zeros_like(levels_ref)

    lane = lax.broadcasted_iota(jnp.int32, levels_ref.shape, 1)
    levels = levels_ref[...]
    for part in range(n_blocks):
        at = step * n_blocks + part
        values = dot(aligned_ref[...], weights[part][...], ((1,), (1,)))
        for ref, rows in zip(kept, kept_rows):
            ref[:, part * tile:(part + 1) * tile] = values[rows]
        codes, level = encode(values[coded:])
        levels = jnp.where(lane == at, level, levels)
        for ref, rows in zip(sent, sent_rows):
            height = rows.stop - rows.start
            for col in range(per_tile):
                here = pl.ds(pl.multiple_of((at * per_tile + col) * height, height), height)
                ref[here] = codes[rows.start - coded:rows.stop - coded, col * LANES:(col + 1) * LANES]
    levels_ref[...] = levels

    @pl.when(step == pl.num_programs(0) - 1)
    def _():
        for ref, rows in zip(sent, sent_rows):
            height = rows.stop - rows.start
            turned = turned_levels(levels[rows.start - coded:rows.stop - coded])
            ref[ref.shape[0] - turned.shape[0]:] = turned


def partial_sums(aligned, align, weight, tile, first, count, kept_rows, sent_rows, later_than, name):
    depth = weight.shape[1]
    width = count * tile
    whole = lambda i: (0, 0)
    operands = [align[0], *align[1]] if aligned is None else [aligned]
    total = operands[0].shape[0]
    coded = min(rows.start for rows in sent_rows)
    n_blocks = 2 if count % 2 == 0 and first % 2 == 0 else 1
    block_at = lambda part: (lambda i: (i * n_blocks + first + part, 0))
    heights = lambda spans: [span.stop - span.start for span in spans]
    in_specs = [pl.BlockSpec(operand.shape, whole) for operand in operands]
    in_specs += [pl.BlockSpec((tile, depth), block_at(part)) for part in range(n_blocks)]
    in_specs += [pl.BlockSpec(memory_space=pl.ANY)] * len(later_than)
    out_specs = [pl.BlockSpec((height, n_blocks * tile), lambda i: (0, i)) for height in heights(kept_rows)]
    out_specs += [pl.BlockSpec(message_shape(height, width), whole) for height in heights(sent_rows)]
    out_shape = [jax.ShapeDtypeStruct((height, width), jnp.float32) for height in heights(kept_rows)]
    out_shape += [jax.ShapeDtypeStruct(message_shape(height, width), jnp.int16) for height in heights(sent_rows)]
    if aligned is None:
        out_specs.insert(0, pl.BlockSpec((total, depth), whole))
        out_shape.insert(0, jax.ShapeDtypeStruct((total, depth), jnp.bfloat16))
    outs = pl.pallas_call(
        functools.partial(
            sums_kernel, 0 if aligned is not None else len(align[1]), n_blocks, len(later_than), coded, kept_rows, sent_rows, tile),
        grid=(count // n_blocks,), in_specs=in_specs, out_specs=out_specs, out_shape=out_shape,
        scratch_shapes=[pltpu.VMEM((total - coded, LANES), jnp.float32)],
        compiler_params=params(),
        cost_estimate=cost(2 * total * width * depth, 2 * width * depth), name=name,
    )(*operands, *[weight] * n_blocks, *later_than)
    if aligned is None:
        aligned, *outs = outs
    return aligned, outs[:len(kept_rows)], outs[len(kept_rows):]


def weight_kernel(n_pieces, first, n_later, tile, aligned_ref, *refs):
    pieces = [ref[...] for ref in refs[:n_pieces]]
    out_ref, held_ref, left_sem = refs[n_pieces + n_later:]
    step = pl.program_id(0)
    last = pl.num_programs(0) - 1
    slots = held_ref.shape[0]

    def leave(at):
        rows = pl.ds(pl.multiple_of((first + at) * tile, tile), tile)
        slot = lax.rem(at, slots)
        return pltpu.make_async_copy(held_ref.at[slot], out_ref.at[rows], left_sem.at[slot])

    @pl.when(step >= slots)
    def _():
        leave(step - slots).wait()

    left = jnp.concatenate(pieces, axis=0)
    depth = aligned_ref.shape[1]
    chunk = tile_of(depth, 1024)
    block = held_ref.at[lax.rem(step, slots)]
    for at in range(0, depth, chunk):
        cols = slice(at, at + chunk)
        block[:, cols] = dot(left, aligned_ref[:, cols], ((0,), (0,))).astype(jnp.bfloat16)
    leave(step).start()

    @pl.when(step == last)
    def _():
        for back in range(slots - 1, -1, -1):
            @pl.when(last >= back)
            def _():
                leave(last - back).wait()


def weight_grads(aligned, pieces, tile, first, count, filled, later_than):
    total, depth = aligned.shape
    rows, hidden = pieces[0].shape
    later = ([] if filled is None else [filled]) + list(later_than)
    return pl.pallas_call(
        functools.partial(weight_kernel, len(pieces), first, len(later), tile),
        grid=(count,),
        in_specs=[pl.BlockSpec((total, depth), lambda i: (0, 0))]
        + [pl.BlockSpec((rows, tile), lambda i: (0, i + first))] * len(pieces)
        + [pl.BlockSpec(memory_space=pl.ANY)] * len(later),
        out_specs=pl.BlockSpec(memory_space=pl.ANY),
        out_shape=jax.ShapeDtypeStruct((hidden, depth), jnp.bfloat16),
        scratch_shapes=[pltpu.VMEM((SLOTS, tile, depth), jnp.bfloat16), pltpu.SemaphoreType.DMA((SLOTS,))],
        input_output_aliases={} if filled is None else {1 + len(pieces): 0},
        compiler_params=params(), cost_estimate=cost(2 * total * count * tile * depth, 2 * count * tile * depth),
        name="weight_grads",
    )(aligned, *pieces, *later)


def fold_kernel(n_others, kept_ref, got_ref, *refs):
    next_ref, sent_ref = refs[n_others:n_others + 2]
    rows, width = kept_ref.shape
    half = next_ref.shape[0]
    sub = tile_of(width, SUB)
    per_tile = sub // LANES
    lane = lax.broadcasted_iota(jnp.int32, (half, LANES), 1)
    levels = jnp.zeros(lane.shape, jnp.float32)
    got_levels = levels_of(got_ref, rows, width)
    for at in range(width // sub):
        cols = slice(at * sub, (at + 1) * sub)
        total = kept_ref[:, cols] + decode(codes_of(got_ref, rows, at * per_tile, per_tile), got_levels[:, at:at + 1])
        next_ref[:, cols] = total[:half]
        codes, level = encode(total[half:])
        for col in range(per_tile):
            first = (at * per_tile + col) * half
            sent_ref[first:first + half] = codes[:, col * LANES:(col + 1) * LANES]
        levels = jnp.where(lane == at, level, levels)
    sent_ref[width // LANES * half:] = turned_levels(levels)


def fold(kept, got, passed, later_than):
    others = [*passed, *later_than]
    vmem, anywhere = pl.BlockSpec(memory_space=pltpu.VMEM), pl.BlockSpec(memory_space=pl.ANY)
    rows, width = kept.shape
    kept, sent, *passed = pl.pallas_call(
        functools.partial(fold_kernel, len(others)),
        in_specs=[vmem] * 2 + [anywhere] * len(others),
        out_specs=[vmem] * 2 + [anywhere] * len(passed),
        out_shape=[jax.ShapeDtypeStruct((rows // 2, width), kept.dtype), jax.ShapeDtypeStruct(message_shape(rows // 2, width), got.dtype)]
        + [jax.ShapeDtypeStruct(array.shape, array.dtype) for array in passed],
        input_output_aliases={2 + at: 2 + at for at in range(len(passed))},
        compiler_params=params(), cost_estimate=cost(kept.size * 20, kept.size * 12), name="fold",
    )(kept, got, *others)
    return kept, sent, passed


def total_kernel(counts, *refs):
    refs = list(refs)
    out_ref = refs.pop()
    base = 0
    for count in counts:
        kept_ref, got, refs = refs[0], refs[1:count], refs[count:]
        rows, width = kept_ref.shape
        sub = tile_of(width, SUB)
        per_tile = sub // LANES
        levels = [levels_of(ref, rows, width) for ref in got]
        for at in range(width // sub):
            cols = slice(at * sub, (at + 1) * sub)
            total = kept_ref[:, cols]
            for ref, level in zip(got, levels):
                total = total + decode(codes_of(ref, rows, at * per_tile, per_tile), level[:, at:at + 1])
            out_ref[:, base + at * sub:base + (at + 1) * sub] = total.astype(jnp.bfloat16)
        base += width


def totals(parts, later_than):
    rows = parts[0][0].shape[0]
    hidden = sum(part[0].shape[1] for part in parts)
    flat = [array for part in parts for array in part]
    return pl.pallas_call(
        functools.partial(total_kernel, [len(part) for part in parts]),
        in_specs=[pl.BlockSpec(memory_space=pltpu.VMEM)] * len(flat) + [pl.BlockSpec(memory_space=pl.ANY)] * len(later_than),
        out_shape=jax.ShapeDtypeStruct((rows, hidden), jnp.bfloat16),
        compiler_params=params(), cost_estimate=cost(rows * hidden * 40, rows * hidden * 14), name="totals",
    )(*flat, *later_than)


def send(value, axis, flip, size):
    return lax.ppermute(value, axis, [(i, i ^ flip) for i in range(size)])


def stack_kernel(n_values, *refs):
    out_ref = refs[-1]
    rows = refs[0].shape[0]
    for at, ref in enumerate(refs[:n_values]):
        out_ref[at * rows:(at + 1) * rows] = ref[...]


def stacked(values, later_than=()):
    rows, width = values[0].shape
    return pl.pallas_call(
        functools.partial(stack_kernel, len(values)),
        in_specs=[pl.BlockSpec(memory_space=pltpu.VMEM)] * len(values) + [pl.BlockSpec(memory_space=pl.ANY)] * len(later_than),
        out_shape=jax.ShapeDtypeStruct((len(values) * rows, width), values[0].dtype),
        compiler_params=params(SMALL_LIMIT), cost_estimate=cost(0, 4 * len(values) * rows * width), name="stacked",
    )(*values, *later_than)


def same_kernel(*refs):
    pass


def handed_on(values, later_than):
    anywhere = pl.BlockSpec(memory_space=pl.ANY)
    return pl.pallas_call(
        same_kernel,
        in_specs=[anywhere] * (len(values) + len(later_than)), out_specs=[anywhere] * len(values),
        out_shape=[jax.ShapeDtypeStruct(value.shape, value.dtype) for value in values],
        input_output_aliases={at: at for at in range(len(values))},
        compiler_params=params(SMALL_LIMIT), cost_estimate=cost(0, 0), name="handed_on",
    )(*values, *later_than)


def chip_order(n_col):
    return [2, *range(n_col - 2, 2, -2)]


def gather_cotangent(cotangent, n_col):
    pieces = [cotangent] + [send(cotangent, "col", flip, n_col) for flip in chip_order(n_col)]
    stacks = [stacked(pieces[:2])]
    stacks.append(stacked(pieces[2:], stacks))
    return stacks + [send(stack, "col", 1, n_col) for stack in stacks]


def halving_order(size):
    order = [0]
    while len(order) < size:
        order = [2 * o for o in order] + [2 * o + 1 for o in order]
    return order


def part_slices(tiles, shares):
    ends = [tiles * sum(shares[:at]) // 7 for at in range(len(shares) + 1)]
    return [(first, last - first) for first, last in zip(ends, ends[1:])]


def halved(kept, got, passed, later_than, n_row):
    step = 2
    while step < n_row:
        kept, sent, passed = fold(kept, got, passed, later_than)
        got = send(sent, "row", step, n_row)
        step *= 2
    return [kept, got], [sent], passed


def body(n_row, n_col, activations, cotangent, down_weight, row_order):
    rows, hidden = activations.shape
    shard = cotangent.shape[0]
    mine_row, mine_col = lax.axis_index("row"), lax.axis_index("col")
    offsets = halving_order(n_row)
    total = n_row * rows

    flips = [0, *chip_order(n_col)]
    flips += [flip ^ 1 for flip in flips]
    order = row_order.reshape(n_row, rows)
    order = jnp.concatenate([lax.dynamic_index_in_dim(order, mine_row ^ o, 0, keepdims=False) for o in offsets])
    owner = mine_col ^ jnp.asarray(flips, jnp.int32)
    named = (owner[:, None] * shard + jnp.arange(shard, dtype=jnp.int32)[None, :]).reshape(-1)
    pick = (order[:, None] == named[None, :]).astype(jnp.bfloat16)

    tile = tile_of(hidden, 256)
    parts = part_slices(hidden // tile, SHARES)
    pieces = gather_cotangent(cotangent, n_col)
    act_pieces = {o: send(activations, "row", o, n_row) for o in [1, *range(2, n_row, 2)]}
    act_pieces[0] = activations

    kept_rows, sent_rows = [slice(0, total // 2)], [slice(total // 2, total)]
    aligned, [kept], [sent] = partial_sums(
        None, (pick, pieces), down_weight, tile, *parts[0], kept_rows, sent_rows, [], "sums_first")
    got = send(sent, "row", 1, n_row)
    evens = range(2, n_row, 2)
    for o, piece in zip(evens, handed_on([act_pieces[o] for o in evens], [aligned])):
        act_pieces[o], act_pieces[o + 1] = piece, send(piece, "row", 1, n_row)

    _, [kept_b], [sent_b] = partial_sums(
        aligned, None, down_weight, tile, *parts[1], kept_rows, sent_rows, [act_pieces[1]], "sums_second")
    done_a, crossed, [sent_b] = halved(kept, got, [sent_b], [], n_row)
    got_b = send(sent_b, "row", 1, n_row)

    spans = [slice(at * rows, (at + 1) * rows) for at in range(n_row)]
    _, [kept_c], sent_c = partial_sums(
        aligned, None, down_weight, tile, *parts[2], spans[:1], spans[1:], crossed, "sums_last")
    done_c = [kept_c] + [send(message, "row", o, n_row) for message, o in zip(sent_c, offsets[1:])]

    grad_pieces = [act_pieces[o] for o in offsets]
    grad_tile = tile_of(hidden, 256)
    (first_a, count_a), (first_b, count_b) = part_slices(hidden // grad_tile, (3, 4))
    grad = weight_grads(aligned, grad_pieces, grad_tile, first_a, count_a, None, sent_c[:1])
    done_b, crossed_b, _ = halved(kept_b, got_b, [], [grad], n_row)
    weight_grad = weight_grads(aligned, grad_pieces, grad_tile, first_b, count_b, grad, crossed_b)
    return weight_grad, totals([done_a, done_b, done_c], [weight_grad])


def solution(mesh):
    in_specs = (P("row", "col"), P("col", "row"), P("col", "row"), P())
    out_specs = (P("col", "row"), P("row", "col"))
    fn = functools.partial(body, mesh.shape["row"], mesh.shape["col"])
    return jax.shard_map(fn, mesh=mesh, in_specs=in_specs, out_specs=out_specs, check_vma=False)
```

```python
import functools

import jax
import jax.numpy as jnp
from jax import lax
from jax.experimental import pallas as pl
from jax.experimental.pallas import tpu as pltpu
from jax.sharding import PartitionSpec as P

LANES = 128
LEVEL_ROWS = 16
STEPS_PER_OCTAVE = 128.0
TOP = 32766.0
LEAST = 2.0 ** -120
VMEM_LIMIT = 48 * 1024 * 1024
SMALL_LIMIT = 8 * 1024 * 1024
SLOTS = 4
SHARES = (2, 3, 2)
SUB = 256


def tile_of(size, largest):
    tile = largest
    while size % tile:
        tile //= 2
    return tile


def dot(left, right, dims):
    return lax.dot_general(left, right, (dims, ((), ())), preferred_element_type=jnp.float32)


def encode(values):
    most = jnp.maximum(jnp.max(jnp.abs(values), axis=1, keepdims=True), LEAST)
    level = jnp.ceil(jnp.log2(most) * STEPS_PER_OCTAVE) + 1.0
    codes = jnp.round(values * jnp.exp2(level * (-1.0 / STEPS_PER_OCTAVE)) * TOP)
    return codes.astype(jnp.int32).astype(jnp.int16), level


def decode(codes, levels):
    return codes.astype(jnp.int32).astype(jnp.float32) * (jnp.exp2(levels * (1.0 / STEPS_PER_OCTAVE)) * (1.0 / TOP))


def message_shape(rows, width):
    return (width // LANES * rows + pl.cdiv(rows, LANES) * LEVEL_ROWS, LANES)


def turned_levels(levels):
    blocks = []
    for at in range(0, levels.shape[0], LANES):
        block = levels[at:at + LANES]
        if block.shape[0] < LANES:
            block = jnp.concatenate([block, jnp.zeros((LANES - block.shape[0], LANES), jnp.float32)], axis=0)
        blocks.append(block.T[:LEVEL_ROWS])
    return jnp.concatenate(blocks, axis=0).astype(jnp.int32).astype(jnp.int16)


def levels_of(message_ref, rows, width):
    turned = message_ref[width // LANES * rows:].astype(jnp.int32).astype(jnp.float32)
    blocks = []
    for at in range(0, turned.shape[0], LEVEL_ROWS):
        block = turned[at:at + LEVEL_ROWS]
        blocks.append(jnp.concatenate([block, jnp.zeros((LANES - LEVEL_ROWS, LANES), jnp.float32)], axis=0).T)
    return jnp.concatenate(blocks, axis=0)[:rows]


def codes_of(message_ref, rows, first, count):
    return jnp.concatenate([message_ref[at * rows:(at + 1) * rows] for at in range(first, first + count)], axis=1)


def params(limit=VMEM_LIMIT):
    return pltpu.CompilerParams(vmem_limit_bytes=limit)


def cost(flops, moved):
    return pl.CostEstimate(flops=flops, bytes_accessed=moved, transcendentals=0)


def align_rows(pick_ref, pieces, aligned_ref):
    depth = aligned_ref.shape[1]
    chunk = tile_of(depth, 512)
    for at in range(0, depth, chunk):
        cols = slice(at, at + chunk)
        gathered = jnp.concatenate([piece[:, cols] for piece in pieces], axis=0)
        aligned_ref[:, cols] = dot(pick_ref[...], gathered, ((1,), (0,))).astype(jnp.bfloat16)


def sums_kernel(n_pieces, n_blocks, n_later, coded, kept_rows, sent_rows, tile, *refs):
    refs = list(refs)
    if n_pieces:
        pick_ref = refs.pop(0)
        pieces = [refs.pop(0) for _ in range(n_pieces)]
    else:
        aligned_ref = refs.pop(0)
    weights = [refs.pop(0) for _ in range(n_blocks)]
    del refs[:n_later]
    if n_pieces:
        aligned_ref = refs.pop(0)
    kept = [refs.pop(0) for _ in kept_rows]
    sent = [refs.pop(0) for _ in sent_rows]
    levels_ref, = refs
    step = pl.program_id(0)
    per_tile = tile // LANES

    @pl.when(step == 0)
    def _():
        if n_pieces:
            align_rows(pick_ref, pieces, aligned_ref)
        levels_ref[...] = jnp.zeros_like(levels_ref)

    lane = lax.broadcasted_iota(jnp.int32, levels_ref.shape, 1)
    levels = levels_ref[...]
    for part in range(n_blocks):
        at = step * n_blocks + part
        values = dot(aligned_ref[...], weights[part][...], ((1,), (1,)))
        for ref, rows in zip(kept, kept_rows):
            ref[:, part * tile:(part + 1) * tile] = values[rows]
        codes, level = encode(values[coded:])
        levels = jnp.where(lane == at, level, levels)
        for ref, rows in zip(sent, sent_rows):
            height = rows.stop - rows.start
            for col in range(per_tile):
                here = pl.ds(pl.multiple_of((at * per_tile + col) * height, height), height)
                ref[here] = codes[rows.start - coded:rows.stop - coded, col * LANES:(col + 1) * LANES]
    levels_ref[...] = levels

    @pl.when(step == pl.num_programs(0) - 1)
    def _():
        for ref, rows in zip(sent, sent_rows):
            height = rows.stop - rows.start
            turned = turned_levels(levels[rows.start - coded:rows.stop - coded])
            ref[ref.shape[0] - turned.shape[0]:] = turned


def partial_sums(aligned, align, weight, tile, first, count, kept_rows, sent_rows, later_than, name):
    depth = weight.shape[1]
    width = count * tile
    whole = lambda i: (0, 0)
    operands = [align[0], *align[1]] if aligned is None else [aligned]
    total = operands[0].shape[0]
    coded = min(rows.start for rows in sent_rows)
    n_blocks = 2 if count % 2 == 0 and first % 2 == 0 else 1
    block_at = lambda part: (lambda i: (i * n_blocks + first + part, 0))
    heights = lambda spans: [span.stop - span.start for span in spans]
    in_specs = [pl.BlockSpec(operand.shape, whole) for operand in operands]
    in_specs += [pl.BlockSpec((tile, depth), block_at(part)) for part in range(n_blocks)]
    in_specs += [pl.BlockSpec(memory_space=pl.ANY)] * len(later_than)
    out_specs = [pl.BlockSpec((height, n_blocks * tile), lambda i: (0, i)) for height in heights(kept_rows)]
    out_specs += [pl.BlockSpec(message_shape(height, width), whole) for height in heights(sent_rows)]
    out_shape = [jax.ShapeDtypeStruct((height, width), jnp.float32) for height in heights(kept_rows)]
    out_shape += [jax.ShapeDtypeStruct(message_shape(height, width), jnp.int16) for height in heights(sent_rows)]
    if aligned is None:
        out_specs.insert(0, pl.BlockSpec((total, depth), whole))
        out_shape.insert(0, jax.ShapeDtypeStruct((total, depth), jnp.bfloat16))
    outs = pl.pallas_call(
        functools.partial(
            sums_kernel, 0 if aligned is not None else len(align[1]), n_blocks, len(later_than), coded, kept_rows, sent_rows, tile),
        grid=(count // n_blocks,), in_specs=in_specs, out_specs=out_specs, out_shape=out_shape,
        scratch_shapes=[pltpu.VMEM((total - coded, LANES), jnp.float32)],
        compiler_params=params(),
        cost_estimate=cost(2 * total * width * depth, 2 * width * depth), name=name,
    )(*operands, *[weight] * n_blocks, *later_than)
    if aligned is None:
        aligned, *outs = outs
    return aligned, outs[:len(kept_rows)], outs[len(kept_rows):]


def weight_kernel(n_pieces, first, n_later, tile, aligned_ref, *refs):
    pieces = [ref[...] for ref in refs[:n_pieces]]
    out_ref, held_ref, left_sem = refs[n_pieces + n_later:]
    step = pl.program_id(0)
    last = pl.num_programs(0) - 1
    slots = held_ref.shape[0]

    def leave(at):
        rows = pl.ds(pl.multiple_of((first + at) * tile, tile), tile)
        slot = lax.rem(at, slots)
        return pltpu.make_async_copy(held_ref.at[slot], out_ref.at[rows], left_sem.at[slot])

    @pl.when(step >= slots)
    def _():
        leave(step - slots).wait()

    left = jnp.concatenate(pieces, axis=0)
    depth = aligned_ref.shape[1]
    chunk = tile_of(depth, 1024)
    block = held_ref.at[lax.rem(step, slots)]
    for at in range(0, depth, chunk):
        cols = slice(at, at + chunk)
        block[:, cols] = dot(left, aligned_ref[:, cols], ((0,), (0,))).astype(jnp.bfloat16)
    leave(step).start()

    @pl.when(step == last)
    def _():
        for back in range(slots - 1, -1, -1):
            @pl.when(last >= back)
            def _():
                leave(last - back).wait()


def weight_grads(aligned, pieces, tile, first, count, filled, later_than):
    total, depth = aligned.shape
    rows, hidden = pieces[0].shape
    later = ([] if filled is None else [filled]) + list(later_than)
    return pl.pallas_call(
        functools.partial(weight_kernel, len(pieces), first, len(later), tile),
        grid=(count,),
        in_specs=[pl.BlockSpec((total, depth), lambda i: (0, 0))]
        + [pl.BlockSpec((rows, tile), lambda i: (0, i + first))] * len(pieces)
        + [pl.BlockSpec(memory_space=pl.ANY)] * len(later),
        out_specs=pl.BlockSpec(memory_space=pl.ANY),
        out_shape=jax.ShapeDtypeStruct((hidden, depth), jnp.bfloat16),
        scratch_shapes=[pltpu.VMEM((SLOTS, tile, depth), jnp.bfloat16), pltpu.SemaphoreType.DMA((SLOTS,))],
        input_output_aliases={} if filled is None else {1 + len(pieces): 0},
        compiler_params=params(), cost_estimate=cost(2 * total * count * tile * depth, 2 * count * tile * depth),
        name="weight_grads",
    )(aligned, *pieces, *later)


def fold_kernel(n_others, kept_ref, got_ref, *refs):
    next_ref, sent_ref = refs[n_others:n_others + 2]
    rows, width = kept_ref.shape
    half = next_ref.shape[0]
    sub = tile_of(width, SUB)
    per_tile = sub // LANES
    lane = lax.broadcasted_iota(jnp.int32, (half, LANES), 1)
    levels = jnp.zeros(lane.shape, jnp.float32)
    got_levels = levels_of(got_ref, rows, width)
    for at in range(width // sub):
        cols = slice(at * sub, (at + 1) * sub)
        total = kept_ref[:, cols] + decode(codes_of(got_ref, rows, at * per_tile, per_tile), got_levels[:, at:at + 1])
        next_ref[:, cols] = total[:half]
        codes, level = encode(total[half:])
        for col in range(per_tile):
            first = (at * per_tile + col) * half
            sent_ref[first:first + half] = codes[:, col * LANES:(col + 1) * LANES]
        levels = jnp.where(lane == at, level, levels)
    sent_ref[width // LANES * half:] = turned_levels(levels)


def fold(kept, got, passed, later_than):
    others = [*passed, *later_than]
    vmem, anywhere = pl.BlockSpec(memory_space=pltpu.VMEM), pl.BlockSpec(memory_space=pl.ANY)
    rows, width = kept.shape
    kept, sent, *passed = pl.pallas_call(
        functools.partial(fold_kernel, len(others)),
        in_specs=[vmem] * 2 + [anywhere] * len(others),
        out_specs=[vmem] * 2 + [anywhere] * len(passed),
        out_shape=[jax.ShapeDtypeStruct((rows // 2, width), kept.dtype), jax.ShapeDtypeStruct(message_shape(rows // 2, width), got.dtype)]
        + [jax.ShapeDtypeStruct(array.shape, array.dtype) for array in passed],
        input_output_aliases={2 + at: 2 + at for at in range(len(passed))},
        compiler_params=params(), cost_estimate=cost(kept.size * 20, kept.size * 12), name="fold",
    )(kept, got, *others)
    return kept, sent, passed


def total_kernel(counts, *refs):
    refs = list(refs)
    out_ref = refs.pop()
    base = 0
    for count in counts:
        kept_ref, got, refs = refs[0], refs[1:count], refs[count:]
        rows, width = kept_ref.shape
        sub = tile_of(width, SUB)
        per_tile = sub // LANES
        levels = [levels_of(ref, rows, width) for ref in got]
        for at in range(width // sub):
            cols = slice(at * sub, (at + 1) * sub)
            total = kept_ref[:, cols]
            for ref, level in zip(got, levels):
                total = total + decode(codes_of(ref, rows, at * per_tile, per_tile), level[:, at:at + 1])
            out_ref[:, base + at * sub:base + (at + 1) * sub] = total.astype(jnp.bfloat16)
        base += width


def totals(parts, later_than):
    rows = parts[0][0].shape[0]
    hidden = sum(part[0].shape[1] for part in parts)
    flat = [array for part in parts for array in part]
    return pl.pallas_call(
        functools.partial(total_kernel, [len(part) for part in parts]),
        in_specs=[pl.BlockSpec(memory_space=pltpu.VMEM)] * len(flat) + [pl.BlockSpec(memory_space=pl.ANY)] * len(later_than),
        out_shape=jax.ShapeDtypeStruct((rows, hidden), jnp.bfloat16),
        compiler_params=params(), cost_estimate=cost(rows * hidden * 40, rows * hidden * 14), name="totals",
    )(*flat, *later_than)


def send(value, axis, flip, size):
    return lax.ppermute(value, axis, [(i, i ^ flip) for i in range(size)])


def stack_kernel(n_values, *refs):
    out_ref = refs[-1]
    rows = refs[0].shape[0]
    for at, ref in enumerate(refs[:n_values]):
        out_ref[at * rows:(at + 1) * rows] = ref[...]


def stacked(values, later_than=()):
    rows, width = values[0].shape
    return pl.pallas_call(
        functools.partial(stack_kernel, len(values)),
        in_specs=[pl.BlockSpec(memory_space=pltpu.VMEM)] * len(values) + [pl.BlockSpec(memory_space=pl.ANY)] * len(later_than),
        out_shape=jax.ShapeDtypeStruct((len(values) * rows, width), values[0].dtype),
        compiler_params=params(SMALL_LIMIT), cost_estimate=cost(0, 4 * len(values) * rows * width), name="stacked",
    )(*values, *later_than)


def same_kernel(*refs):
    pass


def handed_on(values, later_than):
    anywhere = pl.BlockSpec(memory_space=pl.ANY)
    return pl.pallas_call(
        same_kernel,
        in_specs=[anywhere] * (len(values) + len(later_than)), out_specs=[anywhere] * len(values),
        out_shape=[jax.ShapeDtypeStruct(value.shape, value.dtype) for value in values],
        input_output_aliases={at: at for at in range(len(values))},
        compiler_params=params(SMALL_LIMIT), cost_estimate=cost(0, 0), name="handed_on",
    )(*values, *later_than)


def chip_order(n_col):
    return [2, *range(n_col - 2, 2, -2)]


def gather_cotangent(cotangent, n_col):
    pieces = [cotangent] + [send(cotangent, "col", flip, n_col) for flip in chip_order(n_col)]
    stacks = [stacked(pieces[:2])]
    stacks.append(stacked(pieces[2:], stacks))
    return stacks + [send(stack, "col", 1, n_col) for stack in stacks]


def halving_order(size):
    order = [0]
    while len(order) < size:
        order = [2 * o for o in order] + [2 * o + 1 for o in order]
    return order


def part_slices(tiles, shares):
    ends = [tiles * sum(shares[:at]) // 7 for at in range(len(shares) + 1)]
    return [(first, last - first) for first, last in zip(ends, ends[1:])]


def halved(kept, got, passed, later_than, n_row):
    step = 2
    while step < n_row:
        kept, sent, passed = fold(kept, got, passed, later_than)
        got = send(sent, "row", step, n_row)
        step *= 2
    return [kept, got], [sent], passed


def body(n_row, n_col, activations, cotangent, down_weight, row_order):
    rows, hidden = activations.shape
    shard = cotangent.shape[0]
    mine_row, mine_col = lax.axis_index("row"), lax.axis_index("col")
    offsets = halving_order(n_row)
    total = n_row * rows

    flips = [0, *chip_order(n_col)]
    flips += [flip ^ 1 for flip in flips]
    order = row_order.reshape(n_row, rows)
    order = jnp.concatenate([lax.dynamic_index_in_dim(order, mine_row ^ o, 0, keepdims=False) for o in offsets])
    owner = mine_col ^ jnp.asarray(flips, jnp.int32)
    named = (owner[:, None] * shard + jnp.arange(shard, dtype=jnp.int32)[None, :]).reshape(-1)
    pick = (order[:, None] == named[None, :]).astype(jnp.bfloat16)

    tile = tile_of(hidden, 256)
    parts = part_slices(hidden // tile, SHARES)
    pieces = gather_cotangent(cotangent, n_col)
    act_pieces = {o: send(activations, "row", o, n_row) for o in [1, *range(2, n_row, 2)]}
    act_pieces[0] = activations

    kept_rows, sent_rows = [slice(0, total // 2)], [slice(total // 2, total)]
    aligned, [kept], [sent] = partial_sums(
        None, (pick, pieces), down_weight, tile, *parts[0], kept_rows, sent_rows, [], "sums_first")
    got = send(sent, "row", 1, n_row)
    evens = range(2, n_row, 2)
    for o, piece in zip(evens, handed_on([act_pieces[o] for o in evens], [aligned])):
        act_pieces[o], act_pieces[o + 1] = piece, send(piece, "row", 1, n_row)

    _, [kept_b], [sent_b] = partial_sums(
        aligned, None, down_weight, tile, *parts[1], kept_rows, sent_rows, [act_pieces[1]], "sums_second")
    done_a, crossed, [sent_b] = halved(kept, got, [sent_b], [], n_row)
    got_b = send(sent_b, "row", 1, n_row)

    spans = [slice(at * rows, (at + 1) * rows) for at in range(n_row)]
    _, [kept_c], sent_c = partial_sums(
        aligned, None, down_weight, tile, *parts[2], spans[:1], spans[1:], crossed, "sums_last")
    sent_c = dict(zip(offsets[1:], sent_c))
    done_c = [kept_c] + [send(sent_c[o], "row", o, n_row) for o in offsets[1:] if o != 1]

    grad_pieces = [act_pieces[o] for o in offsets]
    grad_tile = tile_of(hidden, 256)
    (first_a, count_a), (first_b, count_b) = part_slices(hidden // grad_tile, (3, 4))
    grad = weight_grads(aligned, grad_pieces, grad_tile, first_a, count_a, None, [sent_c[offsets[1]]])
    done_b, crossed_b, _ = halved(kept_b, got_b, [], [grad], n_row)
    done_c.append(send(handed_on([sent_c[1]], crossed_b)[0], "row", 1, n_row))
    weight_grad = weight_grads(aligned, grad_pieces, grad_tile, first_b, count_b, grad, crossed_b)
    return weight_grad, totals([done_a, done_b, done_c], [weight_grad])


def solution(mesh):
    in_specs = (P("row", "col"), P("col", "row"), P("col", "row"), P())
    out_specs = (P("col", "row"), P("row", "col"))
    fn = functools.partial(body, mesh.shape["row"], mesh.shape["col"])
    return jax.shard_map(fn, mesh=mesh, in_specs=in_specs, out_specs=out_specs, check_vma=False)
```

```python
import functools

import jax
import jax.numpy as jnp
from jax import lax
from jax.experimental import pallas as pl
from jax.experimental.pallas import tpu as pltpu
from jax.sharding import PartitionSpec as P

LANES = 128
LEVEL_ROWS = 16
STEPS_PER_OCTAVE = 128.0
TOP = 32766.0
LEAST = 2.0 ** -120
VMEM_LIMIT = 48 * 1024 * 1024
SMALL_LIMIT = 8 * 1024 * 1024
SLOTS = 4
SHARES = (2, 3, 2)
SUB = 256


def tile_of(size, largest):
    tile = largest
    while size % tile:
        tile //= 2
    return tile


def dot(left, right, dims):
    return lax.dot_general(left, right, (dims, ((), ())), preferred_element_type=jnp.float32)


def encode(values):
    most = jnp.maximum(jnp.max(jnp.abs(values), axis=1, keepdims=True), LEAST)
    level = jnp.ceil(jnp.log2(most) * STEPS_PER_OCTAVE) + 1.0
    codes = jnp.round(values * jnp.exp2(level * (-1.0 / STEPS_PER_OCTAVE)) * TOP)
    return codes.astype(jnp.int32).astype(jnp.int16), level


def decode(codes, levels):
    return codes.astype(jnp.int32).astype(jnp.float32) * (jnp.exp2(levels * (1.0 / STEPS_PER_OCTAVE)) * (1.0 / TOP))


def message_shape(rows, width):
    return (width // LANES * rows + pl.cdiv(rows, LANES) * LEVEL_ROWS, LANES)


def turned_levels(levels):
    blocks = []
    for at in range(0, levels.shape[0], LANES):
        block = levels[at:at + LANES]
        if block.shape[0] < LANES:
            block = jnp.concatenate([block, jnp.zeros((LANES - block.shape[0], LANES), jnp.float32)], axis=0)
        blocks.append(block.T[:LEVEL_ROWS])
    return jnp.concatenate(blocks, axis=0).astype(jnp.int32).astype(jnp.int16)


def levels_of(message_ref, rows, width):
    turned = message_ref[width // LANES * rows:].astype(jnp.int32).astype(jnp.float32)
    blocks = []
    for at in range(0, turned.shape[0], LEVEL_ROWS):
        block = turned[at:at + LEVEL_ROWS]
        blocks.append(jnp.concatenate([block, jnp.zeros((LANES - LEVEL_ROWS, LANES), jnp.float32)], axis=0).T)
    return jnp.concatenate(blocks, axis=0)[:rows]


def codes_of(message_ref, rows, first, count):
    return jnp.concatenate([message_ref[at * rows:(at + 1) * rows] for at in range(first, first + count)], axis=1)


def params(limit=VMEM_LIMIT):
    return pltpu.CompilerParams(vmem_limit_bytes=limit)


def cost(flops, moved):
    return pl.CostEstimate(flops=flops, bytes_accessed=moved, transcendentals=0)


def align_rows(pick_ref, pieces, aligned_ref):
    depth = aligned_ref.shape[1]
    chunk = tile_of(depth, 512)
    for at in range(0, depth, chunk):
        cols = slice(at, at + chunk)
        gathered = jnp.concatenate([piece[:, cols] for piece in pieces], axis=0)
        aligned_ref[:, cols] = dot(pick_ref[...], gathered, ((1,), (0,))).astype(jnp.bfloat16)


def sums_kernel(n_pieces, n_blocks, n_later, coded, kept_rows, sent_rows, tile, *refs):
    refs = list(refs)
    if n_pieces:
        pick_ref = refs.pop(0)
        pieces = [refs.pop(0) for _ in range(n_pieces)]
    else:
        aligned_ref = refs.pop(0)
    weights = [refs.pop(0) for _ in range(n_blocks)]
    del refs[:n_later]
    if n_pieces:
        aligned_ref = refs.pop(0)
    kept = [refs.pop(0) for _ in kept_rows]
    sent = [refs.pop(0) for _ in sent_rows]
    levels_ref, = refs
    step = pl.program_id(0)
    per_tile = tile // LANES

    @pl.when(step == 0)
    def _():
        if n_pieces:
            align_rows(pick_ref, pieces, aligned_ref)
        levels_ref[...] = jnp.zeros_like(levels_ref)

    lane = lax.broadcasted_iota(jnp.int32, levels_ref.shape, 1)
    levels = levels_ref[...]
    for part in range(n_blocks):
        at = step * n_blocks + part
        values = dot(aligned_ref[...], weights[part][...], ((1,), (1,)))
        for ref, rows in zip(kept, kept_rows):
            ref[:, part * tile:(part + 1) * tile] = values[rows]
        codes, level = encode(values[coded:])
        levels = jnp.where(lane == at, level, levels)
        for ref, rows in zip(sent, sent_rows):
            height = rows.stop - rows.start
            for col in range(per_tile):
                here = pl.ds(pl.multiple_of((at * per_tile + col) * height, height), height)
                ref[here] = codes[rows.start - coded:rows.stop - coded, col * LANES:(col + 1) * LANES]
    levels_ref[...] = levels

    @pl.when(step == pl.num_programs(0) - 1)
    def _():
        for ref, rows in zip(sent, sent_rows):
            height = rows.stop - rows.start
            turned = turned_levels(levels[rows.start - coded:rows.stop - coded])
            ref[ref.shape[0] - turned.shape[0]:] = turned


def partial_sums(aligned, align, weight, tile, first, count, kept_rows, sent_rows, later_than, name):
    depth = weight.shape[1]
    width = count * tile
    whole = lambda i: (0, 0)
    operands = [align[0], *align[1]] if aligned is None else [aligned]
    total = operands[0].shape[0]
    coded = min(rows.start for rows in sent_rows)
    n_blocks = 2 if count % 2 == 0 and first % 2 == 0 else 1
    block_at = lambda part: (lambda i: (i * n_blocks + first + part, 0))
    heights = lambda spans: [span.stop - span.start for span in spans]
    in_specs = [pl.BlockSpec(operand.shape, whole) for operand in operands]
    in_specs += [pl.BlockSpec((tile, depth), block_at(part)) for part in range(n_blocks)]
    in_specs += [pl.BlockSpec(memory_space=pl.ANY)] * len(later_than)
    out_specs = [pl.BlockSpec((height, n_blocks * tile), lambda i: (0, i)) for height in heights(kept_rows)]
    out_specs += [pl.BlockSpec(message_shape(height, width), whole) for height in heights(sent_rows)]
    out_shape = [jax.ShapeDtypeStruct((height, width), jnp.float32) for height in heights(kept_rows)]
    out_shape += [jax.ShapeDtypeStruct(message_shape(height, width), jnp.int16) for height in heights(sent_rows)]
    if aligned is None:
        out_specs.insert(0, pl.BlockSpec((total, depth), whole))
        out_shape.insert(0, jax.ShapeDtypeStruct((total, depth), jnp.bfloat16))
    outs = pl.pallas_call(
        functools.partial(
            sums_kernel, 0 if aligned is not None else len(align[1]), n_blocks, len(later_than), coded, kept_rows, sent_rows, tile),
        grid=(count // n_blocks,), in_specs=in_specs, out_specs=out_specs, out_shape=out_shape,
        scratch_shapes=[pltpu.VMEM((total - coded, LANES), jnp.float32)],
        compiler_params=params(),
        cost_estimate=cost(2 * total * width * depth, 2 * width * depth), name=name,
    )(*operands, *[weight] * n_blocks, *later_than)
    if aligned is None:
        aligned, *outs = outs
    return aligned, outs[:len(kept_rows)], outs[len(kept_rows):]


def weight_kernel(offsets, first, n_later, tile, aligned_ref, *refs):
    n_pieces = len(offsets)
    pieces = [ref[...] for ref in refs[:n_pieces]]
    out_ref, held_ref, left_sem = refs[n_pieces + n_later:]
    step = pl.program_id(0)
    last = pl.num_programs(0) - 1
    slots = held_ref.shape[0]

    def leave(at):
        rows = pl.ds(pl.multiple_of((first + at) * tile, tile), tile)
        slot = lax.rem(at, slots)
        return pltpu.make_async_copy(held_ref.at[slot], out_ref.at[rows], left_sem.at[slot])

    @pl.when(step >= slots)
    def _():
        leave(step - slots).wait()

    left = jnp.concatenate([pieces[o] for o in offsets], axis=0)
    depth = aligned_ref.shape[1]
    chunk = tile_of(depth, 1024)
    block = held_ref.at[lax.rem(step, slots)]
    for at in range(0, depth, chunk):
        cols = slice(at, at + chunk)
        block[:, cols] = dot(left, aligned_ref[:, cols], ((0,), (0,))).astype(jnp.bfloat16)
    leave(step).start()

    @pl.when(step == last)
    def _():
        for back in range(slots - 1, -1, -1):
            @pl.when(last >= back)
            def _():
                leave(last - back).wait()


def weight_grads(aligned, pieces, offsets, tile, first, count, filled, later_than):
    total, depth = aligned.shape
    rows, hidden = pieces[0].shape
    later = ([] if filled is None else [filled]) + list(later_than)
    return pl.pallas_call(
        functools.partial(weight_kernel, offsets, first, len(later), tile),
        grid=(count,),
        in_specs=[pl.BlockSpec((total, depth), lambda i: (0, 0))]
        + [pl.BlockSpec((rows, tile), lambda i: (0, i + first))] * len(pieces)
        + [pl.BlockSpec(memory_space=pl.ANY)] * len(later),
        out_specs=pl.BlockSpec(memory_space=pl.ANY),
        out_shape=jax.ShapeDtypeStruct((hidden, depth), jnp.bfloat16),
        scratch_shapes=[pltpu.VMEM((SLOTS, tile, depth), jnp.bfloat16), pltpu.SemaphoreType.DMA((SLOTS,))],
        input_output_aliases={} if filled is None else {1 + len(pieces): 0},
        compiler_params=params(), cost_estimate=cost(2 * total * count * tile * depth, 2 * count * tile * depth),
        name="weight_grads",
    )(aligned, *pieces, *later)


def fold_kernel(n_others, kept_ref, got_ref, *refs):
    next_ref, sent_ref = refs[n_others:n_others + 2]
    rows, width = kept_ref.shape
    half = next_ref.shape[0]
    sub = tile_of(width, SUB)
    per_tile = sub // LANES
    lane = lax.broadcasted_iota(jnp.int32, (half, LANES), 1)
    levels = jnp.zeros(lane.shape, jnp.float32)
    got_levels = levels_of(got_ref, rows, width)
    for at in range(width // sub):
        cols = slice(at * sub, (at + 1) * sub)
        total = kept_ref[:, cols] + decode(codes_of(got_ref, rows, at * per_tile, per_tile), got_levels[:, at:at + 1])
        next_ref[:, cols] = total[:half]
        codes, level = encode(total[half:])
        for col in range(per_tile):
            first = (at * per_tile + col) * half
            sent_ref[first:first + half] = codes[:, col * LANES:(col + 1) * LANES]
        levels = jnp.where(lane == at, level, levels)
    sent_ref[width // LANES * half:] = turned_levels(levels)


def fold(kept, got, passed, later_than):
    others = [*passed, *later_than]
    vmem, anywhere = pl.BlockSpec(memory_space=pltpu.VMEM), pl.BlockSpec(memory_space=pl.ANY)
    rows, width = kept.shape
    kept, sent, *passed = pl.pallas_call(
        functools.partial(fold_kernel, len(others)),
        in_specs=[vmem] * 2 + [anywhere] * len(others),
        out_specs=[vmem] * 2 + [anywhere] * len(passed),
        out_shape=[jax.ShapeDtypeStruct((rows // 2, width), kept.dtype), jax.ShapeDtypeStruct(message_shape(rows // 2, width), got.dtype)]
        + [jax.ShapeDtypeStruct(array.shape, array.dtype) for array in passed],
        input_output_aliases={2 + at: 2 + at for at in range(len(passed))},
        compiler_params=params(), cost_estimate=cost(kept.size * 20, kept.size * 12), name="fold",
    )(kept, got, *others)
    return kept, sent, passed


def total_kernel(counts, *refs):
    refs = list(refs)
    out_ref = refs.pop()
    base = 0
    for count in counts:
        kept_ref, got, refs = refs[0], refs[1:count], refs[count:]
        rows, width = kept_ref.shape
        sub = tile_of(width, SUB)
        per_tile = sub // LANES
        levels = [levels_of(ref, rows, width) for ref in got]
        for at in range(width // sub):
            cols = slice(at * sub, (at + 1) * sub)
            total = kept_ref[:, cols]
            for ref, level in zip(got, levels):
                total = total + decode(codes_of(ref, rows, at * per_tile, per_tile), level[:, at:at + 1])
            out_ref[:, base + at * sub:base + (at + 1) * sub] = total.astype(jnp.bfloat16)
        base += width


def totals(parts, later_than):
    rows = parts[0][0].shape[0]
    hidden = sum(part[0].shape[1] for part in parts)
    flat = [array for part in parts for array in part]
    return pl.pallas_call(
        functools.partial(total_kernel, [len(part) for part in parts]),
        in_specs=[pl.BlockSpec(memory_space=pltpu.VMEM)] * len(flat) + [pl.BlockSpec(memory_space=pl.ANY)] * len(later_than),
        out_shape=jax.ShapeDtypeStruct((rows, hidden), jnp.bfloat16),
        compiler_params=params(), cost_estimate=cost(rows * hidden * 40, rows * hidden * 14), name="totals",
    )(*flat, *later_than)


def send(value, axis, flip, size):
    return lax.ppermute(value, axis, [(i, i ^ flip) for i in range(size)])


def stack_kernel(n_values, *refs):
    out_ref = refs[-1]
    rows = refs[0].shape[0]
    for at, ref in enumerate(refs[:n_values]):
        out_ref[at * rows:(at + 1) * rows] = ref[...]


def stacked(values, later_than=()):
    rows, width = values[0].shape
    return pl.pallas_call(
        functools.partial(stack_kernel, len(values)),
        in_specs=[pl.BlockSpec(memory_space=pltpu.VMEM)] * len(values) + [pl.BlockSpec(memory_space=pl.ANY)] * len(later_than),
        out_shape=jax.ShapeDtypeStruct((len(values) * rows, width), values[0].dtype),
        compiler_params=params(SMALL_LIMIT), cost_estimate=cost(0, 4 * len(values) * rows * width), name="stacked",
    )(*values, *later_than)


def same_kernel(*refs):
    pass


def handed_on(values, later_than):
    anywhere = pl.BlockSpec(memory_space=pl.ANY)
    return pl.pallas_call(
        same_kernel,
        in_specs=[anywhere] * (len(values) + len(later_than)), out_specs=[anywhere] * len(values),
        out_shape=[jax.ShapeDtypeStruct(value.shape, value.dtype) for value in values],
        input_output_aliases={at: at for at in range(len(values))},
        compiler_params=params(SMALL_LIMIT), cost_estimate=cost(0, 0), name="handed_on",
    )(*values, *later_than)


def chip_order(n_col):
    return [2, *range(n_col - 2, 2, -2)]


def gather_cotangent(cotangent, n_col):
    pieces = [cotangent] + [send(cotangent, "col", flip, n_col) for flip in chip_order(n_col)]
    stacks = [stacked(pieces[:2])]
    stacks.append(stacked(pieces[2:], stacks))
    return stacks + [send(stack, "col", 1, n_col) for stack in stacks]


def halving_order(size):
    order = [0]
    while len(order) < size:
        order = [2 * o for o in order] + [2 * o + 1 for o in order]
    return order


def part_slices(tiles, shares):
    ends = [tiles * sum(shares[:at]) // 7 for at in range(len(shares) + 1)]
    return [(first, last - first) for first, last in zip(ends, ends[1:])]


def halved(kept, got, passed, later_than, n_row):
    step = 2
    while step < n_row:
        kept, sent, passed = fold(kept, got, passed, later_than)
        got = send(sent, "row", step, n_row)
        step *= 2
    return [kept, got], [sent], passed


def body(n_row, n_col, activations, cotangent, down_weight, row_order):
    rows, hidden = activations.shape
    shard = cotangent.shape[0]
    mine_row, mine_col = lax.axis_index("row"), lax.axis_index("col")
    offsets = halving_order(n_row)
    total = n_row * rows

    flips = [0, *chip_order(n_col)]
    flips += [flip ^ 1 for flip in flips]
    order = row_order.reshape(n_row, rows)
    order = jnp.concatenate([lax.dynamic_index_in_dim(order, mine_row ^ o, 0, keepdims=False) for o in offsets])
    owner = mine_col ^ jnp.asarray(flips, jnp.int32)
    named = (owner[:, None] * shard + jnp.arange(shard, dtype=jnp.int32)[None, :]).reshape(-1)
    pick = (order[:, None] == named[None, :]).astype(jnp.bfloat16)

    tile = tile_of(hidden, 256)
    parts = part_slices(hidden // tile, SHARES)
    pieces = gather_cotangent(cotangent, n_col)
    act_pieces = {o: send(activations, "row", o, n_row) for o in [1, *range(2, n_row, 2)]}
    act_pieces[0] = activations

    kept_rows, sent_rows = [slice(0, total // 2)], [slice(total // 2, total)]
    aligned, [kept], [sent] = partial_sums(
        None, (pick, pieces), down_weight, tile, *parts[0], kept_rows, sent_rows, [], "sums_first")
    got = send(sent, "row", 1, n_row)
    evens = range(2, n_row, 2)
    for o, piece in zip(evens, handed_on([act_pieces[o] for o in evens], [aligned])):
        act_pieces[o], act_pieces[o + 1] = piece, send(piece, "row", 1, n_row)

    _, [kept_b], [sent_b] = partial_sums(
        aligned, None, down_weight, tile, *parts[1], kept_rows, sent_rows, [act_pieces[1]], "sums_second")
    done_a, crossed, [sent_b] = halved(kept, got, [sent_b], [], n_row)
    got_b = send(sent_b, "row", 1, n_row)

    spans = [slice(at * rows, (at + 1) * rows) for at in range(n_row)]
    _, [kept_c], sent_c = partial_sums(
        aligned, None, down_weight, tile, *parts[2], spans[:1], spans[1:], crossed, "sums_last")
    sent_c = dict(zip(offsets[1:], sent_c))
    done_c = [kept_c] + [send(sent_c[o], "row", o, n_row) for o in offsets[1:] if o != 1]

    grad_pieces = [act_pieces[o] for o in range(n_row)]
    grad_tile = tile_of(hidden, 256)
    (first_a, count_a), (first_b, count_b) = part_slices(hidden // grad_tile, (5, 2))
    grad = weight_grads(aligned, grad_pieces, offsets, grad_tile, first_a, count_a, None, [sent_c[offsets[1]]])
    done_b, crossed_b, _ = halved(kept_b, got_b, [], [grad], n_row)
    done_c.append(send(handed_on([sent_c[1]], crossed_b)[0], "row", 1, n_row))
    weight_grad = weight_grads(aligned, grad_pieces, offsets, grad_tile, first_b, count_b, grad, crossed_b)
    return weight_grad, totals([done_a, done_b, done_c], [weight_grad])


def solution(mesh):
    in_specs = (P("row", "col"), P("col", "row"), P("col", "row"), P())
    out_specs = (P("col", "row"), P("row", "col"))
    fn = functools.partial(body, mesh.shape["row"], mesh.shape["col"])
    return jax.shard_map(fn, mesh=mesh, in_specs=in_specs, out_specs=out_specs, check_vma=False)
```

```python
import functools

import jax
import jax.numpy as jnp
from jax import lax
from jax.experimental import pallas as pl
from jax.experimental.pallas import tpu as pltpu
from jax.sharding import PartitionSpec as P

LANES = 128
LEVEL_ROWS = 16
STEPS_PER_OCTAVE = 128.0
TOP = 32766.0
LEAST = 2.0 ** -120
VMEM_LIMIT = 48 * 1024 * 1024
SMALL_LIMIT = 8 * 1024 * 1024
SLOTS = 4
SHARES = (2, 2, 3)
SUB = 256


def tile_of(size, largest):
    tile = largest
    while size % tile:
        tile //= 2
    return tile


def dot(left, right, dims):
    return lax.dot_general(left, right, (dims, ((), ())), preferred_element_type=jnp.float32)


def encode(values):
    most = jnp.maximum(jnp.max(jnp.abs(values), axis=1, keepdims=True), LEAST)
    level = jnp.ceil(jnp.log2(most) * STEPS_PER_OCTAVE) + 1.0
    codes = jnp.round(values * jnp.exp2(level * (-1.0 / STEPS_PER_OCTAVE)) * TOP)
    return codes.astype(jnp.int32).astype(jnp.int16), level


def decode(codes, levels):
    return codes.astype(jnp.int32).astype(jnp.float32) * (jnp.exp2(levels * (1.0 / STEPS_PER_OCTAVE)) * (1.0 / TOP))


def message_shape(rows, width):
    return (width // LANES * rows + pl.cdiv(rows, LANES) * LEVEL_ROWS, LANES)


def turned_levels(levels):
    blocks = []
    for at in range(0, levels.shape[0], LANES):
        block = levels[at:at + LANES]
        if block.shape[0] < LANES:
            block = jnp.concatenate([block, jnp.zeros((LANES - block.shape[0], LANES), jnp.float32)], axis=0)
        blocks.append(block.T[:LEVEL_ROWS])
    return jnp.concatenate(blocks, axis=0).astype(jnp.int32).astype(jnp.int16)


def levels_of(message_ref, rows, width):
    turned = message_ref[width // LANES * rows:].astype(jnp.int32).astype(jnp.float32)
    blocks = []
    for at in range(0, turned.shape[0], LEVEL_ROWS):
        block = turned[at:at + LEVEL_ROWS]
        blocks.append(jnp.concatenate([block, jnp.zeros((LANES - LEVEL_ROWS, LANES), jnp.float32)], axis=0).T)
    return jnp.concatenate(blocks, axis=0)[:rows]


def codes_of(message_ref, rows, first, count):
    return jnp.concatenate([message_ref[at * rows:(at + 1) * rows] for at in range(first, first + count)], axis=1)


def params(limit=VMEM_LIMIT):
    return pltpu.CompilerParams(vmem_limit_bytes=limit)


def cost(flops, moved):
    return pl.CostEstimate(flops=flops, bytes_accessed=moved, transcendentals=0)


def align_rows(pick_ref, pieces, aligned_ref):
    depth = aligned_ref.shape[1]
    chunk = tile_of(depth, 512)
    for at in range(0, depth, chunk):
        cols = slice(at, at + chunk)
        gathered = jnp.concatenate([piece[:, cols] for piece in pieces], axis=0)
        aligned_ref[:, cols] = dot(pick_ref[...], gathered, ((1,), (0,))).astype(jnp.bfloat16)


def sums_kernel(n_pieces, n_blocks, n_later, coded, kept_rows, sent_rows, tile, *refs):
    refs = list(refs)
    if n_pieces:
        pick_ref = refs.pop(0)
        pieces = [refs.pop(0) for _ in range(n_pieces)]
    else:
        aligned_ref = refs.pop(0)
    weights = [refs.pop(0) for _ in range(n_blocks)]
    del refs[:n_later]
    if n_pieces:
        aligned_ref = refs.pop(0)
    kept = [refs.pop(0) for _ in kept_rows]
    sent = [refs.pop(0) for _ in sent_rows]
    levels_ref, = refs
    step = pl.program_id(0)
    per_tile = tile // LANES

    @pl.when(step == 0)
    def _():
        if n_pieces:
            align_rows(pick_ref, pieces, aligned_ref)
        levels_ref[...] = jnp.zeros_like(levels_ref)

    lane = lax.broadcasted_iota(jnp.int32, levels_ref.shape, 1)
    levels = levels_ref[...]
    for part in range(n_blocks):
        at = step * n_blocks + part
        values = dot(aligned_ref[...], weights[part][...], ((1,), (1,)))
        for ref, rows in zip(kept, kept_rows):
            ref[:, part * tile:(part + 1) * tile] = values[rows]
        codes, level = encode(values[coded:])
        levels = jnp.where(lane == at, level, levels)
        for ref, rows in zip(sent, sent_rows):
            height = rows.stop - rows.start
            for col in range(per_tile):
                here = pl.ds(pl.multiple_of((at * per_tile + col) * height, height), height)
                ref[here] = codes[rows.start - coded:rows.stop - coded, col * LANES:(col + 1) * LANES]
    levels_ref[...] = levels

    @pl.when(step == pl.num_programs(0) - 1)
    def _():
        for ref, rows in zip(sent, sent_rows):
            height = rows.stop - rows.start
            turned = turned_levels(levels[rows.start - coded:rows.stop - coded])
            ref[ref.shape[0] - turned.shape[0]:] = turned


def partial_sums(aligned, align, weight, tile, first, count, kept_rows, sent_rows, later_than, name):
    depth = weight.shape[1]
    width = count * tile
    whole = lambda i: (0, 0)
    operands = [align[0], *align[1]] if aligned is None else [aligned]
    total = operands[0].shape[0]
    coded = min(rows.start for rows in sent_rows)
    n_blocks = 2 if count % 2 == 0 and first % 2 == 0 else 1
    block_at = lambda part: (lambda i: (i * n_blocks + first + part, 0))
    heights = lambda spans: [span.stop - span.start for span in spans]
    in_specs = [pl.BlockSpec(operand.shape, whole) for operand in operands]
    in_specs += [pl.BlockSpec((tile, depth), block_at(part)) for part in range(n_blocks)]
    in_specs += [pl.BlockSpec(memory_space=pl.ANY)] * len(later_than)
    out_specs = [pl.BlockSpec((height, n_blocks * tile), lambda i: (0, i)) for height in heights(kept_rows)]
    out_specs += [pl.BlockSpec(message_shape(height, width), whole) for height in heights(sent_rows)]
    out_shape = [jax.ShapeDtypeStruct((height, width), jnp.float32) for height in heights(kept_rows)]
    out_shape += [jax.ShapeDtypeStruct(message_shape(height, width), jnp.int16) for height in heights(sent_rows)]
    if aligned is None:
        out_specs.insert(0, pl.BlockSpec((total, depth), whole))
        out_shape.insert(0, jax.ShapeDtypeStruct((total, depth), jnp.bfloat16))
    outs = pl.pallas_call(
        functools.partial(
            sums_kernel, 0 if aligned is not None else len(align[1]), n_blocks, len(later_than), coded, kept_rows, sent_rows, tile),
        grid=(count // n_blocks,), in_specs=in_specs, out_specs=out_specs, out_shape=out_shape,
        scratch_shapes=[pltpu.VMEM((total - coded, LANES), jnp.float32)],
        compiler_params=params(),
        cost_estimate=cost(2 * total * width * depth, 2 * width * depth), name=name,
    )(*operands, *[weight] * n_blocks, *later_than)
    if aligned is None:
        aligned, *outs = outs
    return aligned, outs[:len(kept_rows)], outs[len(kept_rows):]


def weight_kernel(offsets, first, n_later, tile, aligned_ref, *refs):
    n_pieces = len(offsets)
    pieces = [ref[...] for ref in refs[:n_pieces]]
    out_ref, held_ref, left_sem = refs[n_pieces + n_later:]
    step = pl.program_id(0)
    last = pl.num_programs(0) - 1
    slots = held_ref.shape[0]

    def leave(at):
        rows = pl.ds(pl.multiple_of((first + at) * tile, tile), tile)
        slot = lax.rem(at, slots)
        return pltpu.make_async_copy(held_ref.at[slot], out_ref.at[rows], left_sem.at[slot])

    @pl.when(step >= slots)
    def _():
        leave(step - slots).wait()

    left = jnp.concatenate([pieces[o] for o in offsets], axis=0)
    depth = aligned_ref.shape[1]
    chunk = tile_of(depth, 1024)
    block = held_ref.at[lax.rem(step, slots)]
    for at in range(0, depth, chunk):
        cols = slice(at, at + chunk)
        block[:, cols] = dot(left, aligned_ref[:, cols], ((0,), (0,))).astype(jnp.bfloat16)
    leave(step).start()

    @pl.when(step == last)
    def _():
        for back in range(slots - 1, -1, -1):
            @pl.when(last >= back)
            def _():
                leave(last - back).wait()


def weight_grads(aligned, pieces, offsets, tile, first, count, filled, later_than):
    total, depth = aligned.shape
    rows, hidden = pieces[0].shape
    later = ([] if filled is None else [filled]) + list(later_than)
    return pl.pallas_call(
        functools.partial(weight_kernel, offsets, first, len(later), tile),
        grid=(count,),
        in_specs=[pl.BlockSpec((total, depth), lambda i: (0, 0))]
        + [pl.BlockSpec((rows, tile), lambda i: (0, i + first))] * len(pieces)
        + [pl.BlockSpec(memory_space=pl.ANY)] * len(later),
        out_specs=pl.BlockSpec(memory_space=pl.ANY),
        out_shape=jax.ShapeDtypeStruct((hidden, depth), jnp.bfloat16),
        scratch_shapes=[pltpu.VMEM((SLOTS, tile, depth), jnp.bfloat16), pltpu.SemaphoreType.DMA((SLOTS,))],
        input_output_aliases={} if filled is None else {1 + len(pieces): 0},
        compiler_params=params(), cost_estimate=cost(2 * total * count * tile * depth, 2 * count * tile * depth),
        name="weight_grads",
    )(aligned, *pieces, *later)


def fold_kernel(n_others, kept_ref, got_ref, *refs):
    next_ref, sent_ref = refs[n_others:n_others + 2]
    rows, width = kept_ref.shape
    half = next_ref.shape[0]
    sub = tile_of(width, SUB)
    per_tile = sub // LANES
    lane = lax.broadcasted_iota(jnp.int32, (half, LANES), 1)
    levels = jnp.zeros(lane.shape, jnp.float32)
    got_levels = levels_of(got_ref, rows, width)
    for at in range(width // sub):
        cols = slice(at * sub, (at + 1) * sub)
        total = kept_ref[:, cols] + decode(codes_of(got_ref, rows, at * per_tile, per_tile), got_levels[:, at:at + 1])
        next_ref[:, cols] = total[:half]
        codes, level = encode(total[half:])
        for col in range(per_tile):
            first = (at * per_tile + col) * half
            sent_ref[first:first + half] = codes[:, col * LANES:(col + 1) * LANES]
        levels = jnp.where(lane == at, level, levels)
    sent_ref[width // LANES * half:] = turned_levels(levels)


def fold(kept, got, passed, later_than):
    others = [*passed, *later_than]
    vmem, anywhere = pl.BlockSpec(memory_space=pltpu.VMEM), pl.BlockSpec(memory_space=pl.ANY)
    rows, width = kept.shape
    kept, sent, *passed = pl.pallas_call(
        functools.partial(fold_kernel, len(others)),
        in_specs=[vmem] * 2 + [anywhere] * len(others),
        out_specs=[vmem] * 2 + [anywhere] * len(passed),
        out_shape=[jax.ShapeDtypeStruct((rows // 2, width), kept.dtype), jax.ShapeDtypeStruct(message_shape(rows // 2, width), got.dtype)]
        + [jax.ShapeDtypeStruct(array.shape, array.dtype) for array in passed],
        input_output_aliases={2 + at: 2 + at for at in range(len(passed))},
        compiler_params=params(), cost_estimate=cost(kept.size * 20, kept.size * 12), name="fold",
    )(kept, got, *others)
    return kept, sent, passed


def total_kernel(counts, *refs):
    refs = list(refs)
    out_ref = refs.pop()
    base = 0
    for count in counts:
        kept_ref, got, refs = refs[0], refs[1:count], refs[count:]
        rows, width = kept_ref.shape
        sub = tile_of(width, SUB)
        per_tile = sub // LANES
        levels = [levels_of(ref, rows, width) for ref in got]
        for at in range(width // sub):
            cols = slice(at * sub, (at + 1) * sub)
            total = kept_ref[:, cols]
            for ref, level in zip(got, levels):
                total = total + decode(codes_of(ref, rows, at * per_tile, per_tile), level[:, at:at + 1])
            out_ref[:, base + at * sub:base + (at + 1) * sub] = total.astype(jnp.bfloat16)
        base += width


def totals(parts, later_than):
    rows = parts[0][0].shape[0]
    hidden = sum(part[0].shape[1] for part in parts)
    flat = [array for part in parts for array in part]
    return pl.pallas_call(
        functools.partial(total_kernel, [len(part) for part in parts]),
        in_specs=[pl.BlockSpec(memory_space=pltpu.VMEM)] * len(flat) + [pl.BlockSpec(memory_space=pl.ANY)] * len(later_than),
        out_shape=jax.ShapeDtypeStruct((rows, hidden), jnp.bfloat16),
        compiler_params=params(), cost_estimate=cost(rows * hidden * 40, rows * hidden * 14), name="totals",
    )(*flat, *later_than)


def send(value, axis, flip, size):
    return lax.ppermute(value, axis, [(i, i ^ flip) for i in range(size)])


def stack_kernel(n_values, *refs):
    out_ref = refs[-1]
    rows = refs[0].shape[0]
    for at, ref in enumerate(refs[:n_values]):
        out_ref[at * rows:(at + 1) * rows] = ref[...]


def stacked(values, later_than=()):
    rows, width = values[0].shape
    return pl.pallas_call(
        functools.partial(stack_kernel, len(values)),
        in_specs=[pl.BlockSpec(memory_space=pltpu.VMEM)] * len(values) + [pl.BlockSpec(memory_space=pl.ANY)] * len(later_than),
        out_shape=jax.ShapeDtypeStruct((len(values) * rows, width), values[0].dtype),
        compiler_params=params(SMALL_LIMIT), cost_estimate=cost(0, 4 * len(values) * rows * width), name="stacked",
    )(*values, *later_than)


def same_kernel(*refs):
    pass


def handed_on(values, later_than):
    anywhere = pl.BlockSpec(memory_space=pl.ANY)
    return pl.pallas_call(
        same_kernel,
        in_specs=[anywhere] * (len(values) + len(later_than)), out_specs=[anywhere] * len(values),
        out_shape=[jax.ShapeDtypeStruct(value.shape, value.dtype) for value in values],
        input_output_aliases={at: at for at in range(len(values))},
        compiler_params=params(SMALL_LIMIT), cost_estimate=cost(0, 0), name="handed_on",
    )(*values, *later_than)


def chip_order(n_col):
    return [2, *range(n_col - 2, 2, -2)]


def gather_cotangent(cotangent, n_col):
    pieces = [cotangent] + [send(cotangent, "col", flip, n_col) for flip in chip_order(n_col)]
    stacks = [stacked(pieces[:2])]
    stacks.append(stacked(pieces[2:], stacks))
    return stacks + [send(stack, "col", 1, n_col) for stack in stacks]


def halving_order(size):
    order = [0]
    while len(order) < size:
        order = [2 * o for o in order] + [2 * o + 1 for o in order]
    return order


def part_slices(tiles, shares):
    ends = [tiles * sum(shares[:at]) // 7 for at in range(len(shares) + 1)]
    return [(first, last - first) for first, last in zip(ends, ends[1:])]


def halved(kept, got, passed, later_than, n_row):
    step = 2
    while step < n_row:
        kept, sent, passed = fold(kept, got, passed, later_than)
        got = send(sent, "row", step, n_row)
        step *= 2
    return [kept, got], [sent], passed


def body(n_row, n_col, activations, cotangent, down_weight, row_order):
    rows, hidden = activations.shape
    shard = cotangent.shape[0]
    mine_row, mine_col = lax.axis_index("row"), lax.axis_index("col")
    offsets = halving_order(n_row)
    total = n_row * rows

    flips = [0, *chip_order(n_col)]
    flips += [flip ^ 1 for flip in flips]
    order = row_order.reshape(n_row, rows)
    order = jnp.concatenate([lax.dynamic_index_in_dim(order, mine_row ^ o, 0, keepdims=False) for o in offsets])
    owner = mine_col ^ jnp.asarray(flips, jnp.int32)
    named = (owner[:, None] * shard + jnp.arange(shard, dtype=jnp.int32)[None, :]).reshape(-1)
    pick = (order[:, None] == named[None, :]).astype(jnp.bfloat16)

    tile = tile_of(hidden, 256)
    parts = part_slices(hidden // tile, SHARES)
    pieces = gather_cotangent(cotangent, n_col)
    act_pieces = {o: send(activations, "row", o, n_row) for o in [1, *range(2, n_row, 2)]}
    act_pieces[0] = activations

    kept_rows, sent_rows = [slice(0, total // 2)], [slice(total // 2, total)]
    aligned, [kept], [sent] = partial_sums(
        None, (pick, pieces), down_weight, tile, *parts[0], kept_rows, sent_rows, [], "sums_first")
    got = send(sent, "row", 1, n_row)
    evens = range(2, n_row, 2)
    for o, piece in zip(evens, handed_on([act_pieces[o] for o in evens], [aligned])):
        act_pieces[o], act_pieces[o + 1] = piece, send(piece, "row", 1, n_row)

    _, [kept_b], [sent_b] = partial_sums(
        aligned, None, down_weight, tile, *parts[1], kept_rows, sent_rows, [act_pieces[1]], "sums_second")
    done_a, crossed, [sent_b] = halved(kept, got, [sent_b], [], n_row)
    got_b = send(sent_b, "row", 1, n_row)

    spans = [slice(at * rows, (at + 1) * rows) for at in range(n_row)]
    _, [kept_c], sent_c = partial_sums(
        aligned, None, down_weight, tile, *parts[2], spans[:1], spans[1:], crossed, "sums_last")
    sent_c = dict(zip(offsets[1:], sent_c))
    done_c = [kept_c] + [send(sent_c[o], "row", o, n_row) for o in offsets[1:] if o != 1]

    grad_pieces = [act_pieces[o] for o in range(n_row)]
    grad_tile = tile_of(hidden, 256)
    (first_a, count_a), (first_b, count_b) = part_slices(hidden // grad_tile, (5, 2))
    grad = weight_grads(aligned, grad_pieces, offsets, grad_tile, first_a, count_a, None, [sent_c[offsets[1]]])
    done_b, crossed_b, _ = halved(kept_b, got_b, [], [grad], n_row)
    done_c.append(send(handed_on([sent_c[1]], crossed_b)[0], "row", 1, n_row))
    weight_grad = weight_grads(aligned, grad_pieces, offsets, grad_tile, first_b, count_b, grad, crossed_b)
    return weight_grad, totals([done_a, done_b, done_c], [weight_grad])


def solution(mesh):
    in_specs = (P("row", "col"), P("col", "row"), P("col", "row"), P())
    out_specs = (P("col", "row"), P("row", "col"))
    fn = functools.partial(body, mesh.shape["row"], mesh.shape["col"])
    return jax.shard_map(fn, mesh=mesh, in_specs=in_specs, out_specs=out_specs, check_vma=False)
```

```python
import functools

import jax
import jax.numpy as jnp
from jax import lax
from jax.experimental import pallas as pl
from jax.experimental.pallas import tpu as pltpu
from jax.sharding import PartitionSpec as P

LANES = 128
LEVEL_ROWS = 16
STEPS_PER_OCTAVE = 128.0
TOP = 32766.0
LEAST = 2.0 ** -120
VMEM_LIMIT = 48 * 1024 * 1024
SMALL_LIMIT = 8 * 1024 * 1024
SLOTS = 4
SHARES = (2, 2, 3)
SUB = 256


def tile_of(size, largest):
    tile = largest
    while size % tile:
        tile //= 2
    return tile


def dot(left, right, dims):
    return lax.dot_general(left, right, (dims, ((), ())), preferred_element_type=jnp.float32)


def encode(values):
    most = jnp.maximum(jnp.max(jnp.abs(values), axis=1, keepdims=True), LEAST)
    level = jnp.ceil(jnp.log2(most) * STEPS_PER_OCTAVE) + 1.0
    codes = jnp.round(values * jnp.exp2(level * (-1.0 / STEPS_PER_OCTAVE)) * TOP)
    return codes.astype(jnp.int32).astype(jnp.int16), level


def decode(codes, levels):
    return codes.astype(jnp.int32).astype(jnp.float32) * (jnp.exp2(levels * (1.0 / STEPS_PER_OCTAVE)) * (1.0 / TOP))


def message_shape(rows, width):
    return (width // LANES * rows + pl.cdiv(rows, LANES) * LEVEL_ROWS, LANES)


def turned_levels(levels):
    blocks = []
    for at in range(0, levels.shape[0], LANES):
        block = levels[at:at + LANES]
        if block.shape[0] < LANES:
            block = jnp.concatenate([block, jnp.zeros((LANES - block.shape[0], LANES), jnp.float32)], axis=0)
        blocks.append(block.T[:LEVEL_ROWS])
    return jnp.concatenate(blocks, axis=0).astype(jnp.int32).astype(jnp.int16)


def levels_of(message_ref, rows, width):
    turned = message_ref[width // LANES * rows:].astype(jnp.int32).astype(jnp.float32)
    blocks = []
    for at in range(0, turned.shape[0], LEVEL_ROWS):
        block = turned[at:at + LEVEL_ROWS]
        blocks.append(jnp.concatenate([block, jnp.zeros((LANES - LEVEL_ROWS, LANES), jnp.float32)], axis=0).T)
    return jnp.concatenate(blocks, axis=0)[:rows]


def codes_of(message_ref, rows, first, count):
    return jnp.concatenate([message_ref[at * rows:(at + 1) * rows] for at in range(first, first + count)], axis=1)


def params(limit=VMEM_LIMIT):
    return pltpu.CompilerParams(vmem_limit_bytes=limit)


def cost(flops, moved):
    return pl.CostEstimate(flops=flops, bytes_accessed=moved, transcendentals=0)


def align_rows(pick_ref, pieces, aligned_ref):
    depth = aligned_ref.shape[1]
    chunk = tile_of(depth, 512)
    for at in range(0, depth, chunk):
        cols = slice(at, at + chunk)
        gathered = jnp.concatenate([piece[:, cols] for piece in pieces], axis=0)
        aligned_ref[:, cols] = dot(pick_ref[...], gathered, ((1,), (0,))).astype(jnp.bfloat16)


def sums_kernel(n_pieces, n_blocks, n_later, coded, kept_rows, sent_rows, tile, *refs):
    refs = list(refs)
    if n_pieces:
        pick_ref = refs.pop(0)
        pieces = [refs.pop(0) for _ in range(n_pieces)]
    else:
        aligned_ref = refs.pop(0)
    weights = [refs.pop(0) for _ in range(n_blocks)]
    del refs[:n_later]
    if n_pieces:
        aligned_ref = refs.pop(0)
    kept = [refs.pop(0) for _ in kept_rows]
    sent = [refs.pop(0) for _ in sent_rows]
    levels_ref, = refs
    step = pl.program_id(0)
    per_tile = tile // LANES

    @pl.when(step == 0)
    def _():
        if n_pieces:
            align_rows(pick_ref, pieces, aligned_ref)
        levels_ref[...] = jnp.zeros_like(levels_ref)

    lane = lax.broadcasted_iota(jnp.int32, levels_ref.shape, 1)
    levels = levels_ref[...]
    for part in range(n_blocks):
        at = step * n_blocks + part
        values = dot(aligned_ref[...], weights[part][...], ((1,), (1,)))
        for ref, rows in zip(kept, kept_rows):
            ref[:, part * tile:(part + 1) * tile] = values[rows]
        codes, level = encode(values[coded:])
        levels = jnp.where(lane == at, level, levels)
        for ref, rows in zip(sent, sent_rows):
            height = rows.stop - rows.start
            for col in range(per_tile):
                here = pl.ds(pl.multiple_of((at * per_tile + col) * height, height), height)
                ref[here] = codes[rows.start - coded:rows.stop - coded, col * LANES:(col + 1) * LANES]
    levels_ref[...] = levels

    @pl.when(step == pl.num_programs(0) - 1)
    def _():
        for ref, rows in zip(sent, sent_rows):
            height = rows.stop - rows.start
            turned = turned_levels(levels[rows.start - coded:rows.stop - coded])
            ref[ref.shape[0] - turned.shape[0]:] = turned


def partial_sums(aligned, align, weight, tile, first, count, kept_rows, sent_rows, later_than, name):
    depth = weight.shape[1]
    width = count * tile
    whole = lambda i: (0, 0)
    operands = [align[0], *align[1]] if aligned is None else [aligned]
    total = operands[0].shape[0]
    coded = min(rows.start for rows in sent_rows)
    n_blocks = 2 if count % 2 == 0 and first % 2 == 0 else 1
    block_at = lambda part: (lambda i: (i * n_blocks + first + part, 0))
    heights = lambda spans: [span.stop - span.start for span in spans]
    in_specs = [pl.BlockSpec(operand.shape, whole) for operand in operands]
    in_specs += [pl.BlockSpec((tile, depth), block_at(part)) for part in range(n_blocks)]
    in_specs += [pl.BlockSpec(memory_space=pl.ANY)] * len(later_than)
    out_specs = [pl.BlockSpec((height, n_blocks * tile), lambda i: (0, i)) for height in heights(kept_rows)]
    out_specs += [pl.BlockSpec(message_shape(height, width), whole) for height in heights(sent_rows)]
    out_shape = [jax.ShapeDtypeStruct((height, width), jnp.float32) for height in heights(kept_rows)]
    out_shape += [jax.ShapeDtypeStruct(message_shape(height, width), jnp.int16) for height in heights(sent_rows)]
    if aligned is None:
        out_specs.insert(0, pl.BlockSpec((total, depth), whole))
        out_shape.insert(0, jax.ShapeDtypeStruct((total, depth), jnp.bfloat16))
    outs = pl.pallas_call(
        functools.partial(
            sums_kernel, 0 if aligned is not None else len(align[1]), n_blocks, len(later_than), coded, kept_rows, sent_rows, tile),
        grid=(count // n_blocks,), in_specs=in_specs, out_specs=out_specs, out_shape=out_shape,
        scratch_shapes=[pltpu.VMEM((total - coded, LANES), jnp.float32)],
        compiler_params=params(),
        cost_estimate=cost(2 * total * width * depth, 2 * width * depth), name=name,
    )(*operands, *[weight] * n_blocks, *later_than)
    if aligned is None:
        aligned, *outs = outs
    return aligned, outs[:len(kept_rows)], outs[len(kept_rows):]


def weight_kernel(offsets, first, n_later, tile, aligned_ref, *refs):
    n_pieces = len(offsets)
    pieces = [ref[...] for ref in refs[:n_pieces]]
    out_ref, held_ref, left_sem = refs[n_pieces + n_later:]
    step = pl.program_id(0)
    last = pl.num_programs(0) - 1
    slots = held_ref.shape[0]

    def leave(at):
        rows = pl.ds(pl.multiple_of((first + at) * tile, tile), tile)
        slot = lax.rem(at, slots)
        return pltpu.make_async_copy(held_ref.at[slot], out_ref.at[rows], left_sem.at[slot])

    @pl.when(step >= slots)
    def _():
        leave(step - slots).wait()

    left = jnp.concatenate([pieces[o] for o in offsets], axis=0)
    depth = aligned_ref.shape[1]
    chunk = tile_of(depth, 1024)
    block = held_ref.at[lax.rem(step, slots)]
    for at in range(0, depth, chunk):
        cols = slice(at, at + chunk)
        block[:, cols] = dot(left, aligned_ref[:, cols], ((0,), (0,))).astype(jnp.bfloat16)
    leave(step).start()

    @pl.when(step == last)
    def _():
        for back in range(slots - 1, -1, -1):
            @pl.when(last >= back)
            def _():
                leave(last - back).wait()


def weight_grads(aligned, pieces, offsets, tile, first, count, filled, later_than):
    total, depth = aligned.shape
    rows, hidden = pieces[0].shape
    later = ([] if filled is None else [filled]) + list(later_than)
    return pl.pallas_call(
        functools.partial(weight_kernel, offsets, first, len(later), tile),
        grid=(count,),
        in_specs=[pl.BlockSpec((total, depth), lambda i: (0, 0))]
        + [pl.BlockSpec((rows, tile), lambda i: (0, i + first))] * len(pieces)
        + [pl.BlockSpec(memory_space=pl.ANY)] * len(later),
        out_specs=pl.BlockSpec(memory_space=pl.ANY),
        out_shape=jax.ShapeDtypeStruct((hidden, depth), jnp.bfloat16),
        scratch_shapes=[pltpu.VMEM((SLOTS, tile, depth), jnp.bfloat16), pltpu.SemaphoreType.DMA((SLOTS,))],
        input_output_aliases={} if filled is None else {1 + len(pieces): 0},
        compiler_params=params(), cost_estimate=cost(2 * total * count * tile * depth, 2 * count * tile * depth),
        name="weight_grads",
    )(aligned, *pieces, *later)


def fold_kernel(n_others, kept_ref, got_ref, *refs):
    next_ref, sent_ref = refs[n_others:n_others + 2]
    rows, width = kept_ref.shape
    half = next_ref.shape[0]
    sub = tile_of(width, SUB)
    per_tile = sub // LANES
    lane = lax.broadcasted_iota(jnp.int32, (half, LANES), 1)
    levels = jnp.zeros(lane.shape, jnp.float32)
    got_levels = levels_of(got_ref, rows, width)
    for at in range(width // sub):
        cols = slice(at * sub, (at + 1) * sub)
        total = kept_ref[:, cols] + decode(codes_of(got_ref, rows, at * per_tile, per_tile), got_levels[:, at:at + 1])
        next_ref[:, cols] = total[:half]
        codes, level = encode(total[half:])
        for col in range(per_tile):
            first = (at * per_tile + col) * half
            sent_ref[first:first + half] = codes[:, col * LANES:(col + 1) * LANES]
        levels = jnp.where(lane == at, level, levels)
    sent_ref[width // LANES * half:] = turned_levels(levels)


def fold(kept, got, passed, later_than):
    others = [*passed, *later_than]
    vmem, anywhere = pl.BlockSpec(memory_space=pltpu.VMEM), pl.BlockSpec(memory_space=pl.ANY)
    rows, width = kept.shape
    kept, sent, *passed = pl.pallas_call(
        functools.partial(fold_kernel, len(others)),
        in_specs=[vmem] * 2 + [anywhere] * len(others),
        out_specs=[vmem] * 2 + [anywhere] * len(passed),
        out_shape=[jax.ShapeDtypeStruct((rows // 2, width), kept.dtype), jax.ShapeDtypeStruct(message_shape(rows // 2, width), got.dtype)]
        + [jax.ShapeDtypeStruct(array.shape, array.dtype) for array in passed],
        input_output_aliases={2 + at: 2 + at for at in range(len(passed))},
        compiler_params=params(), cost_estimate=cost(kept.size * 20, kept.size * 12), name="fold",
    )(kept, got, *others)
    return kept, sent, passed


def total_kernel(counts, *refs):
    refs = list(refs)
    out_ref = refs.pop()
    base = 0
    for count in counts:
        kept_ref, got, refs = refs[0], refs[1:count], refs[count:]
        rows, width = kept_ref.shape
        sub = tile_of(width, SUB)
        per_tile = sub // LANES
        levels = [levels_of(ref, rows, width) for ref in got]
        for at in range(width // sub):
            cols = slice(at * sub, (at + 1) * sub)
            total = kept_ref[:, cols]
            for ref, level in zip(got, levels):
                total = total + decode(codes_of(ref, rows, at * per_tile, per_tile), level[:, at:at + 1])
            out_ref[:, base + at * sub:base + (at + 1) * sub] = total.astype(jnp.bfloat16)
        base += width


def totals(parts, later_than):
    rows = parts[0][0].shape[0]
    hidden = sum(part[0].shape[1] for part in parts)
    flat = [array for part in parts for array in part]
    return pl.pallas_call(
        functools.partial(total_kernel, [len(part) for part in parts]),
        in_specs=[pl.BlockSpec(memory_space=pltpu.VMEM)] * len(flat) + [pl.BlockSpec(memory_space=pl.ANY)] * len(later_than),
        out_shape=jax.ShapeDtypeStruct((rows, hidden), jnp.bfloat16),
        compiler_params=params(), cost_estimate=cost(rows * hidden * 40, rows * hidden * 14), name="totals",
    )(*flat, *later_than)


def send(value, axis, flip, size):
    return lax.ppermute(value, axis, [(i, i ^ flip) for i in range(size)])


def stack_kernel(n_values, *refs):
    out_ref = refs[-1]
    rows = refs[0].shape[0]
    for at, ref in enumerate(refs[:n_values]):
        out_ref[at * rows:(at + 1) * rows] = ref[...]


def stacked(values, later_than=()):
    rows, width = values[0].shape
    return pl.pallas_call(
        functools.partial(stack_kernel, len(values)),
        in_specs=[pl.BlockSpec(memory_space=pltpu.VMEM)] * len(values) + [pl.BlockSpec(memory_space=pl.ANY)] * len(later_than),
        out_shape=jax.ShapeDtypeStruct((len(values) * rows, width), values[0].dtype),
        compiler_params=params(SMALL_LIMIT), cost_estimate=cost(0, 4 * len(values) * rows * width), name="stacked",
    )(*values, *later_than)


def same_kernel(*refs):
    pass


def handed_on(values, later_than):
    anywhere = pl.BlockSpec(memory_space=pl.ANY)
    return pl.pallas_call(
        same_kernel,
        in_specs=[anywhere] * (len(values) + len(later_than)), out_specs=[anywhere] * len(values),
        out_shape=[jax.ShapeDtypeStruct(value.shape, value.dtype) for value in values],
        input_output_aliases={at: at for at in range(len(values))},
        compiler_params=params(SMALL_LIMIT), cost_estimate=cost(0, 0), name="handed_on",
    )(*values, *later_than)


def chip_order(n_col):
    return [2, *range(n_col - 2, 2, -2)]


def gather_cotangent(cotangent, n_col):
    pieces = [cotangent] + [send(cotangent, "col", flip, n_col) for flip in chip_order(n_col)]
    stacks = [stacked(pieces[:2])]
    stacks.append(stacked(pieces[2:], stacks))
    return stacks + [send(stack, "col", 1, n_col) for stack in stacks]


def halving_order(size):
    order = [0]
    while len(order) < size:
        order = [2 * o for o in order] + [2 * o + 1 for o in order]
    return order


def part_slices(tiles, shares):
    ends = [tiles * sum(shares[:at]) // 7 for at in range(len(shares) + 1)]
    return [(first, last - first) for first, last in zip(ends, ends[1:])]


def halved(kept, got, passed, later_than, n_row):
    step = 2
    while step < n_row:
        kept, sent, passed = fold(kept, got, passed, later_than)
        got = send(sent, "row", step, n_row)
        step *= 2
    return [kept, got], [sent], passed


def body(n_row, n_col, activations, cotangent, down_weight, row_order):
    rows, hidden = activations.shape
    shard = cotangent.shape[0]
    mine_row, mine_col = lax.axis_index("row"), lax.axis_index("col")
    offsets = halving_order(n_row)
    total = n_row * rows

    flips = [0, *chip_order(n_col)]
    flips += [flip ^ 1 for flip in flips]
    order = row_order.reshape(n_row, rows)
    order = jnp.concatenate([lax.dynamic_index_in_dim(order, mine_row ^ o, 0, keepdims=False) for o in offsets])
    owner = mine_col ^ jnp.asarray(flips, jnp.int32)
    named = (owner[:, None] * shard + jnp.arange(shard, dtype=jnp.int32)[None, :]).reshape(-1)
    pick = (order[:, None] == named[None, :]).astype(jnp.bfloat16)

    tile = tile_of(hidden, 256)
    parts = part_slices(hidden // tile, SHARES)
    pieces = gather_cotangent(cotangent, n_col)
    act_pieces = {o: send(activations, "row", o, n_row) for o in [1, *range(2, n_row, 2)]}
    act_pieces[0] = activations

    kept_rows, sent_rows = [slice(0, total // 2)], [slice(total // 2, total)]
    aligned, [kept], [sent] = partial_sums(
        None, (pick, pieces), down_weight, tile, *parts[0], kept_rows, sent_rows, [], "sums_first")
    got = send(sent, "row", 1, n_row)
    evens = range(2, n_row, 2)
    for o, piece in zip(evens, handed_on([act_pieces[o] for o in evens], [aligned])):
        act_pieces[o], act_pieces[o + 1] = piece, send(piece, "row", 1, n_row)

    _, [kept_b], [sent_b] = partial_sums(
        aligned, None, down_weight, tile, *parts[1], kept_rows, sent_rows, [act_pieces[1]], "sums_second")
    done_a, crossed, [sent_b] = halved(kept, got, [sent_b], [], n_row)
    got_b = send(sent_b, "row", 1, n_row)

    spans = [slice(at * rows, (at + 1) * rows) for at in range(n_row)]
    _, [kept_c], sent_c = partial_sums(
        aligned, None, down_weight, tile, *parts[2], spans[:1], spans[1:], crossed, "sums_last")
    sent_c = dict(zip(offsets[1:], sent_c))
    done_c = [kept_c] + [send(sent_c[o], "row", o, n_row) for o in offsets[1:] if o != 1]

    grad_pieces = [act_pieces[o] for o in range(n_row)]
    grad_tile = tile_of(hidden, 256)
    (first_a, count_a), (first_b, count_b) = part_slices(hidden // grad_tile, (4, 3))
    grad = weight_grads(aligned, grad_pieces, offsets, grad_tile, first_a, count_a, None, [sent_c[offsets[1]]])
    done_b, crossed_b, _ = halved(kept_b, got_b, [], [grad], n_row)
    done_c.append(send(handed_on([sent_c[1]], crossed_b)[0], "row", 1, n_row))
    weight_grad = weight_grads(aligned, grad_pieces, offsets, grad_tile, first_b, count_b, grad, crossed_b)
    return weight_grad, totals([done_a, done_b, done_c], [weight_grad])


def solution(mesh):
    in_specs = (P("row", "col"), P("col", "row"), P("col", "row"), P())
    out_specs = (P("col", "row"), P("row", "col"))
    fn = functools.partial(body, mesh.shape["row"], mesh.shape["col"])
    return jax.shard_map(fn, mesh=mesh, in_specs=in_specs, out_specs=out_specs, check_vma=False)
```

```python
import functools

import jax
import jax.numpy as jnp
from jax import lax
from jax.experimental import pallas as pl
from jax.experimental.pallas import tpu as pltpu
from jax.sharding import PartitionSpec as P

LANES = 128
LEVEL_ROWS = 16
STEPS_PER_OCTAVE = 128.0
TOP = 32766.0
LEAST = 2.0 ** -120
VMEM_LIMIT = 48 * 1024 * 1024
SMALL_LIMIT = 8 * 1024 * 1024
SLOTS = 4
SHARES = (3, 2, 2)
SUB = 256


def tile_of(size, largest):
    tile = largest
    while size % tile:
        tile //= 2
    return tile


def dot(left, right, dims):
    return lax.dot_general(left, right, (dims, ((), ())), preferred_element_type=jnp.float32)


def encode(values):
    most = jnp.maximum(jnp.max(jnp.abs(values), axis=1, keepdims=True), LEAST)
    level = jnp.ceil(jnp.log2(most) * STEPS_PER_OCTAVE) + 1.0
    codes = jnp.round(values * jnp.exp2(level * (-1.0 / STEPS_PER_OCTAVE)) * TOP)
    return codes.astype(jnp.int32).astype(jnp.int16), level


def decode(codes, levels):
    return codes.astype(jnp.int32).astype(jnp.float32) * (jnp.exp2(levels * (1.0 / STEPS_PER_OCTAVE)) * (1.0 / TOP))


def message_shape(rows, width):
    return (width // LANES * rows + pl.cdiv(rows, LANES) * LEVEL_ROWS, LANES)


def turned_levels(levels):
    blocks = []
    for at in range(0, levels.shape[0], LANES):
        block = levels[at:at + LANES]
        if block.shape[0] < LANES:
            block = jnp.concatenate([block, jnp.zeros((LANES - block.shape[0], LANES), jnp.float32)], axis=0)
        blocks.append(block.T[:LEVEL_ROWS])
    return jnp.concatenate(blocks, axis=0).astype(jnp.int32).astype(jnp.int16)


def levels_of(message_ref, rows, width):
    turned = message_ref[width // LANES * rows:].astype(jnp.int32).astype(jnp.float32)
    blocks = []
    for at in range(0, turned.shape[0], LEVEL_ROWS):
        block = turned[at:at + LEVEL_ROWS]
        blocks.append(jnp.concatenate([block, jnp.zeros((LANES - LEVEL_ROWS, LANES), jnp.float32)], axis=0).T)
    return jnp.concatenate(blocks, axis=0)[:rows]


def codes_of(message_ref, rows, first, count):
    return jnp.concatenate([message_ref[at * rows:(at + 1) * rows] for at in range(first, first + count)], axis=1)


def params(limit=VMEM_LIMIT):
    return pltpu.CompilerParams(vmem_limit_bytes=limit)


def cost(flops, moved):
    return pl.CostEstimate(flops=flops, bytes_accessed=moved, transcendentals=0)


def align_rows(pick_ref, pieces, aligned_ref):
    depth = aligned_ref.shape[1]
    chunk = tile_of(depth, 512)
    for at in range(0, depth, chunk):
        cols = slice(at, at + chunk)
        gathered = jnp.concatenate([piece[:, cols] for piece in pieces], axis=0)
        aligned_ref[:, cols] = dot(pick_ref[...], gathered, ((1,), (0,))).astype(jnp.bfloat16)


def sums_kernel(n_pieces, n_blocks, n_later, coded, kept_rows, sent_rows, tile, *refs):
    refs = list(refs)
    if n_pieces:
        pick_ref = refs.pop(0)
        pieces = [refs.pop(0) for _ in range(n_pieces)]
    else:
        aligned_ref = refs.pop(0)
    weights = [refs.pop(0) for _ in range(n_blocks)]
    del refs[:n_later]
    if n_pieces:
        aligned_ref = refs.pop(0)
    kept = [refs.pop(0) for _ in kept_rows]
    sent = [refs.pop(0) for _ in sent_rows]
    levels_ref, = refs
    step = pl.program_id(0)
    per_tile = tile // LANES

    @pl.when(step == 0)
    def _():
        if n_pieces:
            align_rows(pick_ref, pieces, aligned_ref)
        levels_ref[...] = jnp.zeros_like(levels_ref)

    lane = lax.broadcasted_iota(jnp.int32, levels_ref.shape, 1)
    levels = levels_ref[...]
    for part in range(n_blocks):
        at = step * n_blocks + part
        values = dot(aligned_ref[...], weights[part][...], ((1,), (1,)))
        for ref, rows in zip(kept, kept_rows):
            ref[:, part * tile:(part + 1) * tile] = values[rows]
        codes, level = encode(values[coded:])
        levels = jnp.where(lane == at, level, levels)
        for ref, rows in zip(sent, sent_rows):
            height = rows.stop - rows.start
            for col in range(per_tile):
                here = pl.ds(pl.multiple_of((at * per_tile + col) * height, height), height)
                ref[here] = codes[rows.start - coded:rows.stop - coded, col * LANES:(col + 1) * LANES]
    levels_ref[...] = levels

    @pl.when(step == pl.num_programs(0) - 1)
    def _():
        for ref, rows in zip(sent, sent_rows):
            height = rows.stop - rows.start
            turned = turned_levels(levels[rows.start - coded:rows.stop - coded])
            ref[ref.shape[0] - turned.shape[0]:] = turned


def partial_sums(aligned, align, weight, tile, first, count, kept_rows, sent_rows, later_than, name):
    depth = weight.shape[1]
    width = count * tile
    whole = lambda i: (0, 0)
    operands = [align[0], *align[1]] if aligned is None else [aligned]
    total = operands[0].shape[0]
    coded = min(rows.start for rows in sent_rows)
    n_blocks = 2 if count % 2 == 0 and first % 2 == 0 else 1
    block_at = lambda part: (lambda i: (i * n_blocks + first + part, 0))
    heights = lambda spans: [span.stop - span.start for span in spans]
    in_specs = [pl.BlockSpec(operand.shape, whole) for operand in operands]
    in_specs += [pl.BlockSpec((tile, depth), block_at(part)) for part in range(n_blocks)]
    in_specs += [pl.BlockSpec(memory_space=pl.ANY)] * len(later_than)
    out_specs = [pl.BlockSpec((height, n_blocks * tile), lambda i: (0, i)) for height in heights(kept_rows)]
    out_specs += [pl.BlockSpec(message_shape(height, width), whole) for height in heights(sent_rows)]
    out_shape = [jax.ShapeDtypeStruct((height, width), jnp.float32) for height in heights(kept_rows)]
    out_shape += [jax.ShapeDtypeStruct(message_shape(height, width), jnp.int16) for height in heights(sent_rows)]
    if aligned is None:
        out_specs.insert(0, pl.BlockSpec((total, depth), whole))
        out_shape.insert(0, jax.ShapeDtypeStruct((total, depth), jnp.bfloat16))
    outs = pl.pallas_call(
        functools.partial(
            sums_kernel, 0 if aligned is not None else len(align[1]), n_blocks, len(later_than), coded, kept_rows, sent_rows, tile),
        grid=(count // n_blocks,), in_specs=in_specs, out_specs=out_specs, out_shape=out_shape,
        scratch_shapes=[pltpu.VMEM((total - coded, LANES), jnp.float32)],
        compiler_params=params(),
        cost_estimate=cost(2 * total * width * depth, 2 * width * depth), name=name,
    )(*operands, *[weight] * n_blocks, *later_than)
    if aligned is None:
        aligned, *outs = outs
    return aligned, outs[:len(kept_rows)], outs[len(kept_rows):]


def weight_kernel(offsets, first, n_later, tile, aligned_ref, *refs):
    n_pieces = len(offsets)
    pieces = [ref[...] for ref in refs[:n_pieces]]
    out_ref, held_ref, left_sem = refs[n_pieces + n_later:]
    step = pl.program_id(0)
    last = pl.num_programs(0) - 1
    slots = held_ref.shape[0]

    def leave(at):
        rows = pl.ds(pl.multiple_of((first + at) * tile, tile), tile)
        slot = lax.rem(at, slots)
        return pltpu.make_async_copy(held_ref.at[slot], out_ref.at[rows], left_sem.at[slot])

    @pl.when(step >= slots)
    def _():
        leave(step - slots).wait()

    left = jnp.concatenate([pieces[o] for o in offsets], axis=0)
    depth = aligned_ref.shape[1]
    chunk = tile_of(depth, 1024)
    block = held_ref.at[lax.rem(step, slots)]
    for at in range(0, depth, chunk):
        cols = slice(at, at + chunk)
        block[:, cols] = dot(left, aligned_ref[:, cols], ((0,), (0,))).astype(jnp.bfloat16)
    leave(step).start()

    @pl.when(step == last)
    def _():
        for back in range(slots - 1, -1, -1):
            @pl.when(last >= back)
            def _():
                leave(last - back).wait()


def weight_grads(aligned, pieces, offsets, tile, first, count, filled, later_than):
    total, depth = aligned.shape
    rows, hidden = pieces[0].shape
    later = ([] if filled is None else [filled]) + list(later_than)
    return pl.pallas_call(
        functools.partial(weight_kernel, offsets, first, len(later), tile),
        grid=(count,),
        in_specs=[pl.BlockSpec((total, depth), lambda i: (0, 0))]
        + [pl.BlockSpec((rows, tile), lambda i: (0, i + first))] * len(pieces)
        + [pl.BlockSpec(memory_space=pl.ANY)] * len(later),
        out_specs=pl.BlockSpec(memory_space=pl.ANY),
        out_shape=jax.ShapeDtypeStruct((hidden, depth), jnp.bfloat16),
        scratch_shapes=[pltpu.VMEM((SLOTS, tile, depth), jnp.bfloat16), pltpu.SemaphoreType.DMA((SLOTS,))],
        input_output_aliases={} if filled is None else {1 + len(pieces): 0},
        compiler_params=params(), cost_estimate=cost(2 * total * count * tile * depth, 2 * count * tile * depth),
        name="weight_grads",
    )(aligned, *pieces, *later)


def fold_kernel(n_others, kept_ref, got_ref, *refs):
    next_ref, sent_ref = refs[n_others:n_others + 2]
    rows, width = kept_ref.shape
    half = next_ref.shape[0]
    sub = tile_of(width, SUB)
    per_tile = sub // LANES
    lane = lax.broadcasted_iota(jnp.int32, (half, LANES), 1)
    levels = jnp.zeros(lane.shape, jnp.float32)
    got_levels = levels_of(got_ref, rows, width)
    for at in range(width // sub):
        cols = slice(at * sub, (at + 1) * sub)
        total = kept_ref[:, cols] + decode(codes_of(got_ref, rows, at * per_tile, per_tile), got_levels[:, at:at + 1])
        next_ref[:, cols] = total[:half]
        codes, level = encode(total[half:])
        for col in range(per_tile):
            first = (at * per_tile + col) * half
            sent_ref[first:first + half] = codes[:, col * LANES:(col + 1) * LANES]
        levels = jnp.where(lane == at, level, levels)
    sent_ref[width // LANES * half:] = turned_levels(levels)


def fold(kept, got, passed, later_than):
    others = [*passed, *later_than]
    vmem, anywhere = pl.BlockSpec(memory_space=pltpu.VMEM), pl.BlockSpec(memory_space=pl.ANY)
    rows, width = kept.shape
    kept, sent, *passed = pl.pallas_call(
        functools.partial(fold_kernel, len(others)),
        in_specs=[vmem] * 2 + [anywhere] * len(others),
        out_specs=[vmem] * 2 + [anywhere] * len(passed),
        out_shape=[jax.ShapeDtypeStruct((rows // 2, width), kept.dtype), jax.ShapeDtypeStruct(message_shape(rows // 2, width), got.dtype)]
        + [jax.ShapeDtypeStruct(array.shape, array.dtype) for array in passed],
        input_output_aliases={2 + at: 2 + at for at in range(len(passed))},
        compiler_params=params(), cost_estimate=cost(kept.size * 20, kept.size * 12), name="fold",
    )(kept, got, *others)
    return kept, sent, passed


def total_kernel(counts, *refs):
    refs = list(refs)
    out_ref = refs.pop()
    base = 0
    for count in counts:
        kept_ref, got, refs = refs[0], refs[1:count], refs[count:]
        rows, width = kept_ref.shape
        sub = tile_of(width, SUB)
        per_tile = sub // LANES
        levels = [levels_of(ref, rows, width) for ref in got]
        for at in range(width // sub):
            cols = slice(at * sub, (at + 1) * sub)
            total = kept_ref[:, cols]
            for ref, level in zip(got, levels):
                total = total + decode(codes_of(ref, rows, at * per_tile, per_tile), level[:, at:at + 1])
            out_ref[:, base + at * sub:base + (at + 1) * sub] = total.astype(jnp.bfloat16)
        base += width


def totals(parts, later_than):
    rows = parts[0][0].shape[0]
    hidden = sum(part[0].shape[1] for part in parts)
    flat = [array for part in parts for array in part]
    return pl.pallas_call(
        functools.partial(total_kernel, [len(part) for part in parts]),
        in_specs=[pl.BlockSpec(memory_space=pltpu.VMEM)] * len(flat) + [pl.BlockSpec(memory_space=pl.ANY)] * len(later_than),
        out_shape=jax.ShapeDtypeStruct((rows, hidden), jnp.bfloat16),
        compiler_params=params(), cost_estimate=cost(rows * hidden * 40, rows * hidden * 14), name="totals",
    )(*flat, *later_than)


def send(value, axis, flip, size):
    return lax.ppermute(value, axis, [(i, i ^ flip) for i in range(size)])


def stack_kernel(n_values, *refs):
    out_ref = refs[-1]
    rows = refs[0].shape[0]
    for at, ref in enumerate(refs[:n_values]):
        out_ref[at * rows:(at + 1) * rows] = ref[...]


def stacked(values, later_than=()):
    rows, width = values[0].shape
    return pl.pallas_call(
        functools.partial(stack_kernel, len(values)),
        in_specs=[pl.BlockSpec(memory_space=pltpu.VMEM)] * len(values) + [pl.BlockSpec(memory_space=pl.ANY)] * len(later_than),
        out_shape=jax.ShapeDtypeStruct((len(values) * rows, width), values[0].dtype),
        compiler_params=params(SMALL_LIMIT), cost_estimate=cost(0, 4 * len(values) * rows * width), name="stacked",
    )(*values, *later_than)


def same_kernel(*refs):
    pass


def handed_on(values, later_than):
    anywhere = pl.BlockSpec(memory_space=pl.ANY)
    return pl.pallas_call(
        same_kernel,
        in_specs=[anywhere] * (len(values) + len(later_than)), out_specs=[anywhere] * len(values),
        out_shape=[jax.ShapeDtypeStruct(value.shape, value.dtype) for value in values],
        input_output_aliases={at: at for at in range(len(values))},
        compiler_params=params(SMALL_LIMIT), cost_estimate=cost(0, 0), name="handed_on",
    )(*values, *later_than)


def chip_order(n_col):
    return [2, *range(n_col - 2, 2, -2)]


def gather_cotangent(cotangent, n_col):
    pieces = [cotangent] + [send(cotangent, "col", flip, n_col) for flip in chip_order(n_col)]
    stacks = [stacked(pieces[:2])]
    stacks.append(stacked(pieces[2:], stacks))
    return stacks + [send(stack, "col", 1, n_col) for stack in stacks]


def halving_order(size):
    order = [0]
    while len(order) < size:
        order = [2 * o for o in order] + [2 * o + 1 for o in order]
    return order


def part_slices(tiles, shares):
    ends = [tiles * sum(shares[:at]) // 7 for at in range(len(shares) + 1)]
    return [(first, last - first) for first, last in zip(ends, ends[1:])]


def halved(kept, got, passed, later_than, n_row):
    step = 2
    while step < n_row:
        kept, sent, passed = fold(kept, got, passed, later_than)
        got = send(sent, "row", step, n_row)
        step *= 2
    return [kept, got], [sent], passed


def body(n_row, n_col, activations, cotangent, down_weight, row_order):
    rows, hidden = activations.shape
    shard = cotangent.shape[0]
    mine_row, mine_col = lax.axis_index("row"), lax.axis_index("col")
    offsets = halving_order(n_row)
    total = n_row * rows

    flips = [0, *chip_order(n_col)]
    flips += [flip ^ 1 for flip in flips]
    order = row_order.reshape(n_row, rows)
    order = jnp.concatenate([lax.dynamic_index_in_dim(order, mine_row ^ o, 0, keepdims=False) for o in offsets])
    owner = mine_col ^ jnp.asarray(flips, jnp.int32)
    named = (owner[:, None] * shard + jnp.arange(shard, dtype=jnp.int32)[None, :]).reshape(-1)
    pick = (order[:, None] == named[None, :]).astype(jnp.bfloat16)

    tile = tile_of(hidden, 256)
    parts = part_slices(hidden // tile, SHARES)
    pieces = gather_cotangent(cotangent, n_col)
    act_pieces = {o: send(activations, "row", o, n_row) for o in [1, *range(2, n_row, 2)]}
    act_pieces[0] = activations

    kept_rows, sent_rows = [slice(0, total // 2)], [slice(total // 2, total)]
    aligned, [kept], [sent] = partial_sums(
        None, (pick, pieces), down_weight, tile, *parts[0], kept_rows, sent_rows, [], "sums_first")
    got = send(sent, "row", 1, n_row)
    evens = range(2, n_row, 2)
    for o, piece in zip(evens, handed_on([act_pieces[o] for o in evens], [aligned])):
        act_pieces[o], act_pieces[o + 1] = piece, send(piece, "row", 1, n_row)

    _, [kept_b], [sent_b] = partial_sums(
        aligned, None, down_weight, tile, *parts[1], kept_rows, sent_rows, [act_pieces[1]], "sums_second")
    done_a, crossed, [sent_b] = halved(kept, got, [sent_b], [], n_row)
    got_b = send(sent_b, "row", 1, n_row)

    spans = [slice(at * rows, (at + 1) * rows) for at in range(n_row)]
    _, [kept_c], sent_c = partial_sums(
        aligned, None, down_weight, tile, *parts[2], spans[:1], spans[1:], crossed, "sums_last")
    sent_c = dict(zip(offsets[1:], sent_c))
    done_c = [kept_c] + [send(sent_c[o], "row", o, n_row) for o in offsets[1:] if o != 1]

    grad_pieces = [act_pieces[o] for o in range(n_row)]
    grad_tile = tile_of(hidden, 256)
    (first_a, count_a), (first_b, count_b) = part_slices(hidden // grad_tile, (4, 3))
    grad = weight_grads(aligned, grad_pieces, offsets, grad_tile, first_a, count_a, None, [sent_c[offsets[1]]])
    done_b, crossed_b, _ = halved(kept_b, got_b, [], [grad], n_row)
    done_c.append(send(handed_on([sent_c[1]], crossed_b)[0], "row", 1, n_row))
    weight_grad = weight_grads(aligned, grad_pieces, offsets, grad_tile, first_b, count_b, grad, crossed_b)
    return weight_grad, totals([done_a, done_b, done_c], [weight_grad])


def solution(mesh):
    in_specs = (P("row", "col"), P("col", "row"), P("col", "row"), P())
    out_specs = (P("col", "row"), P("row", "col"))
    fn = functools.partial(body, mesh.shape["row"], mesh.shape["col"])
    return jax.shard_map(fn, mesh=mesh, in_specs=in_specs, out_specs=out_specs, check_vma=False)
```
